32 devices in a mesh: dp: 8 (over z, y), pipe: 2 (over x), pair: 2 (over core).
Axes of the slice: x: 2, y: 2, z: 4, core: 2. Of those that a mesh axis runs over, the one named last changes fastest.
Arguments:
- inputs: bfloat16 [7680, 768], P(('dp', 'pair')), may hold values from -6 to 6
- cotangent: bfloat16 [7680, 768], P(('dp', 'pair')), may hold values from -6 to 6
- text_mask: int32 [32, 176], P(('dp', 'pair')), may hold values 0 or 1
- seg_count: int32 [32], P(('dp', 'pair')), may hold values from 5 to 64, as said below
- align: int32 [32, 176], P(('dp', 'pair')), may hold values from 0 to 63, as said below
- w_qkv: bfloat16 [2, 768, 2304], P('pipe', 'pair'), may hold values from -0.21875 to 0.21875
- w_out: bfloat16 [2, 768, 768], P('pipe', 'pair'), may hold values from -0.875 to 0.875
- w_up: bfloat16 [2, 768, 3072], P('pipe', 'pair'), may hold values from -0.21875 to 0.21875
- w_down: bfloat16 [2, 3072, 768], P('pipe', 'pair'), may hold values from -0.109375 to 0.109375
- bias_qv: bfloat16 [2, 2, 768], P('pipe', None, 'pair'), may hold values from -3 to 3
- bias_up: bfloat16 [2, 3072], P('pipe', 'pair'), may hold values from -3 to 3
- bias_res: bfloat16 [2, 2, 768], P('pipe', None, 'pair'), may hold values from -3 to 3
- norm_gain: bfloat16 [2, 2, 768], P('pipe', None, 'pair'), may hold values from 0.5 to 1.5
- norm_shift: bfloat16 [2, 2, 768], P('pipe', None, 'pair'), may hold values from -3 to 3
Outputs:
- section_out: bfloat16 [2, 7680, 768], P('pipe', ('dp', 'pair'))
- input_grad: bfloat16 [2, 7680, 768], P('pipe', ('dp', 'pair'))
- grad_w_qkv: float32 [2, 768, 2304], P('pipe', 'pair')
- grad_w_out: float32 [2, 768, 768], P('pipe', 'pair')
- grad_w_up: float32 [2, 768, 3072], P('pipe', 'pair')
- grad_w_down: float32 [2, 3072, 768], P('pipe', 'pair')
- grad_bias_qv: float32 [2, 2, 768], P('pipe', None, 'pair')
- grad_bias_up: float32 [2, 3072], P('pipe', 'pair')
- grad_bias_res: float32 [2, 2, 768], P('pipe', None, 'pair')
- grad_norm_gain: float32 [2, 2, 768], P('pipe', None, 'pair')
- grad_norm_shift: float32 [2, 2, 768], P('pipe', None, 'pair')
The draws below stay inside these ranges and needn't reach their ends.
Inputs may be any that keep to these rules, and one draw needn't show every extreme that they name: `seg_count`: heavy-tailed; some document has 64 segments. `align`: each value is below its document's seg_count.
All inputs are finite; a program needn't handle non-finite values. No bound on the sum of `text_mask` on one device may be relied on, other than what follows from the above.
Results may differ from the reference program's by a relative error of at most 0.024.
Values may be sent and summed in bfloat16 or wider, within the bound.
No kernel may reach another device: no remote copies, remote signals or barrier semaphores. Data moves between devices by JAX's collectives and lax.ppermute only.
A program may use at most 192 MiB of HBM per device.

```python
import math
import jax
import jax.numpy as jnp
from jax import lax

D = 768
HEADS = 12
HEAD = 64
FF = 3072
TEXT = 176
SLOTS = 64
SEQ = 240
DOCS = 32
TOKENS = 7680


def segment_layout(key):
    first_key, second_key, third_key = jax.random.split(key, 3)
    lowest = max(1, 5 * SLOTS // 64)
    span = SLOTS - lowest
    factor_one = jax.random.randint(first_key, (DOCS,), 0, span + 1)
    factor_two = jax.random.randint(second_key, (DOCS,), 0, span + 1)
    counts = lowest + factor_one * factor_two // max(span, 1)
    fullest = jax.random.randint(third_key, (), 0, DOCS)
    counts = jnp.where(jnp.arange(DOCS, dtype=jnp.int32) == fullest, SLOTS, counts)
    return (counts.astype(jnp.int32), fullest)


def draw_seg_count(key, part):
    counts, fullest = segment_layout(key)
    return counts


def draw_align(key, part):
    counts, fullest = segment_layout(key)
    key = jax.random.fold_in(key, 2)
    raw_bits = jax.random.randint(key, (DOCS, TEXT), 0, 1 << 20)
    aligned = raw_bits % counts[:, None]
    doc_iota = jnp.arange(DOCS, dtype=jnp.int32)[:, None]
    text_iota = jnp.arange(TEXT, dtype=jnp.int32)[None, :]
    aligned = jnp.where((doc_iota == fullest) & (text_iota == 0), SLOTS - 1, aligned)
    return aligned.astype(jnp.int32)


def touch_ends(values, stream_key, low, top_value):
    dims = values.shape
    index_at = [jax.random.randint(jax.random.fold_in(stream_key, axis), (), 0, dims[axis]) for axis in range(len(dims))]
    values = values.at[tuple(index_at)].set(low)
    longest = dims.index(max(dims))
    index_at[longest] = (index_at[longest] + 1) % dims[longest]
    return values.at[tuple(index_at)].set(top_value)


def block_levels(stream_key, extent, cuts, smallest, largest):
    level, own = 1.0, jax.random.fold_in(stream_key, 6)
    for axis_at, shards_of in cuts:
        draws = jnp.exp(jax.random.uniform(jax.random.fold_in(own, axis_at), (shards_of,), jnp.float32, smallest / len(cuts), largest / len(cuts)))
        level = level * jnp.repeat(draws, extent[axis_at] // shards_of).reshape([-1 if axis == axis_at else 1 for axis in range(len(extent))])
    return level


def gaussian(key, extent, scale, bound, cuts=(), kind=jnp.bfloat16):
    level = block_levels(key, extent, cuts, -0.22, 0.18) if cuts else 1.0
    values = jax.random.normal(key, extent, jnp.float32) * scale * level
    return jnp.minimum(jnp.maximum(values, -bound), bound).astype(kind)


def setup_inputs(seed: int = 0) -> dict:
    splits = jax.random.split(jax.random.key(seed), 15)
    inputs = gaussian(splits[0], (TOKENS, D), 1.0, 6.0, ((0, 16),))
    cotangent = gaussian(splits[1], (TOKENS, D), 1.0, 6.0, ((0, 16),))
    text_mask = touch_ends((jax.random.randint(splits[2], (DOCS, TEXT), 0, 8) < 7).astype(jnp.int32), jax.random.fold_in(splits[2], 1), 0, 1)
    seg_count = draw_seg_count(jax.random.fold_in(splits[14], 71), 0)
    align = draw_align(jax.random.fold_in(splits[14], 71), 0)
    w_qkv = gaussian(splits[5], (2, D, 3 * D), D ** -0.5, 0.21875, ((0, 2), (1, 2)))
    w_out = gaussian(splits[6], (2, D, D), (D // 16) ** -0.5, 0.875, ((0, 2), (1, 2)))
    w_up = gaussian(splits[7], (2, D, FF), D ** -0.5, 0.21875, ((0, 2), (1, 2)))
    w_down = gaussian(splits[8], (2, FF, D), FF ** -0.5, 0.109375, ((0, 2), (1, 2)))
    bias_qv = gaussian(splits[9], (2, 2, D), 0.5, 3.0, ((0, 2), (2, 2)))
    bias_up = gaussian(splits[10], (2, FF), 0.5, 3.0, ((0, 2), (1, 2)))
    bias_res = gaussian(splits[11], (2, 2, D), 0.5, 3.0, ((0, 2), (2, 2)))
    norm_gain = jnp.clip(1.0 + 0.1 * jax.random.normal(splits[12], (2, 2, D), jnp.float32), 0.5, 1.5).astype(jnp.bfloat16)
    norm_shift = gaussian(splits[13], (2, 2, D), 0.5, 3.0, ((0, 2), (2, 2)))
    return dict(inputs=inputs, cotangent=cotangent, text_mask=text_mask, seg_count=seg_count, align=align, w_qkv=w_qkv, w_out=w_out, w_up=w_up, w_down=w_down, bias_qv=bias_qv, bias_up=bias_up, bias_res=bias_res, norm_gain=norm_gain, norm_shift=norm_shift)


epsilon = 1e-06
masked_score = -1e+30
highest = lax.Precision.HIGHEST

@jax.custom_vjp
def low(v):
    return lax.optimization_barrier(v.astype(jnp.bfloat16)).astype(jnp.float32)

@jax.custom_vjp
def low_back(v):
    return v

def low_keep(v):
    return (low(v), None)

def low_pass(kept, grad):
    return (grad,)

def back_keep(v):
    return (v, None)

def back_low(kept, grad):
    return (low(grad),)
low.defvjp(low_keep, low_pass)
low_back.defvjp(back_keep, back_low)

def layer_norm(values, gain, shift):
    center = values - lax.optimization_barrier(jnp.mean(values, axis=-1, keepdims=True))
    spread = lax.optimization_barrier(jnp.mean(center * center, axis=-1, keepdims=True))
    return center * lax.rsqrt(spread + epsilon) * gain + shift

def build_keep(text_mask, seg_count, align):
    documents = align.shape[0]
    slot_iota = jnp.arange(SLOTS, dtype=jnp.int32)
    key_valid = jnp.concatenate([text_mask == 1, slot_iota[None, :] < seg_count[:, None]], axis=1)
    owned_by = align[:, None, :] == slot_iota[None, :, None]
    slot_rows = jnp.concatenate([owned_by, jnp.ones((documents, SLOTS, SLOTS), dtype=bool)], axis=2)
    text_rows = jnp.ones((documents, TEXT, SEQ), dtype=bool)
    allowed = jnp.concatenate([text_rows, slot_rows], axis=1)
    return allowed & key_valid[:, None, :]

def encoder_layer(hidden, keep, weights):
    w_qkv, w_out, w_up, w_down, bias_qv, bias_up, bias_res, norm_gain, norm_shift = weights
    projected = jnp.einsum('gsd,de->gse', hidden, w_qkv, precision=highest)
    queries = low(low_back((projected[..., :D] + bias_qv[0]) * 0.125))
    keys_all = low(low_back(projected[..., D:2 * D]))
    values_all = low(low_back(projected[..., 2 * D:] + bias_qv[1]))
    head_shape = hidden.shape[:2] + (HEADS, HEAD)
    scores = low_back(jnp.einsum('gqhe,gkhe->ghqk', queries.reshape(head_shape), keys_all.reshape(head_shape), precision=highest))
    scores = jnp.where(keep[:, None], scores, masked_score)
    attention = low(jax.nn.softmax(scores, axis=-1))
    context = jnp.einsum('ghqk,gkhe->gqhe', attention, values_all.reshape(head_shape), precision=highest).reshape(hidden.shape)
    context = low(low_back(context))
    attended = low_back(jnp.einsum('gsc,cd->gsd', context, w_out, precision=highest) + bias_res[0])
    normed = layer_norm(hidden + attended, norm_gain[0], norm_shift[0])
    inner = low_back(jnp.einsum('gsd,df->gsf', low(normed), w_up, precision=highest) + bias_up)
    activated = low(jax.nn.gelu(inner))
    expanded = low_back(jnp.einsum('gsf,fd->gsd', activated, w_down, precision=highest) + bias_res[1])
    return layer_norm(normed + expanded, norm_gain[1], norm_shift[1])

def reference(inputs, cotangent, text_mask, seg_count, align, w_qkv, w_out, w_up, w_down, bias_qv, bias_up, bias_res, norm_gain, norm_shift):
    params = tuple((array.astype(jnp.float32) for array in (w_qkv, w_out, w_up, w_down, bias_qv, bias_up, bias_res, norm_gain, norm_shift)))
    keep = build_keep(text_mask, seg_count, align)
    group = math.gcd(DOCS, 16)
    blocks = DOCS // group

    def regroup(array):
        return array.reshape((blocks, group) + array.shape[1:])
    start = regroup(inputs.astype(jnp.float32).reshape(DOCS, SEQ, D))
    keep_blocks = regroup(keep)
    probe = jnp.zeros_like(start)

    def forward(start, params, probe):

        def per_block(pieces):
            block_in, block_keep, block_probe = pieces
            first = low(encoder_layer(block_in, block_keep, tuple((leaf[0] for leaf in params))))
            second = encoder_layer(low_back(first) + block_probe, block_keep, tuple((leaf[1] for leaf in params)))
            return (first, second)
        return lax.map(jax.checkpoint(per_block), (start, keep_blocks, probe))
    (first, second), pullback = jax.vjp(forward, start, params, probe)
    upstream = regroup(cotangent.astype(jnp.float32).reshape(DOCS, SEQ, D))
    grad_start, grad_params, grad_probe = pullback((jnp.zeros_like(first), upstream))

    def flatten_rows(array):
        return array.reshape(TOKENS, D)
    section_out = jnp.stack([flatten_rows(first), flatten_rows(second)]).astype(jnp.bfloat16)
    input_grad = jnp.stack([flatten_rows(grad_start), flatten_rows(grad_probe)]).astype(jnp.bfloat16)
    return (section_out, input_grad, grad_params[0], grad_params[1], grad_params[2], grad_params[3], grad_params[4], grad_params[5], grad_params[6], grad_params[7], grad_params[8])
```

```python
import jax
import jax.numpy as jnp
from jax import lax
from jax.sharding import PartitionSpec as P

D = 768
HEADS = 12
HEAD = 64
TEXT = 176
SLOTS = 64
SEQ = 240
MB = 2
DOC_MB = 1


epsilon = 1e-06
masked_score = -1e30


def passed_along(block, axis, distance):
    devices = range(lax.axis_size(axis))
    route = [(i - distance, i) for i in devices if i - distance in devices]
    return lax.ppermute(block, axis, route)


def layer_norm(values, gain, shift):
    center = values - jnp.mean(values, axis=-1, keepdims=True)
    spread = jnp.mean(center * center, axis=-1, keepdims=True)
    return center * lax.rsqrt(spread + epsilon) * gain + shift


def build_keep(text_mask, seg_count, align):
    documents = align.shape[0]
    slot_iota = jnp.arange(SLOTS, dtype=jnp.int32)
    key_valid = jnp.concatenate([text_mask == 1, slot_iota[None, :] < seg_count[:, None]], axis=1)
    owned_by = align[:, None, :] == slot_iota[None, :, None]
    slot_rows = jnp.concatenate([owned_by, jnp.ones((documents, SLOTS, SLOTS), dtype=bool)], axis=2)
    text_rows = jnp.ones((documents, TEXT, SEQ), dtype=bool)
    allowed = jnp.concatenate([text_rows, slot_rows], axis=1)
    return allowed & key_valid[:, None, :]


def split_heads(array, documents):
    return array.reshape(documents, SEQ, HEADS, HEAD)


def head_scores(queries, keys_all, keep):
    documents = keep.shape[0]
    scores = jnp.einsum(
        "dqhe,dkhe->dhqk",
        split_heads(queries, documents),
        split_heads(keys_all, documents),
        preferred_element_type=jnp.float32,
    )
    return jnp.where(keep[:, None], scores, masked_score)


def layer_forward(tokens_in, keep, weights):
    w_qkv, w_out, w_up, w_down, bias_qv, bias_up, bias_res, norm_gain, norm_shift = weights
    row_count = tokens_in.shape[0]
    documents = keep.shape[0]
    projected = jnp.dot(tokens_in, w_qkv, preferred_element_type=jnp.float32)
    queries = ((projected[:, :D] + bias_qv[0]) * 0.125).astype(jnp.bfloat16)
    keys_all = projected[:, D : 2 * D].astype(jnp.bfloat16)
    values_all = (projected[:, 2 * D :] + bias_qv[1]).astype(jnp.bfloat16)
    scores = head_scores(queries, keys_all, keep)
    log_total = jax.nn.logsumexp(scores, axis=-1, keepdims=True)
    attention = jnp.exp(scores - log_total).astype(jnp.bfloat16)
    context = jnp.einsum(
        "dhqk,dkhe->dqhe",
        attention,
        split_heads(values_all, documents),
        preferred_element_type=jnp.float32,
    )
    context = context.reshape(row_count, D).astype(jnp.bfloat16)
    summed_one = (
        tokens_in.astype(jnp.float32)
        + jnp.dot(context, w_out, preferred_element_type=jnp.float32)
        + bias_res[0]
    )
    normed = layer_norm(summed_one, norm_gain[0], norm_shift[0])
    normed_low = normed.astype(jnp.bfloat16)
    inner = jnp.dot(normed_low, w_up, preferred_element_type=jnp.float32) + bias_up
    activated = jax.nn.gelu(inner).astype(jnp.bfloat16)
    summed_two = (
        normed + jnp.dot(activated, w_down, preferred_element_type=jnp.float32) + bias_res[1]
    )
    layer_out = layer_norm(summed_two, norm_gain[1], norm_shift[1]).astype(jnp.bfloat16)
    return (
        layer_out,
        (
            tokens_in,
            queries,
            keys_all,
            values_all,
            log_total,
            context,
            summed_one,
            normed_low,
            inner,
            activated,
            summed_two,
        ),
    )


def layer_backward(grad_out, saved, keep, weights):
    w_qkv, w_out, w_up, w_down, bias_qv, bias_up, bias_res, norm_gain, norm_shift = weights
    (
        tokens_in,
        queries,
        keys_all,
        values_all,
        log_total,
        context,
        summed_one,
        normed_low,
        inner,
        activated,
        summed_two,
    ) = saved
    row_count = tokens_in.shape[0]
    documents = keep.shape[0]
    gain_wide = norm_gain.astype(jnp.float32)
    shift_wide = norm_shift.astype(jnp.float32)
    unused, second_back = jax.vjp(layer_norm, summed_two, gain_wide[1], shift_wide[1])
    grad_two, gain_two, shift_two = second_back(grad_out.astype(jnp.float32))
    branch_low = grad_two.astype(jnp.bfloat16)
    grad_active = jnp.einsum("rd,fd->rf", branch_low, w_down, preferred_element_type=jnp.float32)
    unused, gelu_back = jax.vjp(jax.nn.gelu, inner)
    inner_low = gelu_back(grad_active)[0].astype(jnp.bfloat16)
    grad_normed = grad_two + jnp.einsum(
        "rf,df->rd", inner_low, w_up, preferred_element_type=jnp.float32
    )
    unused, first_back = jax.vjp(layer_norm, summed_one, gain_wide[0], shift_wide[0])
    grad_one, gain_one, shift_one = first_back(grad_normed)
    attend_low = grad_one.astype(jnp.bfloat16)
    context_low = jnp.einsum(
        "rd,cd->rc", attend_low, w_out, preferred_element_type=jnp.float32
    ).astype(jnp.bfloat16)
    scores = head_scores(queries, keys_all, keep)
    attention_wide = jnp.exp(scores - log_total)
    attention = attention_wide.astype(jnp.bfloat16)
    context_heads = split_heads(context_low, documents)
    grad_attention = jnp.einsum(
        "dqhe,dkhe->dhqk",
        context_heads,
        split_heads(values_all, documents),
        preferred_element_type=jnp.float32,
    )
    grad_values = jnp.einsum(
        "dhqk,dqhe->dkhe", attention, context_heads, preferred_element_type=jnp.float32
    )
    grad_values = grad_values.reshape(row_count, D).astype(jnp.bfloat16)
    row_terms = jnp.sum(attention_wide * grad_attention, axis=-1, keepdims=True)
    grad_scores = (attention_wide * (grad_attention - row_terms)).astype(jnp.bfloat16)
    grad_queries = jnp.einsum(
        "dhqk,dkhe->dqhe",
        grad_scores,
        split_heads(keys_all, documents),
        preferred_element_type=jnp.float32,
    )
    grad_queries = grad_queries.reshape(row_count, D).astype(jnp.bfloat16) * 0.125
    grad_keys = jnp.einsum(
        "dhqk,dqhe->dkhe",
        grad_scores,
        split_heads(queries, documents),
        preferred_element_type=jnp.float32,
    )
    grad_keys = grad_keys.reshape(row_count, D).astype(jnp.bfloat16)
    grad_proj = jnp.concatenate([grad_queries, grad_keys, grad_values], axis=1)
    grad_in = (
        grad_one + jnp.einsum("re,de->rd", grad_proj, w_qkv, preferred_element_type=jnp.float32)
    ).astype(jnp.bfloat16)
    grad_gains = jnp.stack([gain_one, gain_two])
    grad_shifts = jnp.stack([shift_one, shift_two])
    factors = (
        tokens_in,
        grad_proj,
        context,
        attend_low,
        normed_low,
        inner_low,
        activated,
        branch_low,
    )
    return (grad_in, (grad_gains, grad_shifts), factors)


def weight_products(factors):
    tokens_in, grad_proj, context, attend_low, normed_low, inner_low, activated, branch_low = (
        factors
    )
    grad_wqkv = jnp.einsum("rd,re->de", tokens_in, grad_proj, preferred_element_type=jnp.float32)
    grad_wout = jnp.einsum("rc,rd->cd", context, attend_low, preferred_element_type=jnp.float32)
    grad_up = jnp.einsum("rd,rf->df", normed_low, inner_low, preferred_element_type=jnp.float32)
    grad_down = jnp.einsum("rf,rd->fd", activated, branch_low, preferred_element_type=jnp.float32)
    proj_sums = jnp.sum(grad_proj.astype(jnp.float32), axis=0)
    grad_bias_qv = jnp.stack([proj_sums[:D], proj_sums[2 * D :]])
    grad_bias_up = jnp.sum(inner_low.astype(jnp.float32), axis=0)
    grad_bias_res = jnp.stack(
        [
            jnp.sum(attend_low.astype(jnp.float32), axis=0),
            jnp.sum(branch_low.astype(jnp.float32), axis=0),
        ]
    )
    return (grad_wqkv, grad_wout, grad_up, grad_down, grad_bias_qv, grad_bias_up, grad_bias_res)


def ring_levels(total):
    sizes = []
    while total > 1:
        size = max([k for k in range(2, 9) if total % k == 0], default=total)
        sizes.append(size)
        total //= size
    return sizes


def ring_route(total, stride, size):
    order = list(range(size))
    if total == size and size % 2 == 0:
        order = list(range(0, size, 2)) + list(range(size - 1, 0, -2))
    place = [0] * total
    route = []
    for device in range(total):
        place[device] = order.index(device // stride % size)
    for device in range(total):
        after = order[(place[device] + 1) % size]
        base = device - device // stride % size * stride
        target = base + after * stride
        route.append((device * 2, target * 2))
        route.append((target * 2 + 1, device * 2 + 1))
    return (place, route)


def ring_place(total, stride, size):
    place, route = ring_route(total, stride, size)
    at = jnp.asarray(place, jnp.int32)[lax.axis_index("dp")]
    at = jnp.where(lax.axis_index("pair") == 0, at, (size - at) % size)
    return (at, route)


def ring_scatter(terms, total, stride, size):
    at, route = ring_place(total, stride, size)
    parts = range(len(terms))

    def term(part, step):
        index = (at + step + 2 * size) % size
        value = 0.0
        for leaf in terms[part]:
            rows = leaf.shape[0] // size
            piece = lax.dynamic_slice_in_dim(leaf, index * rows, rows, 0)
            value = value + piece.astype(jnp.float32)
        return value

    running = [term(part, 0).astype(jnp.bfloat16) for part in parts]
    for step in range(size - 1):
        for part in parts:
            arrived = lax.ppermute(running[part], ("dp", "pair"), route)
            running[part] = (arrived.astype(jnp.float32) + term(part, -step - 1)).astype(
                jnp.bfloat16
            )
    return running


def ring_gather(pieces, total, stride, size, dtype):
    at, route = ring_place(total, stride, size)
    running = list(pieces)
    totals = [
        jnp.zeros((size * leaf.shape[0],) + leaf.shape[1:], dtype) for leaf in pieces
    ]
    for step in range(size):
        index = (at + 1 - step + 2 * size) % size
        for part, leaf in enumerate(running):
            totals[part] = lax.dynamic_update_slice_in_dim(
                totals[part], leaf.astype(dtype), index * leaf.shape[0], 0
            )
        if step < size - 1:
            running = [lax.ppermute(leaf, ("dp", "pair"), route) for leaf in running]
    return totals


def ring_sum(terms):
    total = lax.axis_size("dp")
    levels = []
    stride = 1
    for size in ring_levels(total):
        levels.append((stride, size))
        stride *= size
    for stride, size in levels:
        pieces = ring_scatter(terms, total, stride, size)
        terms = [(piece,) for piece in pieces]
    for depth, (stride, size) in enumerate(levels[::-1]):
        dtype = jnp.float32 if depth == len(levels) - 1 else jnp.bfloat16
        pieces = ring_gather(pieces, total, stride, size, dtype)
    return pieces


def pair_halves(total, axis):
    half = total.shape[axis] // 2
    me = lax.axis_index("pair")
    own = lax.dynamic_slice_in_dim(total, me * half, half, axis)
    away = lax.dynamic_slice_in_dim(total, (1 - me) * half, half, axis)
    return (own, lax.ppermute(away.astype(jnp.bfloat16), "pair", [(0, 1), (1, 0)]))


def local(
    inputs,
    cotangent,
    text_mask,
    seg_count,
    align,
    w_qkv,
    w_out,
    w_up,
    w_down,
    bias_qv,
    bias_up,
    bias_res,
    norm_gain,
    norm_shift,
):
    section_index = lax.axis_index("pipe")
    layer_weights = (
        lax.all_gather(w_qkv[0], "pair", axis=0, tiled=True),
        lax.all_gather(w_out[0], "pair", axis=0, tiled=True),
        lax.all_gather(w_up[0], "pair", axis=0, tiled=True),
        lax.all_gather(w_down[0], "pair", axis=0, tiled=True),
        lax.all_gather(bias_qv[0], "pair", axis=1, tiled=True),
        lax.all_gather(bias_up[0], "pair", axis=0, tiled=True),
        lax.all_gather(bias_res[0], "pair", axis=1, tiled=True),
        lax.all_gather(norm_gain[0], "pair", axis=1, tiled=True),
        lax.all_gather(norm_shift[0], "pair", axis=1, tiled=True),
    )
    layer_weights = tuple(layer_weights)
    keep_all = build_keep(text_mask, seg_count, align)
    row_count = DOC_MB * SEQ
    received = jnp.zeros((row_count, D), jnp.bfloat16)
    kept_list = []
    output_list = []
    for moment in range(MB + 1):
        batch_index = jnp.clip(moment - section_index, 0, MB - 1)
        own_rows = lax.dynamic_slice_in_dim(inputs, min(moment, MB - 1) * row_count, row_count, 0)
        layer_in = jnp.where(section_index == 0, own_rows, received)
        keep_now = lax.dynamic_slice_in_dim(keep_all, batch_index * DOC_MB, DOC_MB, 0)
        layer_out, kept = layer_forward(layer_in, keep_now, layer_weights)
        kept_list.append(kept)
        output_list.append(layer_out)
        if moment < MB:
            received = passed_along(layer_out, "pipe", 1)
    section_out = jnp.concatenate(
        [
            jnp.where(section_index == 0, output_list[number], output_list[number + 1])
            for number in range(MB)
        ],
        axis=0,
    )
    received = jnp.zeros((row_count, D), jnp.bfloat16)
    norm_total = None
    grad_list = []
    factor_list = []
    for moment in range(MB + 1):
        raw_index = MB - moment - section_index
        valid = (raw_index >= 0) & (raw_index < MB)
        batch_index = jnp.clip(raw_index, 0, MB - 1)
        own_grad = lax.dynamic_slice_in_dim(
            cotangent, max(MB - 1 - moment, 0) * row_count, row_count, 0
        )
        grad_now = jnp.where(section_index == 1, own_grad, received)
        grad_now = jnp.where(valid, grad_now, jnp.zeros_like(grad_now))
        saved = kept_list[MB - moment]
        keep_now = lax.dynamic_slice_in_dim(keep_all, batch_index * DOC_MB, DOC_MB, 0)
        grad_in, norm_terms, factors = layer_backward(grad_now, saved, keep_now, layer_weights)
        if norm_total is None:
            norm_total = norm_terms
        else:
            norm_total = jax.tree.map(jnp.add, norm_total, norm_terms)
        grad_list.append(grad_in)
        factor_list.append(factors)
        if moment < MB:
            received = passed_along(grad_in, "pipe", -1)
    input_grad = jnp.concatenate(
        [
            jnp.where(section_index == 0, grad_list[MB - number], grad_list[MB - number - 1])
            for number in range(MB)
        ],
        axis=0,
    )
    chosen = jax.tree.map(
        lambda *leaves: jnp.concatenate(
            [
                jnp.where(section_index == 0, leaves[number + 1], leaves[number])
                for number in range(MB)
            ],
            axis=0,
        ),
        *factor_list,
    )
    grad_total = weight_products(chosen) + (norm_total[0], norm_total[1])
    halves = [pair_halves(leaf, 0) for leaf in grad_total[:4]]
    order = (3, 2, 0, 1)
    summed_big = ring_sum([halves[k] for k in order])
    big = [None] * 4
    for slot, k in enumerate(order):
        big[k] = summed_big[slot]
    small_axes = (1, 0, 1, 1, 1)
    shares = [
        lax.psum_scatter(leaf, "pair", scatter_dimension=axis, tiled=True)
        for leaf, axis in zip(grad_total[4:], small_axes)
    ]
    small = lax.psum(tuple(shares), "dp")
    return (section_out[None], input_grad[None]) + tuple(
        (leaf[None] for leaf in tuple(big) + tuple(small))
    )


def solution(mesh):
    return jax.shard_map(
        local,
        mesh=mesh,
        in_specs=(
            P(("dp", "pair"), None),
            P(("dp", "pair"), None),
            P(("dp", "pair"), None),
            P(("dp", "pair")),
            P(("dp", "pair"), None),
            P("pipe", "pair", None),
            P("pipe", "pair", None),
            P("pipe", "pair", None),
            P("pipe", "pair", None),
            P("pipe", None, "pair"),
            P("pipe", "pair"),
            P("pipe", None, "pair"),
            P("pipe", None, "pair"),
            P("pipe", None, "pair"),
        ),
        out_specs=(
            P("pipe", ("dp", "pair"), None),
            P("pipe", ("dp", "pair"), None),
            P("pipe", "pair", None),
            P("pipe", "pair", None),
            P("pipe", "pair", None),
            P("pipe", "pair", None),
            P("pipe", None, "pair"),
            P("pipe", "pair"),
            P("pipe", None, "pair"),
            P("pipe", None, "pair"),
            P("pipe", None, "pair"),
        ),
        check_vma=False,
    )
```

```python
import jax
import jax.numpy as jnp
from jax import lax
from jax.experimental import pallas as pl
from jax.experimental.pallas import tpu as pltpu
from jax.sharding import PartitionSpec as P

D = 768
HEADS = 12
HEAD = 64
FF = 3072
TEXT = 176
SLOTS = 64
SEQ = 240
KEYS = 256
MB = 2
LANES = 128
STEP = 256


epsilon = 1e-06
masked_score = -1e30
gelu_one = 0.7978845608028654
gelu_two = 0.044715
low = jnp.bfloat16
wide = jnp.float32
swap = [(0, 1), (1, 0)]


def passed_along(block, axis, distance):
    devices = range(lax.axis_size(axis))
    route = [(i - distance, i) for i in devices if i - distance in devices]
    return lax.ppermute(block, axis, route)


def dot(left, right):
    return lax.dot_general(left, right, (((1,), (0,)), ((), ())), preferred_element_type=wide)


def dot_rows(left, right):
    return lax.dot_general(left, right, (((1,), (1,)), ((), ())), preferred_element_type=wide)


def dot_columns(left, right):
    return lax.dot_general(left, right, (((0,), (0,)), ((), ())), preferred_element_type=wide)


def column_sum(values):
    return jnp.sum(values, axis=0, keepdims=True)


def at_columns(start, size=STEP):
    return slice(start, start + size)


def in_first():
    return lax.axis_index("pipe") == 0


def forward_doc(moment):
    first, second = (min(moment, MB - 1), max(moment - 1, 0))
    return jnp.where(in_first(), first, second)


def backward_doc(moment):
    first, second = (min(MB - moment, MB - 1), max(MB - 1 - moment, 0))
    return jnp.where(in_first(), first, second)


def score_bias(code_ref, document):
    code = code_ref[pl.ds(document * 8, 1), :]
    slot = lax.broadcasted_iota(jnp.int32, (SEQ, KEYS), 0) - TEXT
    keep = (code > -2) & ((slot < 0) | (code == -1) | (code == slot))
    return jnp.where(keep, 0.0, masked_score)


def head_masks(rows):
    first = lax.broadcasted_iota(jnp.int32, (rows, LANES), 1) < HEAD
    return (first, ~first)


def only(mask, values):
    return jnp.where(mask, values, jnp.zeros_like(values))


def normalize(values):
    center = values - jnp.mean(values, axis=1, keepdims=True)
    scale = lax.rsqrt(jnp.mean(center * center, axis=1, keepdims=True) + epsilon)
    return (center * scale, scale)


def normalize_back(grad, normal, scale):
    flat = jnp.mean(grad, axis=1, keepdims=True)
    along = jnp.mean(grad * normal, axis=1, keepdims=True)
    return scale * (grad - flat - normal * along)


def join_kernel(*refs):
    count = (len(refs) - 1) // 3
    own, other, full, sems = (
        refs[:count],
        refs[count : 2 * count],
        refs[2 * count : 3 * count],
        refs[3 * count],
    )
    me = lax.axis_index("pair")
    copies = []
    for k in range(count):
        rows = own[k].shape[0]
        for part, (source, place) in enumerate(((own[k], me), (other[k], 1 - me))):
            copies.append(
                pltpu.make_async_copy(
                    source,
                    full[k].at[pl.ds(pl.multiple_of(place * rows, rows), rows)],
                    sems.at[2 * k + part],
                )
            )
    for copy in copies:
        copy.start()
    for copy in copies:
        copy.wait()


def attend_kernel(
    moment, own_ref, received_ref, w_ref, code_ref, vec_ref, x_ref, q_ref, k_ref, v_ref, c_ref, l_ref
):
    row = min(moment, MB - 1) * SEQ
    x = jnp.where(in_first(), own_ref[row : row + SEQ, :], received_ref[...])
    x_ref[...] = x
    for start in range(0, D, STEP):
        cols = at_columns(start)
        queries = dot(x, w_ref[:, cols]) + vec_ref[0:1, cols]
        q_ref[:, cols] = (queries * 0.125).astype(low)
        k_ref[0:SEQ, cols] = dot(x, w_ref[:, at_columns(D + start)]).astype(low)
        values = dot(x, w_ref[:, at_columns(2 * D + start)]) + vec_ref[1:2, cols]
        v_ref[0:SEQ, cols] = values.astype(low)
    k_ref[SEQ:KEYS, :] = jnp.zeros((KEYS - SEQ, D), low)
    v_ref[SEQ:KEYS, :] = jnp.zeros((KEYS - SEQ, D), low)
    bias = score_bias(code_ref, forward_doc(moment))
    of_query = head_masks(SEQ)
    of_key = head_masks(KEYS)
    ones = jnp.ones((KEYS, LANES), low)
    for start in range(0, D, LANES):
        cols = at_columns(start, LANES)
        q, k, v = (q_ref[:, cols], k_ref[:, cols], v_ref[:, cols])
        total = None
        tops = []
        for head in range(2):
            scores = dot_rows(only(of_query[head], q), k) + bias
            top = jnp.max(scores, axis=1, keepdims=True)
            weight = jnp.exp(scores - top).astype(low)
            both = jnp.concatenate([only(of_key[head], v), only(of_key[head], ones)], axis=1)
            part = dot(weight, both)
            total = part if total is None else total + part
            tops.append(top)
        sums = total[:, LANES:]
        c_ref[:, cols] = (total[:, :LANES] / sums).astype(low)
        l_ref[:, cols] = jnp.where(of_query[0], tops[0], tops[1]) + jnp.log(sums)


def feed_kernel(
    x_ref, c_ref, wo_ref, wu_ref, wd_ref, vec_ref, bu_ref,
    y_ref, h1_ref, n1_ref, f_ref, s_ref, h2_ref, rs_ref, r_ref,
):
    c = c_ref[...]
    for start in range(0, D, STEP):
        cols = at_columns(start)
        r_ref[:, cols] = x_ref[:, cols].astype(wide) + dot(c, wo_ref[:, cols]) + vec_ref[2:3, cols]
    h1, scale_one = normalize(r_ref[...])
    h1_ref[...] = h1
    n1 = h1 * vec_ref[4:5, :] + vec_ref[6:7, :]
    n1_low = n1.astype(low)
    n1_ref[...] = n1_low
    r_ref[...] = n1 + vec_ref[3:4, :]
    for start in range(0, FF, STEP):
        cols = at_columns(start)
        u = dot(n1_low, wu_ref[:, cols]) + bu_ref[0:1, cols]
        square = u * u
        bend = jnp.tanh(u * (gelu_one + gelu_one * gelu_two * square))
        half = 0.5 + 0.5 * bend
        f_ref[:, cols] = (u * half).astype(low)
        slope = half + u * (half * (1.0 - bend)) * (gelu_one + 3 * gelu_one * gelu_two * square)
        s_ref[:, cols] = slope.astype(low)
    f = f_ref[...]
    for start in range(0, D, STEP):
        cols = at_columns(start)
        r_ref[:, cols] = r_ref[:, cols] + dot(f, wd_ref[:, cols])
    h2, scale_two = normalize(r_ref[...])
    h2_ref[...] = h2
    y_ref[...] = (h2 * vec_ref[5:6, :] + vec_ref[7:8, :]).astype(low)
    rs_ref[...] = jnp.where(head_masks(SEQ)[0], scale_one, scale_two)


def top_back_kernel(moment, own_ref, received_ref, h2_ref, rs_ref, vec_ref, dr2_ref, e2_ref, sm_ref):
    row = max(MB - 1 - moment, 0) * SEQ
    g = jnp.where(in_first(), received_ref[...], own_ref[row : row + SEQ, :]).astype(wide)
    h2 = h2_ref[...]
    dr2 = normalize_back(g * vec_ref[5:6, :], h2, rs_ref[:, HEAD : HEAD + 1])
    e2 = dr2.astype(low)
    dr2_ref[...] = dr2
    e2_ref[...] = e2
    sm_ref[0:1, :] = column_sum(g * h2)
    sm_ref[1:2, :] = column_sum(g)
    sm_ref[2:3, :] = column_sum(e2.astype(wide))


def feed_back_kernel(
    dr2_ref, e2_ref, s_ref, h1_ref, rs_ref, wd_ref, wu_ref, vec_ref,
    du_ref, dr1_ref, e1_ref, sm_ref, smu_ref,
):
    e2 = e2_ref[...]
    for start in range(0, FF, STEP):
        cols = at_columns(start)
        du = (dot_rows(e2, wd_ref[cols, :]) * s_ref[:, cols].astype(wide)).astype(low)
        du_ref[:, cols] = du
        smu_ref[0:1, cols] = column_sum(du.astype(wide))
    du = du_ref[...]
    for start in range(0, D, STEP):
        cols = at_columns(start)
        dr1_ref[:, cols] = dr2_ref[:, cols] + dot_rows(du, wu_ref[cols, :])
    g = dr1_ref[...]
    h1 = h1_ref[...]
    dr1 = normalize_back(g * vec_ref[4:5, :], h1, rs_ref[:, 0:1])
    e1 = dr1.astype(low)
    dr1_ref[...] = dr1
    e1_ref[...] = e1
    sm_ref[0:1, :] = column_sum(g * h1)
    sm_ref[1:2, :] = column_sum(g)
    sm_ref[2:3, :] = column_sum(e1.astype(wide))


def attend_back_kernel(
    moment, dr1_ref, e1_ref, q_ref, k_ref, v_ref, c_ref, l_ref, wo_ref, wq_ref, code_ref,
    dp_ref, gi_ref, sm_ref, dc_ref,
):
    e1 = e1_ref[...]
    for start in range(0, D, STEP):
        cols = at_columns(start)
        dc_ref[:, cols] = dot_rows(e1, wo_ref[cols, :]).astype(low)
    bias = score_bias(code_ref, backward_doc(moment))
    of_query = head_masks(SEQ)
    of_key = head_masks(KEYS)
    for start in range(0, D, LANES):
        cols = at_columns(start, LANES)
        q, k, v, dc = (q_ref[:, cols], k_ref[:, cols], v_ref[:, cols], dc_ref[:, cols])
        product = dc.astype(wide) * c_ref[:, cols].astype(wide)
        dq, dk, dv = (0.0, 0.0, 0.0)
        for head in range(2):
            q_head, dc_head = (only(of_query[head], q), only(of_query[head], dc))
            logs = l_ref[:, start + HEAD * head : start + HEAD * head + 1]
            p = jnp.exp(dot_rows(q_head, k) + bias - logs)
            inner = jnp.sum(only(of_query[head], product), axis=1, keepdims=True)
            ds = (p * (dot_rows(dc_head, v) - inner)).astype(low)
            dq = dq + dot(ds, only(of_key[head], k))
            dk = dk + dot_columns(ds, q_head)
            dv = dv + dot_columns(p.astype(low), dc_head)
        dq = dq.astype(low) * low(0.125)
        dv = dv[:SEQ].astype(low)
        dp_ref[:, cols] = dq
        dp_ref[:, at_columns(D + start, LANES)] = dk[:SEQ].astype(low)
        dp_ref[:, at_columns(2 * D + start, LANES)] = dv
        sm_ref[0:1, cols] = column_sum(dq.astype(wide))
        sm_ref[1:2, cols] = column_sum(dv.astype(wide))
    dp = dp_ref[...]
    for start in range(0, D, STEP):
        cols = at_columns(start)
        gi_ref[:, cols] = (dr1_ref[:, cols] + dot_rows(dp, wq_ref[cols, :])).astype(low)


def weight_kernel(pairs, *refs):
    me = lax.axis_index("pair")
    first = in_first()
    own_ref, away_ref = refs[-2:]
    for part, owner in ((away_ref, 1 - me), (own_ref, me)):
        column = 0
        for k in range(pairs):
            left = refs[6 * k : 6 * k + 3]
            right = refs[6 * k + 3 : 6 * k + 6]
            half = left[0].shape[1] // 2
            width = right[0].shape[1]
            block = 384
            for row in range(0, half, block):
                at = pl.ds(pl.multiple_of(owner * half + row, LANES), block)
                moved = jnp.where(first, left[2][:, at], left[0][:, at])
                lefts = jnp.concatenate([left[1][:, at], moved], axis=0)
                for start in range(0, width, STEP):
                    cols = at_columns(start)
                    moved = jnp.where(first, right[2][:, cols], right[0][:, cols])
                    rights = jnp.concatenate([right[1][:, cols], moved], axis=0)
                    part[row : row + block, at_columns(column + start)] = dot_columns(
                        lefts, rights
                    ).astype(low)
            column += width


def near(shape, dtype):
    return pltpu.VMEM(shape, dtype)


def far(shape, dtype):
    return jax.ShapeDtypeStruct(shape, dtype)


def run(kernel, name, operands, outputs, scratch=(), flops=0, placed=True):
    space = pltpu.VMEM if placed else pl.ANY
    if placed:
        operands = [pltpu.with_memory_space_constraint(leaf, pltpu.VMEM) for leaf in operands]
    return pl.pallas_call(
        kernel,
        out_shape=tuple(outputs),
        in_specs=[pl.BlockSpec(memory_space=space)] * len(operands),
        out_specs=tuple(pl.BlockSpec(memory_space=pltpu.VMEM) for leaf in outputs),
        scratch_shapes=list(scratch),
        name=name,
        cost_estimate=pl.CostEstimate(flops=flops, bytes_accessed=0, transcendentals=0),
        compiler_params=pltpu.CompilerParams(vmem_limit_bytes=12 << 20),
    )(*operands)


def join_halves(name, own, other):
    outputs = [near((2 * leaf.shape[0], leaf.shape[1]), leaf.dtype) for leaf in own]
    scratch = [pltpu.SemaphoreType.DMA((2 * len(own),))]
    return run(join_kernel, name, list(own) + list(other), outputs, scratch, placed=False)


def attend(moment, own, received, w_qkv, code, vec):
    rows = near((SEQ, D), low)
    keys = near((KEYS, D), low)
    outputs = [rows, rows, keys, keys, rows, near((SEQ, D), wide)]
    return run(
        lambda *refs: attend_kernel(moment, *refs),
        "attend",
        [own, received, w_qkv, code, vec],
        outputs,
        flops=2 * SEQ * D * (3 * D + 4 * KEYS),
    )


def feed(x, c, w_out, w_up, w_down, vec, bu):
    rows = near((SEQ, D), low)
    rows_wide = near((SEQ, D), wide)
    inner = near((SEQ, FF), low)
    outputs = [rows, rows_wide, rows, inner, inner, rows_wide, near((SEQ, LANES), wide)]
    return run(
        feed_kernel,
        "feed",
        [x, c, w_out, w_up, w_down, vec, bu],
        outputs,
        [pltpu.VMEM((SEQ, D), wide)],
        flops=2 * SEQ * D * (D + 2 * FF),
    )


def top_back(moment, own, received, h2, rs, vec):
    outputs = [near((SEQ, D), wide), near((SEQ, D), low), near((8, D), wide)]
    return run(
        lambda *refs: top_back_kernel(moment, *refs),
        "top_back",
        [own, received, h2, rs, vec],
        outputs,
        flops=2 * SEQ * D * D,
    )


def feed_back(dr2, e2, slope, h1, rs, w_down, w_up, vec):
    outputs = [
        near((SEQ, FF), low),
        near((SEQ, D), wide),
        near((SEQ, D), low),
        near((8, D), wide),
        near((8, FF), wide),
    ]
    return run(
        feed_back_kernel,
        "feed_back",
        [dr2, e2, slope, h1, rs, w_down, w_up, vec],
        outputs,
        flops=2 * SEQ * D * 2 * FF,
    )


def attend_back(moment, dr1, e1, q, k, v, c, logs, w_out, w_qkv, code):
    outputs = [near((SEQ, 3 * D), low), near((SEQ, D), low), near((8, D), wide)]
    return run(
        lambda *refs: attend_back_kernel(moment, *refs),
        "attend_back",
        [dr1, e1, q, k, v, c, logs, w_out, w_qkv, code],
        outputs,
        [pltpu.VMEM((SEQ, D), low)],
        flops=2 * SEQ * D * (4 * D + 10 * KEYS),
    )


def weight_halves(name, pairs):
    half = pairs[0][0][0].shape[1] // 2
    width = sum(right[0].shape[1] for left, right in pairs)
    operands = [leaf for left, right in pairs for leaf in tuple(left) + tuple(right)]
    return run(
        lambda *refs: weight_kernel(len(pairs), *refs),
        name,
        operands,
        [far((half, width), low), far((half, width), low)],
        flops=2 * MB * SEQ * 2 * half * width,
    )


def ring_levels(total):
    sizes = []
    while total > 1:
        size = max([k for k in range(2, 9) if total % k == 0], default=total)
        sizes.append(size)
        total //= size
    return sizes


def ring_route(total, stride, size):
    order = list(range(size))
    if total == size and size % 2 == 0:
        order = list(range(0, size, 2)) + list(range(size - 1, 0, -2))
    place = [0] * total
    route = []
    for device in range(total):
        place[device] = order.index(device // stride % size)
    for device in range(total):
        after = order[(place[device] + 1) % size]
        base = device - device // stride % size * stride
        target = base + after * stride
        route.append((device * 2, target * 2))
        route.append((target * 2 + 1, device * 2 + 1))
    return (place, route)


def ring_place(total, stride, size):
    place, route = ring_route(total, stride, size)
    at = jnp.asarray(place, jnp.int32)[lax.axis_index("dp")]
    at = jnp.where(lax.axis_index("pair") == 0, at, (size - at) % size)
    return (at, route)


def ring_scatter(terms, total, stride, size):
    at, route = ring_place(total, stride, size)
    parts = range(len(terms))

    def term(part, step):
        index = (at + step + 2 * size) % size
        value = 0.0
        for leaf in terms[part]:
            rows = leaf.shape[0] // size
            piece = lax.dynamic_slice_in_dim(leaf, index * rows, rows, 0)
            value = value + piece.astype(jnp.float32)
        return value

    running = [term(part, 0).astype(jnp.bfloat16) for part in parts]
    for step in range(size - 1):
        for part in parts:
            arrived = lax.ppermute(running[part], ("dp", "pair"), route)
            running[part] = (arrived.astype(jnp.float32) + term(part, -step - 1)).astype(
                jnp.bfloat16
            )
    return running


def ring_gather(pieces, total, stride, size, dtype):
    at, route = ring_place(total, stride, size)
    running = list(pieces)
    totals = [
        jnp.zeros((size * leaf.shape[0],) + leaf.shape[1:], dtype) for leaf in pieces
    ]
    for step in range(size):
        index = (at + 1 - step + 2 * size) % size
        for part, leaf in enumerate(running):
            totals[part] = lax.dynamic_update_slice_in_dim(
                totals[part], leaf.astype(dtype), index * leaf.shape[0], 0
            )
        if step < size - 1:
            running = [lax.ppermute(leaf, ("dp", "pair"), route) for leaf in running]
    return totals


def ring_sum(terms):
    total = lax.axis_size("dp")
    levels = []
    stride = 1
    for size in ring_levels(total):
        levels.append((stride, size))
        stride *= size
    for stride, size in levels:
        pieces = ring_scatter(terms, total, stride, size)
        terms = [(piece,) for piece in pieces]
    for depth, (stride, size) in enumerate(levels[::-1]):
        dtype = jnp.float32 if depth == len(levels) - 1 else jnp.bfloat16
        pieces = ring_gather(pieces, total, stride, size, dtype)
    return pieces


def beside(own, other, axis):
    ahead = lax.axis_index("pair") == 0
    return jnp.where(
        ahead,
        jnp.concatenate([own, other], axis=axis),
        jnp.concatenate([other, own], axis=axis),
    )


def own_and_away(total, axis):
    half = total.shape[axis] // 2
    me = lax.axis_index("pair")
    own = lax.dynamic_slice_in_dim(total, me * half, half, axis)
    away = lax.dynamic_slice_in_dim(total, (1 - me) * half, half, axis)
    return (own, away)


def sum_small(values):
    total = lax.axis_size("dp")
    if total & (total - 1):
        return lax.psum(values, "dp")
    stride = 1
    while stride < total:
        values = values + lax.ppermute(values, "dp", [(i, i ^ stride) for i in range(total)])
        stride *= 2
    return values


def local(
    inputs,
    cotangent,
    text_mask,
    seg_count,
    align,
    w_qkv,
    w_out,
    w_up,
    w_down,
    bias_qv,
    bias_up,
    bias_res,
    norm_gain,
    norm_shift,
):
    section_index = lax.axis_index("pipe")
    packed = jnp.concatenate(
        [bias_qv[0], bias_res[0], norm_gain[0], norm_shift[0], bias_up[0].reshape(4, D // 2)]
    )
    halves = (packed, w_qkv[0], w_out[0], w_up[0], w_down[0])
    others = [lax.ppermute(leaf, "pair", swap) for leaf in halves]
    vec = beside(packed[:8], others[0][:8], 1).astype(wide)
    bu = beside(packed[8:].reshape(1, FF // 2), others[0][8:].reshape(1, FF // 2), 1).astype(wide)
    (wq,) = join_halves("join_qkv", halves[1:2], others[1:2])
    wo, wu, wd = join_halves("join_feed", halves[2:], others[2:])

    slot_iota = jnp.arange(SLOTS, dtype=jnp.int32)
    code = jnp.concatenate(
        [
            jnp.where(text_mask == 1, align, -2),
            jnp.where(slot_iota[None, :] < seg_count[:, None], -1, -2),
            jnp.full((MB, KEYS - SEQ), -2, jnp.int32),
        ],
        axis=1,
    )
    code = jnp.repeat(code, 8, axis=0)

    received = inputs[:SEQ]
    saved = []
    outs = []
    for moment in range(MB + 1):
        x, q, k, v, c, logs = attend(moment, inputs, received, wq, code, vec)
        y, h1, n1, f, slope, h2, rs = feed(x, c, wo, wu, wd, vec, bu)
        saved.append((x, q, k, v, c, logs, h1, n1, f, slope, h2, rs))
        outs.append(y)
        if moment < MB:
            received = passed_along(y, "pipe", 1)
    is_first = section_index == 0
    section_out = jnp.concatenate(
        [jnp.where(is_first, outs[number], outs[number + 1]) for number in range(MB)]
    )

    received = cotangent[:SEQ]
    grads = []
    factors = []
    small = []
    for moment in range(MB + 1):
        x, q, k, v, c, logs, h1, n1, f, slope, h2, rs = saved[MB - moment]
        dr2, e2, small_top = top_back(moment, cotangent, received, h2, rs, vec)
        factors.append([x, None, c, None, n1, None, f, e2])
        if moment == MB:
            lefts, rights = [[leaf[at] for leaf in factors] for at in (6, 7)]
            down_own, down_away = weight_halves("weight_down", [(lefts, rights)])
        du, dr1, e1, small_feed, small_up = feed_back(dr2, e2, slope, h1, rs, wd, wu, vec)
        factors[-1][5] = du
        if moment == MB:
            lefts, rights = [[leaf[at] for leaf in factors] for at in (4, 5)]
            up_own, up_away = weight_halves("weight_up", [(lefts, rights)])
        dp, gi, small_attend = attend_back(moment, dr1, e1, q, k, v, c, logs, wo, wq, code)
        factors[-1][1] = dp
        factors[-1][3] = e1
        grads.append(gi)
        small.append((small_top, small_feed, small_attend, small_up))
        if moment < MB:
            received = passed_along(gi, "pipe", -1)
    pairs = [[[leaf[at] for leaf in factors] for at in (k, k + 1)] for k in (0, 2)]
    rest_own, rest_away = weight_halves("weight_rest", pairs)
    input_grad = jnp.concatenate(
        [
            jnp.where(is_first, grads[MB - number], grads[MB - number - 1])
            for number in range(MB)
        ]
    )

    terms = [
        (own, lax.ppermute(away, "pair", swap))
        for own, away in ((down_own, down_away), (up_own, up_away), (rest_own, rest_away))
    ]
    grad_down, grad_up, rest = ring_sum(terms)

    tops, feeds, attends, ups = [
        small[1][at] + jnp.where(is_first, small[2][at], small[0][at]) for at in range(4)
    ]
    rows = jnp.stack(
        [attends[0], attends[1], feeds[2], tops[2], feeds[0], tops[0], feeds[1], tops[1]]
    )
    rows_own, rows_away = own_and_away(rows, 1)
    up_sum_own, up_sum_away = own_and_away(ups[0], 0)
    flat_own = jnp.concatenate([rows_own.reshape(-1), up_sum_own])
    flat_away = jnp.concatenate([rows_away.reshape(-1), up_sum_away])
    flat = sum_small(flat_own + lax.ppermute(flat_away, "pair", swap))
    rows = flat[: 4 * D].reshape(8, D // 2)
    summed = (
        rest[:, : 3 * D],
        rest[:, 3 * D :],
        grad_up,
        grad_down,
        rows[0:2],
        flat[4 * D :],
        rows[2:4],
        rows[4:6],
        rows[6:8],
    )
    return (section_out[None], input_grad[None]) + tuple((leaf[None] for leaf in summed))


def solution(mesh):
    return jax.shard_map(
        local,
        mesh=mesh,
        in_specs=(
            P(("dp", "pair"), None),
            P(("dp", "pair"), None),
            P(("dp", "pair"), None),
            P(("dp", "pair")),
            P(("dp", "pair"), None),
            P("pipe", "pair", None),
            P("pipe", "pair", None),
            P("pipe", "pair", None),
            P("pipe", "pair", None),
            P("pipe", None, "pair"),
            P("pipe", "pair"),
            P("pipe", None, "pair"),
            P("pipe", None, "pair"),
            P("pipe", None, "pair"),
        ),
        out_specs=(
            P("pipe", ("dp", "pair"), None),
            P("pipe", ("dp", "pair"), None),
            P("pipe", "pair", None),
            P("pipe", "pair", None),
            P("pipe", "pair", None),
            P("pipe", "pair", None),
            P("pipe", None, "pair"),
            P("pipe", "pair"),
            P("pipe", None, "pair"),
            P("pipe", None, "pair"),
            P("pipe", None, "pair"),
        ),
        check_vma=False,
    )
```

```python
import jax
import jax.numpy as jnp
from jax import lax
from jax.experimental import pallas as pl
from jax.experimental.pallas import tpu as pltpu
from jax.sharding import PartitionSpec as P

D = 768
HEADS = 12
HEAD = 64
FF = 3072
TEXT = 176
SLOTS = 64
SEQ = 240
KEYS = 256
MB = 2
LANES = 128
STEP = 256


epsilon = 1e-06
masked_score = -1e30
gelu_one = 0.7978845608028654
gelu_two = 0.044715
low = jnp.bfloat16
wide = jnp.float32
swap = [(0, 1), (1, 0)]
combine_cost = 1 << 35
store_cost = 1 << 29


def passed_along(block, axis, distance):
    devices = range(lax.axis_size(axis))
    route = [(i - distance, i) for i in devices if i - distance in devices]
    return lax.ppermute(block, axis, route)


def after(value, earlier):
    return value if earlier is None else lax.optimization_barrier((value, earlier))[0]


def dot(left, right):
    return lax.dot_general(left, right, (((1,), (0,)), ((), ())), preferred_element_type=wide)


def dot_rows(left, right):
    return lax.dot_general(left, right, (((1,), (1,)), ((), ())), preferred_element_type=wide)


def dot_columns(left, right):
    return lax.dot_general(left, right, (((0,), (0,)), ((), ())), preferred_element_type=wide)


def column_sum(values):
    return jnp.sum(values, axis=0, keepdims=True)


def at_columns(start, size=STEP):
    return slice(start, start + size)


def score_bias(code_ref, document):
    code = code_ref[8 * document : 8 * document + 1, :]
    slot = lax.broadcasted_iota(jnp.int32, (SEQ, KEYS), 0) - TEXT
    keep = (code > -2) & ((slot < 0) | (code == -1) | (code == slot))
    return jnp.where(keep, 0.0, masked_score)


def head_masks(rows):
    first = lax.broadcasted_iota(jnp.int32, (rows, LANES), 1) < HEAD
    return (first, ~first)


def only(mask, values):
    return jnp.where(mask, values, jnp.zeros_like(values))


def normalize(values):
    center = values - jnp.mean(values, axis=1, keepdims=True)
    scale = lax.rsqrt(jnp.mean(center * center, axis=1, keepdims=True) + epsilon)
    return (center * scale, scale)


def normalize_back(grad, normal, scale):
    flat = jnp.mean(grad, axis=1, keepdims=True)
    along = jnp.mean(grad * normal, axis=1, keepdims=True)
    return scale * (grad - flat - normal * along)


def rows_of(document, size=SEQ):
    return slice(document * size, document * size + size)


def pack_kernel(count_ref, *refs):
    sources, (packed_ref, code_ref), held, sems = (refs[:7], refs[7:9], refs[9:16], refs[16])
    copies = [
        pltpu.make_async_copy(source, target, sems.at[k])
        for k, (source, target) in enumerate(zip(sources, held))
    ]
    for copy in copies:
        copy.start()
    for copy in copies:
        copy.wait()
    half = D // 2
    for place, ref in enumerate(held[:4]):
        packed_ref[2 * place : 2 * place + 2, :] = ref[...].astype(wide)
    for place in range(FF // D):
        packed_ref[8 + place : 9 + place, :] = held[4][
            0:1, half * place : half * place + half
        ].astype(wide)
    packed_ref[12:16, :] = jnp.zeros((4, half), wide)
    code = jnp.where(held[5][...] == 1, held[6][...], -2)
    slot = lax.broadcasted_iota(jnp.int32, (1, SLOTS), 1)
    for document in range(MB):
        rows = slice(8 * document, 8 * document + 8)
        code_ref[rows, :] = jnp.full((8, KEYS), -2, jnp.int32)
        code_ref[8 * document : 8 * document + 1, 0:TEXT] = code[document : document + 1, :]
        code_ref[8 * document : 8 * document + 1, TEXT:SEQ] = jnp.where(
            slot < count_ref[document], -1, -2
        )


def unpack_kernel(own_ref, other_ref, vec_ref, bu_ref):
    half = D // 2
    me = lax.axis_index("pair")
    for ref, place in ((own_ref, me), (other_ref, 1 - me)):
        vec_ref[:, pl.ds(pl.multiple_of(place * half, LANES), half)] = ref[0:8, :]
        for row in range(FF // D):
            start = place * (FF // 2) + row * half
            bu_ref[0:1, pl.ds(pl.multiple_of(start, LANES), half)] = ref[8 + row : 9 + row, :]


def join_kernel(count, place_of, *refs):
    half, full, sems = (refs[:count], refs[-count - 1 : -1], refs[-1])
    place = place_of(lax.axis_index("pair"))
    copies = []
    for k in range(count):
        rows = half[k].shape[0]
        if rows == full[k].shape[0]:
            target = full[k]
        else:
            target = full[k].at[pl.ds(pl.multiple_of(place * rows, rows), rows)]
        copies.append(pltpu.make_async_copy(half[k], target, sems.at[k]))
    for copy in copies:
        copy.start()
    for copy in copies:
        copy.wait()


def attend_kernel(
    document, source_row, source_ref, w_ref, code_ref, vec_ref,
    x_ref, q_ref, k_ref, v_ref, c_ref, l_ref,
):
    rows, keys = (rows_of(document), rows_of(document, KEYS))
    real = slice(document * KEYS, document * KEYS + SEQ)
    rest = slice(document * KEYS + SEQ, document * KEYS + KEYS)
    x = source_ref[source_row : source_row + SEQ, :]
    x_ref[rows, :] = x
    for start in range(0, D, STEP):
        cols = at_columns(start)
        queries = dot(x, w_ref[:, cols]) + vec_ref[0:1, cols]
        q_ref[rows, cols] = (queries * 0.125).astype(low)
        k_ref[real, cols] = dot(x, w_ref[:, at_columns(D + start)]).astype(low)
        values = dot(x, w_ref[:, at_columns(2 * D + start)]) + vec_ref[1:2, cols]
        v_ref[real, cols] = values.astype(low)
    k_ref[rest, :] = jnp.zeros((KEYS - SEQ, D), low)
    v_ref[rest, :] = jnp.zeros((KEYS - SEQ, D), low)
    bias = score_bias(code_ref, document)
    of_query = head_masks(SEQ)
    of_key = head_masks(KEYS)
    ones = jnp.ones((KEYS, LANES), low)
    for start in range(0, D, LANES):
        cols = at_columns(start, LANES)
        q, k, v = (q_ref[rows, cols], k_ref[keys, cols], v_ref[keys, cols])
        total = None
        tops = []
        for head in range(2):
            scores = dot_rows(only(of_query[head], q), k) + bias
            top = jnp.max(scores, axis=1, keepdims=True)
            weight = jnp.exp(scores - top).astype(low)
            both = jnp.concatenate([only(of_key[head], v), only(of_key[head], ones)], axis=1)
            part = dot(weight, both)
            total = part if total is None else total + part
            tops.append(top)
        sums = total[:, LANES:]
        c_ref[rows, cols] = (total[:, :LANES] / sums).astype(low)
        l_ref[rows, cols] = jnp.where(of_query[0], tops[0], tops[1]) + jnp.log(sums)


def feed_up_kernel(
    document, x_ref, c_ref, wo_ref, wu_ref, vec_ref, bu_ref,
    h1_ref, n1_ref, f_ref, s_ref, rs_ref, r_ref,
):
    rows = rows_of(document)
    c = c_ref[rows, :]
    for start in range(0, D, STEP):
        cols = at_columns(start)
        r_ref[:, cols] = (
            x_ref[rows, cols].astype(wide) + dot(c, wo_ref[:, cols]) + vec_ref[2:3, cols]
        )
    h1, scale = normalize(r_ref[...])
    h1_ref[rows, :] = h1
    rs_ref[rows, :] = jnp.broadcast_to(scale, (SEQ, LANES))
    n1 = h1 * vec_ref[4:5, :] + vec_ref[6:7, :]
    n1_low = n1.astype(low)
    n1_ref[rows, :] = n1_low
    r_ref[...] = n1 + vec_ref[3:4, :]
    for start in range(0, FF, STEP):
        cols = at_columns(start)
        u = dot(n1_low, wu_ref[:, cols]) + bu_ref[0:1, cols]
        square = u * u
        bend = jnp.tanh(u * (gelu_one + gelu_one * gelu_two * square))
        half = 0.5 + 0.5 * bend
        f_ref[rows, cols] = (u * half).astype(low)
        slope = half + u * (half * (1.0 - bend)) * (gelu_one + 3 * gelu_one * gelu_two * square)
        s_ref[rows, cols] = slope.astype(low)


def feed_down_kernel(
    document, r_ref, f_ref, wd_ref, vec_ref, section_ref, h2_ref, rs_ref, *rest
):
    sum_ref = rest[-1]
    rows = rows_of(document)
    f = f_ref[rows, :]
    for start in range(0, D, STEP):
        cols = at_columns(start)
        sum_ref[:, cols] = r_ref[:, cols] + dot(f, wd_ref[:, cols])
    h2, scale = normalize(sum_ref[...])
    h2_ref[rows, :] = h2
    rs_ref[rows, :] = jnp.broadcast_to(scale, (SEQ, LANES))
    y = (h2 * vec_ref[5:6, :] + vec_ref[7:8, :]).astype(low)
    section_ref[rows, :] = y
    for y_ref in rest[:-1]:
        y_ref[...] = y


def top_back_kernel(
    document, source_row, source_ref, h2_ref, rs_ref, vec_ref, e2_ref, sm_ref, dr2_ref
):
    rows = rows_of(document)
    g = source_ref[source_row : source_row + SEQ, :].astype(wide)
    h2 = h2_ref[rows, :]
    dr2 = normalize_back(g * vec_ref[5:6, :], h2, rs_ref[rows, 0:1])
    e2 = dr2.astype(low)
    dr2_ref[...] = dr2
    e2_ref[rows, :] = e2
    sm_ref[8 * document : 8 * document + 1, :] = column_sum(g * h2)
    sm_ref[8 * document + 1 : 8 * document + 2, :] = column_sum(g)
    sm_ref[8 * document + 2 : 8 * document + 3, :] = column_sum(e2.astype(wide))


def feed_back_kernel(
    document, dr2_ref, e2_ref, s_ref, h1_ref, rs_ref, wd_ref, wu_ref, vec_ref,
    du_ref, e1_ref, sm_ref, smu_ref, dr1_ref,
):
    rows = rows_of(document)
    e2 = e2_ref[rows, :]
    for start in range(0, FF, STEP):
        cols = at_columns(start)
        du = (dot_rows(e2, wd_ref[cols, :]) * s_ref[rows, cols].astype(wide)).astype(low)
        du_ref[rows, cols] = du
        smu_ref[8 * document : 8 * document + 1, cols] = column_sum(du.astype(wide))
    du = du_ref[rows, :]
    for start in range(0, D, STEP):
        cols = at_columns(start)
        dr1_ref[:, cols] = dr2_ref[:, cols] + dot_rows(du, wu_ref[cols, :])
    g = dr1_ref[...]
    h1 = h1_ref[rows, :]
    dr1 = normalize_back(g * vec_ref[4:5, :], h1, rs_ref[rows, 0:1])
    e1 = dr1.astype(low)
    dr1_ref[...] = dr1
    e1_ref[rows, :] = e1
    sm_ref[8 * document : 8 * document + 1, :] = column_sum(g * h1)
    sm_ref[8 * document + 1 : 8 * document + 2, :] = column_sum(g)
    sm_ref[8 * document + 2 : 8 * document + 3, :] = column_sum(e1.astype(wide))


def attend_back_kernel(
    document, first, last, e1_ref, q_ref, k_ref, v_ref, c_ref, l_ref, wo_ref, code_ref, *refs
):
    dc_ref = refs[-1]
    if last == D:
        dr1_ref, wq_ref, dp_ref, sm_ref, ig_ref = refs[:5]
    else:
        dp_ref, sm_ref = refs[:2]
    rows, keys = (rows_of(document), rows_of(document, KEYS))
    e1 = e1_ref[rows, :]
    for start in range(first, last, STEP):
        cols = at_columns(start)
        dc_ref[:, cols] = dot_rows(e1, wo_ref[cols, :]).astype(low)
    bias = score_bias(code_ref, document)
    of_query = head_masks(SEQ)
    of_key = head_masks(KEYS)
    for start in range(first, last, LANES):
        cols = at_columns(start, LANES)
        q, k, v, dc = (q_ref[rows, cols], k_ref[keys, cols], v_ref[keys, cols], dc_ref[:, cols])
        product = dc.astype(wide) * c_ref[rows, cols].astype(wide)
        dq, dk, dv = (0.0, 0.0, 0.0)
        for head in range(2):
            q_head, dc_head = (only(of_query[head], q), only(of_query[head], dc))
            logs = l_ref[rows, start + HEAD * head : start + HEAD * head + 1]
            p = jnp.exp(dot_rows(q_head, k) + bias - logs)
            inner = jnp.sum(only(of_query[head], product), axis=1, keepdims=True)
            ds = (p * (dot_rows(dc_head, v) - inner)).astype(low)
            dq = dq + dot(ds, only(of_key[head], k))
            dk = dk + dot_columns(ds, q_head)
            dv = dv + dot_columns(p.astype(low), dc_head)
        dq = dq.astype(low) * low(0.125)
        dv = dv[:SEQ].astype(low)
        dp_ref[rows, cols] = dq
        dp_ref[rows, at_columns(D + start, LANES)] = dk[:SEQ].astype(low)
        dp_ref[rows, at_columns(2 * D + start, LANES)] = dv
        sm_ref[8 * document : 8 * document + 1, cols] = column_sum(dq.astype(wide))
        sm_ref[8 * document + 1 : 8 * document + 2, cols] = column_sum(dv.astype(wide))
    if last < D:
        return
    dp = dp_ref[rows, :]
    for start in range(0, D, STEP):
        cols = at_columns(start)
        gi = (dr1_ref[:, cols] + dot_rows(dp, wq_ref[cols, :])).astype(low)
        ig_ref[rows, cols] = gi
        for gi_ref in refs[5:-1]:
            gi_ref[:, cols] = gi


def weight_kernel(pairs, *refs):
    me = lax.axis_index("pair")
    sums = refs[2 * pairs : -2]
    away_ref, own_ref = refs[-2:]
    block = D // 2
    for part, owner in ((away_ref, 1 - me), (own_ref, me)):
        column = 0
        for k in range(pairs):
            left, right = refs[2 * k : 2 * k + 2]
            half = left.shape[1] // 2
            width = right.shape[1]
            for row in range(0, half, block):
                lefts = left[:, pl.ds(pl.multiple_of(owner * half + row, LANES), block)]
                for start in range(0, width, STEP):
                    part[row : row + block, at_columns(column + start)] = dot_columns(
                        lefts, right[:, at_columns(start)]
                    ).astype(low)
            column += width
        if sums:
            small_part(sums, owner, part, column)


def small_part(sums, owner, part, column):
    top_ref, feed_ref, attend_ref, up_ref = sums
    order = (
        (attend_ref, 0), (attend_ref, 1), (feed_ref, 2), (top_ref, 2),
        (feed_ref, 0), (top_ref, 0), (feed_ref, 1), (top_ref, 1),
    )
    places = [(ref, row, D // 2) for ref, row in order] + [(up_ref, 0, FF // 2)]
    lines = []
    for ref, row, half in places:
        for start in range(0, half, LANES):
            cols = pl.ds(pl.multiple_of(owner * half + start, LANES), LANES)
            lines.append(ref[row : row + 1, cols] + ref[row + 8 : row + 9, cols])
    lines.append(jnp.zeros((48 - len(lines), LANES), wide))
    tile = at_columns(column, LANES)
    part[0:48, tile] = jnp.concatenate(lines, axis=0).astype(low)
    part[48:, tile] = jnp.zeros((part.shape[0] - 48, LANES), low)


def ring_row(stride, size, step, rows):
    index = lax.rem(ring_at(stride, size) - step + size, size)
    return pl.multiple_of(index * rows, rows)


def combine_kernel(stride, size, step, *refs):
    terms, arrived, out_ref = (refs[:2], refs[2:-1], refs[-1])
    first = ring_row(stride, size, step, out_ref.shape[0])

    def piece(k, carry):
        here = pl.ds(pl.multiple_of(k * 16, 16), 16)
        there = pl.ds(pl.multiple_of(first + k * 16, 16), 16)
        value = terms[0][there, :].astype(wide) + terms[1][there, :].astype(wide)
        for ref in arrived:
            value = value + ref[here, :].astype(wide)
        out_ref[here, :] = value.astype(low)
        return carry

    lax.fori_loop(0, out_ref.shape[0] // 16, piece, 0)


def store_kernel(stride, size, step, cuts, block_ref, *refs):
    count = len(cuts)
    totals, scratch, sems = (refs[:count], refs[count:-1], refs[-1])
    rows = block_ref.shape[0]
    first = ring_row(stride, size, step - 1, rows)

    def piece(k, carry):
        here = pl.ds(pl.multiple_of(k * 16, 16), 16)
        column = 0
        for part, cut in enumerate(cuts):
            scratch[part][here, :] = block_ref[here, column : column + cut].astype(wide)
            column += cut
        return carry

    lax.fori_loop(0, rows // 16, piece, 0)
    copies = [
        pltpu.make_async_copy(scratch[k], totals[k].at[pl.ds(first, rows)], sems.at[k])
        for k in range(count)
    ]
    for copy in copies:
        copy.start()
    for copy in copies:
        copy.wait()


def finish_kernel(sum_ref, qv_ref, up_ref, res_ref, gain_ref, shift_ref, held_ref, sem):
    copy = pltpu.make_async_copy(sum_ref.at[pl.ds(0, 48)], held_ref, sem.at[0])
    copy.start()
    copy.wait()
    line = 0
    for ref in (qv_ref, res_ref, gain_ref, shift_ref, up_ref):
        for row in range(ref.shape[0]):
            for start in range(0, ref.shape[1], LANES):
                ref[row : row + 1, at_columns(start, LANES)] = held_ref[line : line + 1, :]
                line += 1


def near(shape, dtype):
    return pltpu.VMEM(shape, dtype)


def far(shape, dtype):
    return pltpu.HBM(shape, dtype)


def run(
    kernel, name, operands, outputs, scratch=(), flops=0, section=None, keep=None, spaces=None
):
    keep = [] if keep is None else list(keep)
    count = len(operands)
    spaces = [pltpu.VMEM] * count if spaces is None else list(spaces)
    placed = [getattr(leaf, "memory_space", pltpu.VMEM) for leaf in outputs]
    spaces += placed[: len(keep)]
    operands = [
        leaf
        if space in (None, pltpu.SMEM)
        else pltpu.with_memory_space_constraint(leaf, space)
        for leaf, space in zip(list(operands) + keep, spaces)
    ]

    def body(*refs):
        used = refs[:count] + refs[count + len(keep) :]
        if section is None:
            kernel(*used)
        else:
            pl.when(lax.axis_index("pipe") == section)(lambda: kernel(*used))

    return pl.pallas_call(
        body,
        out_shape=tuple(outputs),
        in_specs=[pl.BlockSpec(memory_space=space or pltpu.VMEM) for space in spaces],
        out_specs=tuple(pl.BlockSpec(memory_space=space) for space in placed),
        scratch_shapes=list(scratch),
        input_output_aliases={count + k: k for k in range(len(keep))},
        name=name,
        cost_estimate=pl.CostEstimate(flops=flops, bytes_accessed=0, transcendentals=0),
        compiler_params=pltpu.CompilerParams(vmem_limit_bytes=4 << 20),
    )(*operands)


def join_halves(name, halves, place_of, space, keep=None, whole=()):
    outputs = [near((2 * leaf.shape[0], leaf.shape[1]), leaf.dtype) for leaf in halves]
    outputs += [near(leaf.shape, leaf.dtype) for leaf in whole]
    halves = list(halves) + list(whole)
    return run(
        lambda *refs: join_kernel(len(halves), place_of, *refs),
        name,
        halves,
        outputs,
        [pltpu.SemaphoreType.DMA((len(halves),))],
        keep=keep,
        flops=1 << 30,
        spaces=[space] * len(halves),
    )


def attend(section, document, source, source_row, w_qkv, code, vec, keep):
    rows = near((MB * SEQ, D), low)
    keys = near((MB * KEYS, D), low)
    return run(
        lambda *refs: attend_kernel(document, source_row, *refs),
        "attend",
        [source, w_qkv, code, vec],
        [rows, rows, keys, keys, rows, near((MB * SEQ, D), wide)],
        flops=2 * SEQ * D * (3 * D + 4 * KEYS),
        section=section,
        keep=keep,
    )


def feed_up(section, document, x, c, w_out, w_up, vec, bu, keep):
    rows = near((MB * SEQ, D), low)
    inner = near((MB * SEQ, FF), low)
    outs = run(
        lambda *refs: feed_up_kernel(document, *refs),
        "feed_up",
        [x, c, w_out, w_up, vec, bu],
        [near((MB * SEQ, D), wide), rows, inner, inner, near((MB * SEQ, LANES), wide)]
        + [near((SEQ, D), wide)],
        flops=2 * SEQ * D * (D + FF),
        section=section,
        keep=keep,
    )
    return (outs[:-1], outs[-1])


def feed_down(section, document, r, f, w_down, vec, keep):
    outs = run(
        lambda *refs: feed_down_kernel(document, *refs),
        "feed_down",
        [r, f, w_down, vec],
        [near((MB * SEQ, D), low), near((MB * SEQ, D), wide), near((MB * SEQ, LANES), wide)]
        + [near((SEQ, D), low)] * (1 - section),
        [pltpu.VMEM((SEQ, D), wide)],
        flops=2 * SEQ * D * FF,
        section=section,
        keep=keep,
    )
    return (outs[:3], outs[3:])


def top_back(section, document, source, source_row, h2, rs, vec, keep):
    outs = run(
        lambda *refs: top_back_kernel(document, source_row, *refs),
        "top_back",
        [source, h2, rs, vec],
        [near((MB * SEQ, D), low), near((MB * 8, D), wide), near((SEQ, D), wide)],
        flops=2 * SEQ * D * D,
        section=section,
        keep=keep,
    )
    return (outs[:-1], outs[-1])


def feed_back(section, document, dr2, e2, slope, h1, rs, w_down, w_up, vec, keep):
    outs = run(
        lambda *refs: feed_back_kernel(document, *refs),
        "feed_back",
        [dr2, e2, slope, h1, rs, w_down, w_up, vec],
        [near((MB * SEQ, FF), low), near((MB * SEQ, D), low), near((MB * 8, D), wide)]
        + [near((MB * 8, FF), wide), near((SEQ, D), wide)],
        flops=2 * SEQ * D * 2 * FF,
        section=section,
        keep=keep,
    )
    return (outs[:-1], outs[-1])


def attend_back(section, document, first, last, e1, saved, w_out, code, extra, keep):
    outputs = [near((MB * SEQ, 3 * D), low), near((MB * 8, D), wide)]
    if last == D:
        outputs += [near((MB * SEQ, D), low)] + [near((SEQ, D), low)] * section
    share = 6 * D if last == D else 0
    return run(
        lambda *refs: attend_back_kernel(document, first, last, *refs),
        "attend_back",
        [e1, *saved, w_out, code, *extra],
        outputs,
        [pltpu.VMEM((SEQ, D), low)],
        flops=2 * SEQ * ((last - first) * (D + 10 * KEYS) + share * D),
        section=section,
        keep=keep,
    )


def weight_halves(name, *pairs, sums=()):
    half = pairs[0][0].shape[1] // 2
    width = sum(right.shape[1] for left, right in pairs) + (LANES if sums else 0)
    return run(
        lambda *refs: weight_kernel(len(pairs), *refs),
        name,
        [leaf for pair in pairs for leaf in pair] + list(sums),
        [near((half, width), low), near((half, width), low)],
        flops=2 * MB * SEQ * 2 * half * width,
    )


def ring_levels(total):
    sizes = []
    while total > 1:
        size = max([k for k in range(2, 9) if total % k == 0], default=total)
        sizes.append(size)
        total //= size
    return sizes


def ring_place(total, stride, size, device):
    own = device // stride % size
    if total == size and size % 2 == 0:
        return jnp.where(own % 2 == 0, own // 2, size - (own + 1) // 2)
    return own


def ring_at(stride, size):
    at = ring_place(lax.axis_size("dp"), stride, size, lax.axis_index("dp"))
    return jnp.where(lax.axis_index("pair") == 0, at, lax.rem(size - at, size))


def ring_route(total, stride, size):
    order = list(range(size))
    if total == size and size % 2 == 0:
        order = list(range(0, size, 2)) + list(range(size - 1, 0, -2))
    route = []
    for device in range(total):
        own = device // stride % size
        target = order[(order.index(own) + 1) % size]
        target = device + (target - own) * stride
        route.append((device * 2, target * 2))
        route.append((target * 2 + 1, device * 2 + 1))
    return route


def ring_combine(stride, size, step, terms, arrived):
    rows = terms[0].shape[0] // size
    width = terms[0].shape[1]
    if rows % 16 == 0:
        return run(
            lambda *refs: combine_kernel(stride, size, step, *refs),
            "combine",
            list(terms) + arrived,
            [near((rows, width), low)],
            flops=combine_cost,
        )[0]
    index = (ring_at(stride, size) - step + size) % size
    value = 0.0
    for leaf in terms:
        piece = lax.dynamic_slice_in_dim(leaf, index * rows, rows, 0)
        value = value + piece.astype(wide)
    for leaf in arrived:
        value = value + leaf.astype(wide)
    return value.astype(low)


def ring_store(stride, size, step, block, cuts, totals, dtype):
    rows = block.shape[0]
    if rows % 16 == 0 and dtype == wide:
        return run(
            lambda *refs: store_kernel(stride, size, step, cuts, *refs),
            "store",
            [block],
            [far((size * rows, cut), wide) for cut in cuts],
            [pltpu.VMEM((rows, cut), wide) for cut in cuts]
            + [pltpu.SemaphoreType.DMA((len(cuts),))],
            flops=store_cost,
            keep=totals,
        )
    if totals is None:
        totals = [jnp.zeros((size * rows, cut), dtype) for cut in cuts]
    index = (ring_at(stride, size) + 1 - step + size) % size
    column = 0
    stored = []
    for leaf, cut in zip(totals, cuts):
        piece = block[:, column : column + cut].astype(dtype)
        stored.append(lax.dynamic_update_slice_in_dim(leaf, piece, index * rows, 0))
        column += cut
    return stored


def ring_steps(terms, widths):
    total = lax.axis_size("dp")
    levels = []
    stride = 1
    for size in ring_levels(total):
        levels.append((stride, size))
        stride *= size
    token = yield None
    terms = [terms[0], after(terms[1], token)]
    running = None
    for stride, size in levels:
        route = ring_route(total, stride, size)
        if running is not None:
            terms = [running, jnp.zeros_like(running)]
        for step in range(size):
            arrived = []
            if step > 0:
                arrived = [after(lax.ppermute(running, ("dp", "pair"), route), token)]
            running = ring_combine(stride, size, step, terms, arrived)
            token = yield running
    for depth, (stride, size) in enumerate(levels[::-1]):
        route = ring_route(total, stride, size)
        last = depth == len(levels) - 1
        dtype, cuts = (wide, widths) if last else (low, [sum(widths)])
        totals = None
        for step in range(size):
            if step > 0:
                running = after(lax.ppermute(running, ("dp", "pair"), route), token)
            totals = ring_store(stride, size, step, running, cuts, totals, dtype)
            if step > 0:
                token = yield tuple(totals)
        running = totals[0]
    return totals


class Steps:
    def __init__(self, steps, left=0):
        self.steps, self.left, self.result = (steps, left, None)
        next(steps)

    def advance(self, token):
        self.left -= 1
        try:
            return self.steps.send(token)
        except StopIteration as done:
            self.result = done.value
            return token


def ring(own, away, widths):
    left = sum(2 * size - 1 for size in ring_levels(lax.axis_size("dp")))
    return Steps(ring_steps([own, from_pair(away)], widths), left)


def finish(sums):
    pairs = jax.ShapeDtypeStruct((2, D // 2), wide)
    outputs = [pairs, jax.ShapeDtypeStruct((1, FF // 2), wide), pairs, pairs, pairs]
    scratch = [pltpu.VMEM((48, LANES), wide), pltpu.SemaphoreType.DMA((1,))]
    return run(finish_kernel, "finish", [sums], outputs, scratch, spaces=[pltpu.HBM])


def export_kernel(*refs):
    count = len(refs) // 2
    copies = [
        pltpu.make_async_copy(refs[k], refs[count + k], refs[-1].at[k]) for k in range(count)
    ]
    for copy in copies:
        copy.start()
    for copy in copies:
        copy.wait()


def export_steps(leaves):
    token = yield None
    stored = run(
        export_kernel,
        "export",
        [after(leaves[0], token)] + list(leaves[1:]),
        [far(leaf.shape, leaf.dtype) for leaf in leaves],
        [pltpu.SemaphoreType.DMA((len(leaves),))],
    )
    token = yield tuple(stored)
    return stored


def from_pair(leaf):
    return lax.ppermute(leaf, "pair", swap)


def local(
    inputs,
    cotangent,
    text_mask,
    seg_count,
    align,
    w_qkv,
    w_out,
    w_up,
    w_down,
    bias_qv,
    bias_up,
    bias_res,
    norm_gain,
    norm_shift,
):
    own = [w_qkv[0], w_out[0], w_up[0], w_down[0]]
    other_qkv = from_pair(own[0])
    params = [bias_qv[0], bias_res[0], norm_gain[0], norm_shift[0], bias_up, text_mask, align]
    packed, code = run(
        pack_kernel,
        "pack",
        [seg_count] + params,
        [near((16, D // 2), wide), near((MB * 8, KEYS), jnp.int32)],
        [pltpu.VMEM(leaf.shape, leaf.dtype) for leaf in params]
        + [pltpu.SemaphoreType.DMA((len(params),))],
        flops=1 << 28,
        spaces=[pltpu.SMEM] + [pltpu.HBM] * len(params),
    )
    packed_other = from_pair(packed)
    mine = lambda me: me
    others = lambda me: 1 - me
    other_out = from_pair(own[1])
    held = [after(own[0], (packed, other_out)), own[1]]
    joined = join_halves("join_own", held, mine, pltpu.HBM, whole=(inputs, cotangent))
    inputs, cotangent = joined[2:]
    vec, bu = run(
        unpack_kernel,
        "unpack",
        [packed, after(packed_other, joined[0])],
        [near((8, D), wide), near((8, FF), wide)],
    )
    other_qkv = after(other_qkv, vec)
    other_up = from_pair(after(own[2], other_qkv))
    wq, wo = join_halves("join_qkv", [other_qkv, other_out], others, pltpu.VMEM, joined[:2])

    attended, raised, lowered = (None, None, None)
    arrived = [None] * MB
    for section in range(2):
        for document in range(MB):
            source, row = (
                (inputs, document * SEQ) if section == 0 else (arrived[document], 0)
            )
            attended = attend(section, document, source, row, wq, code, vec, attended)
            if raised is None:
                held = [after(own[2], attended[0]), own[3]]
                joined = join_halves("join_own", held, mine, pltpu.HBM)
                other_up = after(other_up, attended[0])
                other_down = from_pair(after(own[3], other_up))
                (wu,) = join_halves("join_up", [other_up], others, pltpu.VMEM, joined[:1])
            raised, r = feed_up(
                section, document, attended[0], attended[4], wo, wu, vec, bu, raised
            )
            if lowered is None:
                other_down = after(other_down, r)
                (wd,) = join_halves("join_down", [other_down], others, pltpu.VMEM, joined[1:])
            lowered, y = feed_down(section, document, r, raised[2], wd, vec, lowered)
            if section == 0:
                arrived[document] = passed_along(y[0], "pipe", 1)
    x, q, k, v, c, logs = attended
    h1, n1, f, slope, rs1 = raised
    section_out, h2, rs2 = lowered

    topped, fed_back, attended_back = (None, None, None)
    arrived = [None] * MB
    saved = (q, k, v, c, logs)
    for section in range(1, -1, -1):
        for document in range(MB - 1, -1, -1):
            source, row = (
                (cotangent, document * SEQ) if section == 1 else (arrived[document], 0)
            )
            last = section == 0 and document == 0
            if attended_back is not None:
                source = after(source, attended_back[0])
            topped, dr2 = top_back(section, document, source, row, h2, rs2, vec, topped)
            if last:
                away, own = weight_halves("weight_down", (f, topped[0]))
                dr2 = after(dr2, away)
                ring_down = ring(own, away, [D])
            fed_back, dr1 = feed_back(
                section, document, dr2, topped[0], slope, h1, rs1, wd, wu, vec, fed_back
            )
            if not last:
                attended_back = attend_back(
                    section, document, 0, D, fed_back[1], saved, wo, code, (dr1, wq), attended_back
                )
            if section == 1:
                arrived[document] = passed_along(attended_back[3], "pipe", -1)
                attended_back = attended_back[:3]
    e2, small_top = topped
    du, e1, small_feed, small_up = fed_back
    away, own = weight_halves("weight_up", (n1, du))
    ring_up = ring(own, away, [FF])
    token = ring_down.advance(away)
    dp, small_attend, input_grad = attend_back(
        section, document, 0, D, after(e1, token), saved, wo, code, (dr1, wq), attended_back
    )
    sums = [small_top, small_feed, small_attend, small_up]
    away, own = weight_halves("weight_rest", (x, dp), (c, e1), sums=sums)
    ring_rest = ring(own, away, [3 * D, D, LANES])
    token = away

    rings = [ring_down, ring_up, ring_rest]
    export = Steps(export_steps([section_out, input_grad]))
    token = ring_down.advance(token)
    token = ring_up.advance(token)
    turn = 0
    while any(each.left > 0 for each in rings):
        extra = [ring_rest] if turn < 2 else []
        for each in [ring_rest, ring_down] + extra + [ring_up]:
            if each.left > 0:
                token = each.advance(token)
        turn += 1
        if turn == 2:
            token = export.advance(token)
    for each in rings + [export]:
        while each.result is None:
            token = each.advance(token)
    (grad_down,), (grad_up,), (grad_qkv, grad_out, sums) = (each.result for each in rings)
    section_out, input_grad = export.result
    grad_qv, grad_bias_up, grad_res, grad_gain, grad_shift = finish(sums)
    results = (section_out, input_grad, grad_qkv, grad_out, grad_up, grad_down, grad_qv)
    results += (grad_bias_up, grad_res, grad_gain, grad_shift)
    return tuple(leaf if leaf is grad_bias_up else leaf[None] for leaf in results)


def solution(mesh):
    return jax.shard_map(
        local,
        mesh=mesh,
        in_specs=(
            P(("dp", "pair"), None),
            P(("dp", "pair"), None),
            P(("dp", "pair"), None),
            P(("dp", "pair")),
            P(("dp", "pair"), None),
            P("pipe", "pair", None),
            P("pipe", "pair", None),
            P("pipe", "pair", None),
            P("pipe", "pair", None),
            P("pipe", None, "pair"),
            P("pipe", "pair"),
            P("pipe", None, "pair"),
            P("pipe", None, "pair"),
            P("pipe", None, "pair"),
        ),
        out_specs=(
            P("pipe", ("dp", "pair"), None),
            P("pipe", ("dp", "pair"), None),
            P("pipe", "pair", None),
            P("pipe", "pair", None),
            P("pipe", "pair", None),
            P("pipe", "pair", None),
            P("pipe", None, "pair"),
            P("pipe", "pair"),
            P("pipe", None, "pair"),
            P("pipe", None, "pair"),
            P("pipe", None, "pair"),
        ),
        check_vma=False,
    )
```

```python
import jax
import jax.numpy as jnp
from jax import lax
from jax.experimental import pallas as pl
from jax.experimental.pallas import tpu as pltpu
from jax.sharding import PartitionSpec as P

D = 768
HEADS = 12
HEAD = 64
FF = 3072
TEXT = 176
SLOTS = 64
SEQ = 240
KEYS = 256
MB = 2
LANES = 128
STEP = 256


epsilon = 1e-06
masked_score = -1e30
gelu_one = 0.7978845608028654
gelu_two = 0.044715
low = jnp.bfloat16
wide = jnp.float32
swap = [(0, 1), (1, 0)]
combine_cost = 1 << 35
store_cost = 1 << 29


def passed_along(block, axis, distance):
    devices = range(lax.axis_size(axis))
    route = [(i - distance, i) for i in devices if i - distance in devices]
    return lax.ppermute(block, axis, route)


def after(value, earlier):
    return value if earlier is None else lax.optimization_barrier((value, earlier))[0]


def dot(left, right):
    return lax.dot_general(left, right, (((1,), (0,)), ((), ())), preferred_element_type=wide)


def dot_rows(left, right):
    return lax.dot_general(left, right, (((1,), (1,)), ((), ())), preferred_element_type=wide)


def dot_columns(left, right):
    return lax.dot_general(left, right, (((0,), (0,)), ((), ())), preferred_element_type=wide)


def column_sum(values):
    return jnp.sum(values, axis=0, keepdims=True)


def at_columns(start, size=STEP):
    return slice(start, start + size)


def score_bias(code_ref, document):
    code = code_ref[8 * document : 8 * document + 1, :]
    slot = lax.broadcasted_iota(jnp.int32, (SEQ, KEYS), 0) - TEXT
    keep = (code > -2) & ((slot < 0) | (code == -1) | (code == slot))
    return jnp.where(keep, 0.0, masked_score)


def head_masks(rows):
    first = lax.broadcasted_iota(jnp.int32, (rows, LANES), 1) < HEAD
    return (first, ~first)


def only(mask, values):
    return jnp.where(mask, values, jnp.zeros_like(values))


def normalize(values):
    center = values - jnp.mean(values, axis=1, keepdims=True)
    scale = lax.rsqrt(jnp.mean(center * center, axis=1, keepdims=True) + epsilon)
    return (center * scale, scale)


def normalize_back(grad, normal, scale):
    flat = jnp.mean(grad, axis=1, keepdims=True)
    along = jnp.mean(grad * normal, axis=1, keepdims=True)
    return scale * (grad - flat - normal * along)


def rows_of(document, size=SEQ):
    return slice(document * size, document * size + size)


def pack_kernel(count_ref, *refs):
    sources, (packed_ref, code_ref), held, sems = (refs[:7], refs[7:9], refs[9:16], refs[16])
    copies = [
        pltpu.make_async_copy(source, target, sems.at[k])
        for k, (source, target) in enumerate(zip(sources, held))
    ]
    for copy in copies:
        copy.start()
    for copy in copies:
        copy.wait()
    half = D // 2
    for place, ref in enumerate(held[:4]):
        packed_ref[2 * place : 2 * place + 2, :] = ref[...].astype(wide)
    for place in range(FF // D):
        packed_ref[8 + place : 9 + place, :] = held[4][
            0:1, half * place : half * place + half
        ].astype(wide)
    packed_ref[12:16, :] = jnp.zeros((4, half), wide)
    code = jnp.where(held[5][...] == 1, held[6][...], -2)
    slot = lax.broadcasted_iota(jnp.int32, (1, SLOTS), 1)
    for document in range(MB):
        rows = slice(8 * document, 8 * document + 8)
        code_ref[rows, :] = jnp.full((8, KEYS), -2, jnp.int32)
        code_ref[8 * document : 8 * document + 1, 0:TEXT] = code[document : document + 1, :]
        code_ref[8 * document : 8 * document + 1, TEXT:SEQ] = jnp.where(
            slot < count_ref[document], -1, -2
        )


def unpack_kernel(own_ref, other_ref, vec_ref, bu_ref):
    half = D // 2
    me = lax.axis_index("pair")
    for ref, place in ((own_ref, me), (other_ref, 1 - me)):
        vec_ref[:, pl.ds(pl.multiple_of(place * half, LANES), half)] = ref[0:8, :]
        for row in range(FF // D):
            start = place * (FF // 2) + row * half
            bu_ref[0:1, pl.ds(pl.multiple_of(start, LANES), half)] = ref[8 + row : 9 + row, :]


def join_kernel(count, place_of, *refs):
    half, full, sems = (refs[:count], refs[-count - 1 : -1], refs[-1])
    place = place_of(lax.axis_index("pair"))
    copies = []
    for k in range(count):
        rows = half[k].shape[0]
        if rows == full[k].shape[0]:
            target = full[k]
        else:
            target = full[k].at[pl.ds(pl.multiple_of(place * rows, rows), rows)]
        copies.append(pltpu.make_async_copy(half[k], target, sems.at[k]))
    for copy in copies:
        copy.start()
    for copy in copies:
        copy.wait()


def attend_kernel(
    document, source_row, source_ref, w_ref, code_ref, vec_ref,
    x_ref, q_ref, k_ref, v_ref, c_ref, l_ref,
):
    rows, keys = (rows_of(document), rows_of(document, KEYS))
    real = slice(document * KEYS, document * KEYS + SEQ)
    rest = slice(document * KEYS + SEQ, document * KEYS + KEYS)
    x = source_ref[source_row : source_row + SEQ, :]
    x_ref[rows, :] = x
    for start in range(0, D, STEP):
        cols = at_columns(start)
        queries = dot(x, w_ref[:, cols]) + vec_ref[0:1, cols]
        q_ref[rows, cols] = (queries * 0.125).astype(low)
        k_ref[real, cols] = dot(x, w_ref[:, at_columns(D + start)]).astype(low)
        values = dot(x, w_ref[:, at_columns(2 * D + start)]) + vec_ref[1:2, cols]
        v_ref[real, cols] = values.astype(low)
    k_ref[rest, :] = jnp.zeros((KEYS - SEQ, D), low)
    v_ref[rest, :] = jnp.zeros((KEYS - SEQ, D), low)
    bias = score_bias(code_ref, document)
    of_query = head_masks(SEQ)
    of_key = head_masks(KEYS)
    ones = jnp.ones((KEYS, LANES), low)
    for start in range(0, D, LANES):
        cols = at_columns(start, LANES)
        q, k, v = (q_ref[rows, cols], k_ref[keys, cols], v_ref[keys, cols])
        total = None
        tops = []
        for head in range(2):
            scores = dot_rows(only(of_query[head], q), k) + bias
            top = jnp.max(scores, axis=1, keepdims=True)
            weight = jnp.exp(scores - top).astype(low)
            both = jnp.concatenate([only(of_key[head], v), only(of_key[head], ones)], axis=1)
            part = dot(weight, both)
            total = part if total is None else total + part
            tops.append(top)
        sums = total[:, LANES:]
        c_ref[rows, cols] = (total[:, :LANES] / sums).astype(low)
        l_ref[rows, cols] = jnp.where(of_query[0], tops[0], tops[1]) + jnp.log(sums)


def feed_up_kernel(
    document, x_ref, c_ref, wo_ref, wu_ref, vec_ref, bu_ref,
    h1_ref, n1_ref, f_ref, s_ref, rs_ref, r_ref,
):
    rows = rows_of(document)
    c = c_ref[rows, :]
    for start in range(0, D, STEP):
        cols = at_columns(start)
        r_ref[:, cols] = (
            x_ref[rows, cols].astype(wide) + dot(c, wo_ref[:, cols]) + vec_ref[2:3, cols]
        )
    h1, scale = normalize(r_ref[...])
    h1_ref[rows, :] = h1
    rs_ref[rows, :] = jnp.broadcast_to(scale, (SEQ, LANES))
    n1 = h1 * vec_ref[4:5, :] + vec_ref[6:7, :]
    n1_low = n1.astype(low)
    n1_ref[rows, :] = n1_low
    r_ref[...] = n1 + vec_ref[3:4, :]
    for start in range(0, FF, STEP):
        cols = at_columns(start)
        u = dot(n1_low, wu_ref[:, cols]) + bu_ref[0:1, cols]
        square = u * u
        bend = jnp.tanh(u * (gelu_one + gelu_one * gelu_two * square))
        half = 0.5 + 0.5 * bend
        f_ref[rows, cols] = (u * half).astype(low)
        slope = half + u * (half * (1.0 - bend)) * (gelu_one + 3 * gelu_one * gelu_two * square)
        s_ref[rows, cols] = slope.astype(low)


def feed_down_kernel(
    document, r_ref, f_ref, wd_ref, vec_ref, section_ref, h2_ref, rs_ref, *rest
):
    sum_ref = rest[-1]
    rows = rows_of(document)
    f = f_ref[rows, :]
    for start in range(0, D, STEP):
        cols = at_columns(start)
        sum_ref[:, cols] = r_ref[:, cols] + dot(f, wd_ref[:, cols])
    h2, scale = normalize(sum_ref[...])
    h2_ref[rows, :] = h2
    rs_ref[rows, :] = jnp.broadcast_to(scale, (SEQ, LANES))
    y = (h2 * vec_ref[5:6, :] + vec_ref[7:8, :]).astype(low)
    section_ref[rows, :] = y
    for y_ref in rest[:-1]:
        y_ref[...] = y


def top_back_kernel(
    document, source_row, source_ref, h2_ref, rs_ref, vec_ref, e2_ref, sm_ref, dr2_ref
):
    rows = rows_of(document)
    g = source_ref[source_row : source_row + SEQ, :].astype(wide)
    h2 = h2_ref[rows, :]
    dr2 = normalize_back(g * vec_ref[5:6, :], h2, rs_ref[rows, 0:1])
    e2 = dr2.astype(low)
    dr2_ref[...] = dr2
    e2_ref[rows, :] = e2
    sm_ref[8 * document : 8 * document + 1, :] = column_sum(g * h2)
    sm_ref[8 * document + 1 : 8 * document + 2, :] = column_sum(g)
    sm_ref[8 * document + 2 : 8 * document + 3, :] = column_sum(e2.astype(wide))


def feed_back_kernel(
    document, dr2_ref, e2_ref, s_ref, h1_ref, rs_ref, wd_ref, wu_ref, vec_ref,
    du_ref, e1_ref, sm_ref, smu_ref, dr1_ref,
):
    rows = rows_of(document)
    e2 = e2_ref[rows, :]
    for start in range(0, FF, STEP):
        cols = at_columns(start)
        du = (dot_rows(e2, wd_ref[cols, :]) * s_ref[rows, cols].astype(wide)).astype(low)
        du_ref[rows, cols] = du
        smu_ref[8 * document : 8 * document + 1, cols] = column_sum(du.astype(wide))
    du = du_ref[rows, :]
    for start in range(0, D, STEP):
        cols = at_columns(start)
        dr1_ref[:, cols] = dr2_ref[:, cols] + dot_rows(du, wu_ref[cols, :])
    g = dr1_ref[...]
    h1 = h1_ref[rows, :]
    dr1 = normalize_back(g * vec_ref[4:5, :], h1, rs_ref[rows, 0:1])
    e1 = dr1.astype(low)
    dr1_ref[...] = dr1
    e1_ref[rows, :] = e1
    sm_ref[8 * document : 8 * document + 1, :] = column_sum(g * h1)
    sm_ref[8 * document + 1 : 8 * document + 2, :] = column_sum(g)
    sm_ref[8 * document + 2 : 8 * document + 3, :] = column_sum(e1.astype(wide))


def attend_back_kernel(
    document, first, last, e1_ref, q_ref, k_ref, v_ref, c_ref, l_ref, wo_ref, code_ref, *refs
):
    dc_ref = refs[-1]
    if last == D:
        dr1_ref, wq_ref, dp_ref, sm_ref, ig_ref = refs[:5]
    else:
        dp_ref, sm_ref = refs[:2]
    rows, keys = (rows_of(document), rows_of(document, KEYS))
    e1 = e1_ref[rows, :]
    for start in range(first, last, STEP):
        cols = at_columns(start)
        dc_ref[:, cols] = dot_rows(e1, wo_ref[cols, :]).astype(low)
    bias = score_bias(code_ref, document)
    of_query = head_masks(SEQ)
    of_key = head_masks(KEYS)
    for start in range(first, last, LANES):
        cols = at_columns(start, LANES)
        q, k, v, dc = (q_ref[rows, cols], k_ref[keys, cols], v_ref[keys, cols], dc_ref[:, cols])
        product = dc.astype(wide) * c_ref[rows, cols].astype(wide)
        dq, dk, dv = (0.0, 0.0, 0.0)
        for head in range(2):
            q_head, dc_head = (only(of_query[head], q), only(of_query[head], dc))
            logs = l_ref[rows, start + HEAD * head : start + HEAD * head + 1]
            p = jnp.exp(dot_rows(q_head, k) + bias - logs)
            inner = jnp.sum(only(of_query[head], product), axis=1, keepdims=True)
            ds = (p * (dot_rows(dc_head, v) - inner)).astype(low)
            dq = dq + dot(ds, only(of_key[head], k))
            dk = dk + dot_columns(ds, q_head)
            dv = dv + dot_columns(p.astype(low), dc_head)
        dq = dq.astype(low) * low(0.125)
        dv = dv[:SEQ].astype(low)
        dp_ref[rows, cols] = dq
        dp_ref[rows, at_columns(D + start, LANES)] = dk[:SEQ].astype(low)
        dp_ref[rows, at_columns(2 * D + start, LANES)] = dv
        sm_ref[8 * document : 8 * document + 1, cols] = column_sum(dq.astype(wide))
        sm_ref[8 * document + 1 : 8 * document + 2, cols] = column_sum(dv.astype(wide))
    if last < D:
        return
    dp = dp_ref[rows, :]
    for start in range(0, D, STEP):
        cols = at_columns(start)
        gi = (dr1_ref[:, cols] + dot_rows(dp, wq_ref[cols, :])).astype(low)
        ig_ref[rows, cols] = gi
        for gi_ref in refs[5:-1]:
            gi_ref[:, cols] = gi


def weight_kernel(pairs, rows, added, *refs):
    me = lax.axis_index("pair")
    sums = refs[2 * pairs : -2]
    away_ref, own_ref = refs[-2:]
    block = D // 2
    for part, owner in ((away_ref, 1 - me), (own_ref, me)):
        column = 0
        for k in range(pairs):
            left, right = refs[2 * k : 2 * k + 2]
            half = left.shape[1] // 2
            width = right.shape[1]
            for row in range(0, half, block):
                lefts = left[rows, pl.ds(pl.multiple_of(owner * half + row, LANES), block)]
                for start in range(0, width, STEP):
                    place = (slice(row, row + block), at_columns(column + start))
                    value = dot_columns(lefts, right[rows, at_columns(start)])
                    if added:
                        value = value + part[place].astype(wide)
                    part[place] = value.astype(low)
            column += width
        if sums:
            small_part(sums, owner, part, column)


def last_weight_kernel(pairs, *refs):
    first = lax.axis_index("pipe") == 0
    pl.when(first)(lambda: weight_kernel(pairs, rows_of(1), True, *refs))
    pl.when(jnp.logical_not(first))(
        lambda: weight_kernel(pairs, slice(0, MB * SEQ), False, *refs)
    )


def small_part(sums, owner, part, column):
    top_ref, feed_ref, attend_ref, up_ref = sums
    order = (
        (attend_ref, 0), (attend_ref, 1), (feed_ref, 2), (top_ref, 2),
        (feed_ref, 0), (top_ref, 0), (feed_ref, 1), (top_ref, 1),
    )
    places = [(ref, row, D // 2) for ref, row in order] + [(up_ref, 0, FF // 2)]
    lines = []
    for ref, row, half in places:
        for start in range(0, half, LANES):
            cols = pl.ds(pl.multiple_of(owner * half + start, LANES), LANES)
            lines.append(ref[row : row + 1, cols] + ref[row + 8 : row + 9, cols])
    lines.append(jnp.zeros((48 - len(lines), LANES), wide))
    tile = at_columns(column, LANES)
    part[0:48, tile] = jnp.concatenate(lines, axis=0).astype(low)
    part[48:, tile] = jnp.zeros((part.shape[0] - 48, LANES), low)


def ring_row(stride, size, step, rows):
    index = lax.rem(ring_at(stride, size) - step + size, size)
    return pl.multiple_of(index * rows, rows)


def combine_kernel(stride, size, step, *refs):
    terms, arrived, out_ref = (refs[:2], refs[2:-1], refs[-1])
    first = ring_row(stride, size, step, out_ref.shape[0])

    def piece(k, carry):
        here = pl.ds(pl.multiple_of(k * 16, 16), 16)
        there = pl.ds(pl.multiple_of(first + k * 16, 16), 16)
        value = terms[0][there, :].astype(wide) + terms[1][there, :].astype(wide)
        for ref in arrived:
            value = value + ref[here, :].astype(wide)
        out_ref[here, :] = value.astype(low)
        return carry

    lax.fori_loop(0, out_ref.shape[0] // 16, piece, 0)


def store_kernel(stride, size, step, cuts, block_ref, *refs):
    count = len(cuts)
    totals, scratch, sems = (refs[:count], refs[count:-1], refs[-1])
    rows = block_ref.shape[0]
    first = ring_row(stride, size, step - 1, rows)

    def piece(k, carry):
        here = pl.ds(pl.multiple_of(k * 16, 16), 16)
        column = 0
        for part, cut in enumerate(cuts):
            scratch[part][here, :] = block_ref[here, column : column + cut].astype(wide)
            column += cut
        return carry

    lax.fori_loop(0, rows // 16, piece, 0)
    copies = [
        pltpu.make_async_copy(scratch[k], totals[k].at[pl.ds(first, rows)], sems.at[k])
        for k in range(count)
    ]
    for copy in copies:
        copy.start()
    for copy in copies:
        copy.wait()


def finish_kernel(sum_ref, qv_ref, up_ref, res_ref, gain_ref, shift_ref, held_ref, sem):
    copy = pltpu.make_async_copy(sum_ref.at[pl.ds(0, 48)], held_ref, sem.at[0])
    copy.start()
    copy.wait()
    line = 0
    for ref in (qv_ref, res_ref, gain_ref, shift_ref, up_ref):
        for row in range(ref.shape[0]):
            for start in range(0, ref.shape[1], LANES):
                ref[row : row + 1, at_columns(start, LANES)] = held_ref[line : line + 1, :]
                line += 1


def near(shape, dtype):
    return pltpu.VMEM(shape, dtype)


def far(shape, dtype):
    return pltpu.HBM(shape, dtype)


def run(
    kernel, name, operands, outputs, scratch=(), flops=0, section=None, keep=None, spaces=None
):
    keep = [] if keep is None else list(keep)
    count = len(operands)
    spaces = [pltpu.VMEM] * count if spaces is None else list(spaces)
    placed = [getattr(leaf, "memory_space", pltpu.VMEM) for leaf in outputs]
    spaces += placed[: len(keep)]
    operands = [
        leaf
        if space in (None, pltpu.SMEM)
        else pltpu.with_memory_space_constraint(leaf, space)
        for leaf, space in zip(list(operands) + keep, spaces)
    ]

    def body(*refs):
        used = refs[:count] + refs[count + len(keep) :]
        if section is None:
            kernel(*used)
        else:
            pl.when(lax.axis_index("pipe") == section)(lambda: kernel(*used))

    return pl.pallas_call(
        body,
        out_shape=tuple(outputs),
        in_specs=[pl.BlockSpec(memory_space=space or pltpu.VMEM) for space in spaces],
        out_specs=tuple(pl.BlockSpec(memory_space=space) for space in placed),
        scratch_shapes=list(scratch),
        input_output_aliases={count + k: k for k in range(len(keep))},
        name=name,
        cost_estimate=pl.CostEstimate(flops=flops, bytes_accessed=0, transcendentals=0),
        compiler_params=pltpu.CompilerParams(vmem_limit_bytes=4 << 20),
    )(*operands)


def join_halves(name, halves, place_of, space, keep=None, whole=()):
    outputs = [near((2 * leaf.shape[0], leaf.shape[1]), leaf.dtype) for leaf in halves]
    outputs += [near(leaf.shape, leaf.dtype) for leaf in whole]
    halves = list(halves) + list(whole)
    return run(
        lambda *refs: join_kernel(len(halves), place_of, *refs),
        name,
        halves,
        outputs,
        [pltpu.SemaphoreType.DMA((len(halves),))],
        keep=keep,
        spaces=[space] * len(halves),
    )


def attend(section, document, source, source_row, w_qkv, code, vec, keep):
    rows = near((MB * SEQ, D), low)
    keys = near((MB * KEYS, D), low)
    return run(
        lambda *refs: attend_kernel(document, source_row, *refs),
        "attend",
        [source, w_qkv, code, vec],
        [rows, rows, keys, keys, rows, near((MB * SEQ, D), wide)],
        flops=2 * SEQ * D * (3 * D + 4 * KEYS),
        section=section,
        keep=keep,
    )


def feed_up(section, document, x, c, w_out, w_up, vec, bu, keep):
    rows = near((MB * SEQ, D), low)
    inner = near((MB * SEQ, FF), low)
    outs = run(
        lambda *refs: feed_up_kernel(document, *refs),
        "feed_up",
        [x, c, w_out, w_up, vec, bu],
        [near((MB * SEQ, D), wide), rows, inner, inner, near((MB * SEQ, LANES), wide)]
        + [near((SEQ, D), wide)],
        flops=2 * SEQ * D * (D + FF),
        section=section,
        keep=keep,
    )
    return (outs[:-1], outs[-1])


def feed_down(section, document, r, f, w_down, vec, keep):
    outs = run(
        lambda *refs: feed_down_kernel(document, *refs),
        "feed_down",
        [r, f, w_down, vec],
        [near((MB * SEQ, D), low), near((MB * SEQ, D), wide), near((MB * SEQ, LANES), wide)]
        + [near((SEQ, D), low)] * (1 - section),
        [pltpu.VMEM((SEQ, D), wide)],
        flops=2 * SEQ * D * FF,
        section=section,
        keep=keep,
    )
    return (outs[:3], outs[3:])


def top_back(section, document, source, source_row, h2, rs, vec, keep):
    outs = run(
        lambda *refs: top_back_kernel(document, source_row, *refs),
        "top_back",
        [source, h2, rs, vec],
        [near((MB * SEQ, D), low), near((MB * 8, D), wide), near((SEQ, D), wide)],
        flops=2 * SEQ * D * D,
        section=section,
        keep=keep,
    )
    return (outs[:-1], outs[-1])


def feed_back(section, document, dr2, e2, slope, h1, rs, w_down, w_up, vec, keep):
    outs = run(
        lambda *refs: feed_back_kernel(document, *refs),
        "feed_back",
        [dr2, e2, slope, h1, rs, w_down, w_up, vec],
        [near((MB * SEQ, FF), low), near((MB * SEQ, D), low), near((MB * 8, D), wide)]
        + [near((MB * 8, FF), wide), near((SEQ, D), wide)],
        flops=2 * SEQ * D * 2 * FF,
        section=section,
        keep=keep,
    )
    return (outs[:-1], outs[-1])


def attend_back(section, document, first, last, e1, saved, w_out, code, extra, keep):
    outputs = [near((MB * SEQ, 3 * D), low), near((MB * 8, D), wide)]
    if last == D:
        outputs += [near((MB * SEQ, D), low)] + [near((SEQ, D), low)] * section
    share = 6 * D if last == D else 0
    return run(
        lambda *refs: attend_back_kernel(document, first, last, *refs),
        "attend_back",
        [e1, *saved, w_out, code, *extra],
        outputs,
        [pltpu.VMEM((SEQ, D), low)],
        flops=2 * SEQ * ((last - first) * (D + 10 * KEYS) + share * D),
        section=section,
        keep=keep,
    )


def weight_halves(name, *pairs, sums=None, keep=None):
    half = pairs[0][0].shape[1] // 2
    width = sum(right.shape[1] for left, right in pairs) + (LANES if sums is not None else 0)
    if keep is None:
        kernel = lambda *refs: weight_kernel(len(pairs), rows_of(0), False, *refs)
    else:
        kernel = lambda *refs: last_weight_kernel(len(pairs), *refs)
    return run(
        kernel,
        name,
        [leaf for pair in pairs for leaf in pair] + list(sums or ()),
        [near((half, width), low), near((half, width), low)],
        flops=2 * MB * SEQ * 2 * half * width,
        section=0 if keep is None else None,
        keep=keep,
    )


def ring_levels(total):
    sizes = []
    while total > 1:
        size = max([k for k in range(2, 9) if total % k == 0], default=total)
        sizes.append(size)
        total //= size
    return sizes


def ring_place(total, stride, size, device):
    own = device // stride % size
    if total == size and size % 2 == 0:
        return jnp.where(own % 2 == 0, own // 2, size - (own + 1) // 2)
    return own


def ring_at(stride, size):
    at = ring_place(lax.axis_size("dp"), stride, size, lax.axis_index("dp"))
    return jnp.where(lax.axis_index("pair") == 0, at, lax.rem(size - at, size))


def ring_route(total, stride, size):
    order = list(range(size))
    if total == size and size % 2 == 0:
        order = list(range(0, size, 2)) + list(range(size - 1, 0, -2))
    route = []
    for device in range(total):
        own = device // stride % size
        target = order[(order.index(own) + 1) % size]
        target = device + (target - own) * stride
        route.append((device * 2, target * 2))
        route.append((target * 2 + 1, device * 2 + 1))
    return route


def ring_combine(stride, size, step, terms, arrived):
    rows = terms[0].shape[0] // size
    width = terms[0].shape[1]
    if rows % 16 == 0:
        return run(
            lambda *refs: combine_kernel(stride, size, step, *refs),
            "combine",
            list(terms) + arrived,
            [near((rows, width), low)],
            flops=combine_cost,
        )[0]
    index = (ring_at(stride, size) - step + size) % size
    value = 0.0
    for leaf in terms:
        piece = lax.dynamic_slice_in_dim(leaf, index * rows, rows, 0)
        value = value + piece.astype(wide)
    for leaf in arrived:
        value = value + leaf.astype(wide)
    return value.astype(low)


def ring_store(stride, size, step, block, cuts, totals, dtype):
    rows = block.shape[0]
    if rows % 16 == 0 and dtype == wide:
        return run(
            lambda *refs: store_kernel(stride, size, step, cuts, *refs),
            "store",
            [block],
            [far((size * rows, cut), wide) for cut in cuts],
            [pltpu.VMEM((rows, cut), wide) for cut in cuts]
            + [pltpu.SemaphoreType.DMA((len(cuts),))],
            flops=store_cost,
            keep=totals,
        )
    if totals is None:
        totals = [jnp.zeros((size * rows, cut), dtype) for cut in cuts]
    index = (ring_at(stride, size) + 1 - step + size) % size
    column = 0
    stored = []
    for leaf, cut in zip(totals, cuts):
        piece = block[:, column : column + cut].astype(dtype)
        stored.append(lax.dynamic_update_slice_in_dim(leaf, piece, index * rows, 0))
        column += cut
    return stored


def ring_steps(terms, widths):
    total = lax.axis_size("dp")
    levels = []
    stride = 1
    for size in ring_levels(total):
        levels.append((stride, size))
        stride *= size
    token = yield None
    terms = [terms[0], after(terms[1], token)]
    running = None
    for stride, size in levels:
        route = ring_route(total, stride, size)
        if running is not None:
            terms = [running, jnp.zeros_like(running)]
        for step in range(size):
            arrived = []
            if step > 0:
                arrived = [after(lax.ppermute(running, ("dp", "pair"), route), token)]
            running = ring_combine(stride, size, step, terms, arrived)
            token = yield running
    for depth, (stride, size) in enumerate(levels[::-1]):
        route = ring_route(total, stride, size)
        last = depth == len(levels) - 1
        dtype, cuts = (wide, widths) if last else (low, [sum(widths)])
        totals = None
        for step in range(size):
            if step > 0:
                running = after(lax.ppermute(running, ("dp", "pair"), route), token)
            totals = ring_store(stride, size, step, running, cuts, totals, dtype)
            if step > 0:
                token = yield tuple(totals)
        running = totals[0]
    return totals


class Steps:
    def __init__(self, steps, left=0):
        self.steps, self.left, self.result = (steps, left, None)
        next(steps)

    def advance(self, token):
        self.left -= 1
        try:
            return self.steps.send(token)
        except StopIteration as done:
            self.result = done.value
            return token


def ring(own, away, widths):
    left = sum(2 * size - 1 for size in ring_levels(lax.axis_size("dp")))
    return Steps(ring_steps([own, from_pair(away)], widths), left)


def finish(sums):
    pairs = jax.ShapeDtypeStruct((2, D // 2), wide)
    outputs = [pairs, jax.ShapeDtypeStruct((1, FF // 2), wide), pairs, pairs, pairs]
    scratch = [pltpu.VMEM((48, LANES), wide), pltpu.SemaphoreType.DMA((1,))]
    return run(finish_kernel, "finish", [sums], outputs, scratch, spaces=[pltpu.HBM])


def export_kernel(*refs):
    count = len(refs) // 2
    copies = [
        pltpu.make_async_copy(refs[k], refs[count + k], refs[-1].at[k]) for k in range(count)
    ]
    for copy in copies:
        copy.start()
    for copy in copies:
        copy.wait()


def export_steps(leaves):
    token = yield None
    stored = run(
        export_kernel,
        "export",
        [after(leaves[0], token)] + list(leaves[1:]),
        [far(leaf.shape, leaf.dtype) for leaf in leaves],
        [pltpu.SemaphoreType.DMA((len(leaves),))],
    )
    token = yield tuple(stored)
    return stored


def from_pair(leaf):
    return lax.ppermute(leaf, "pair", swap)


def local(
    inputs,
    cotangent,
    text_mask,
    seg_count,
    align,
    w_qkv,
    w_out,
    w_up,
    w_down,
    bias_qv,
    bias_up,
    bias_res,
    norm_gain,
    norm_shift,
):
    own = [w_qkv[0], w_out[0], w_up[0], w_down[0]]
    other_qkv = from_pair(own[0])
    params = [bias_qv[0], bias_res[0], norm_gain[0], norm_shift[0], bias_up, text_mask, align]
    packed, code = run(
        pack_kernel,
        "pack",
        [seg_count] + params,
        [near((16, D // 2), wide), near((MB * 8, KEYS), jnp.int32)],
        [pltpu.VMEM(leaf.shape, leaf.dtype) for leaf in params]
        + [pltpu.SemaphoreType.DMA((len(params),))],
        spaces=[pltpu.SMEM] + [pltpu.HBM] * len(params),
    )
    packed_other = from_pair(packed)
    mine = lambda me: me
    others = lambda me: 1 - me
    other_out = from_pair(own[1])
    held = [after(own[0], packed), own[1]]
    joined = join_halves("join_own", held, mine, pltpu.HBM, whole=(inputs,))
    inputs = joined[2]
    vec, bu = run(
        unpack_kernel,
        "unpack",
        [packed, after(packed_other, joined[0])],
        [near((8, D), wide), near((8, FF), wide)],
    )
    other_qkv, other_out, vec = lax.optimization_barrier((other_qkv, other_out, vec))
    other_up = from_pair(after(own[2], other_qkv))
    wq, wo = join_halves("join_qkv", [other_qkv, other_out], others, pltpu.VMEM, joined[:2])

    attended, raised, lowered = (None, None, None)
    topped, fed_back, attended_back = (None, None, None)
    onward, backward = ([None] * MB, [None] * MB)
    for section, document in ((0, 0), (0, 1), (1, 0), (1, 1)):
        source, row = (inputs, document * SEQ) if section == 0 else (onward[document], 0)
        if attended_back is not None:
            source = after(source, attended_back[0])
        attended = attend(section, document, source, row, wq, code, vec, attended)
        x, q, k, v, c, logs = attended
        if raised is None:
            joined = join_halves("join_own", [after(own[2], x)], mine, pltpu.HBM)
            other_up = after(other_up, joined[0])
            other_down = from_pair(after(own[3], other_up))
            (wu,) = join_halves("join_up", [other_up], others, pltpu.VMEM, joined)
        raised, r = feed_up(section, document, x, c, wo, wu, vec, bu, raised)
        h1, n1, f, slope, rs1 = raised
        if lowered is None:
            joined = join_halves(
                "join_own", [after(own[3], r)], mine, pltpu.HBM, whole=(cotangent,)
            )
            cotangent = joined[1]
            other_down = after(other_down, joined[0])
            (wd,) = join_halves("join_down", [other_down], others, pltpu.VMEM, joined[:1])
        lowered, y = feed_down(section, document, r, f, wd, vec, lowered)
        section_out, h2, rs2 = lowered
        if section == 0:
            onward[document] = passed_along(y[0], "pipe", 1)
            continue
        topped, dr2 = top_back(section, document, cotangent, document * SEQ, h2, rs2, vec, topped)
        fed_back, dr1 = feed_back(
            section, document, dr2, topped[0], slope, h1, rs1, wd, wu, vec, fed_back
        )
        attended_back = attend_back(
            section, document, 0, D, fed_back[1], (q, k, v, c, logs), wo, code, (dr1, wq),
            attended_back,
        )
        backward[document] = passed_along(attended_back[3], "pipe", -1)
        attended_back = attended_back[:3]
    saved = (q, k, v, c, logs)

    source = after(backward[0], attended_back[0])
    topped, dr2 = top_back(0, 0, source, 0, h2, rs2, vec, topped)
    fed_back, dr1 = feed_back(0, 0, dr2, topped[0], slope, h1, rs1, wd, wu, vec, fed_back)
    attended_back = attend_back(
        0, 0, 0, D, fed_back[1], saved, wo, code, (dr1, wq), attended_back
    )
    share_down = weight_halves("weight_down", (f, topped[0]))
    share_up = weight_halves("weight_up", (n1, fed_back[0]))
    empty = (topped[1], fed_back[2], attended_back[1], fed_back[3])
    share_rest = weight_halves("weight_rest", (x, attended_back[0]), (c, fed_back[1]), sums=empty)

    source = after(backward[1], (share_down[0], share_up[0], share_rest[0]))
    topped, dr2 = top_back(0, 1, source, 0, h2, rs2, vec, topped)
    away, own = weight_halves("weight_down", (f, topped[0]), keep=share_down)
    dr2 = after(dr2, away)
    ring_down = ring(own, away, [D])
    fed_back, dr1 = feed_back(0, 1, dr2, topped[0], slope, h1, rs1, wd, wu, vec, fed_back)
    e2, small_top = topped
    du, e1, small_feed, small_up = fed_back
    away, own = weight_halves("weight_up", (n1, du), keep=share_up)
    ring_up = ring(own, away, [FF])
    token = ring_down.advance(away)
    cut = 2 * STEP
    begun = attend_back(
        0, 1, 0, cut, after(e1, token), saved, wo, code, (), attended_back[:2]
    )
    token = ring_down.advance(begun[0])
    token = ring_up.advance(token)
    dp, small_attend, input_grad = attend_back(
        0, 1, cut, D, after(e1, token), saved, wo, code, (dr1, wq),
        [*begun, attended_back[2]],
    )
    token = ring_down.advance(dp)
    token = ring_up.advance(token)
    dp = after(dp, token)
    sums = [small_top, small_feed, small_attend, small_up]
    away, own = weight_halves("weight_rest", (x, dp), (c, e1), sums=sums, keep=share_rest)
    ring_rest = ring(own, away, [3 * D, D, LANES])
    token = away

    rings = [ring_down, ring_up, ring_rest]
    export = Steps(export_steps([section_out, input_grad]))
    token = ring_down.advance(token)
    token = ring_up.advance(token)
    turn = 0
    while any(each.left > 0 for each in rings):
        extra = [ring_rest] if turn < 2 else []
        for each in [ring_rest, ring_down] + extra + [ring_up]:
            if each.left > 0:
                token = each.advance(token)
        turn += 1
        if turn == 2:
            token = export.advance(token)
    for each in rings + [export]:
        while each.result is None:
            token = each.advance(token)
    (grad_down,), (grad_up,), (grad_qkv, grad_out, sums) = (each.result for each in rings)
    section_out, input_grad = export.result
    grad_qv, grad_bias_up, grad_res, grad_gain, grad_shift = finish(sums)
    results = (section_out, input_grad, grad_qkv, grad_out, grad_up, grad_down, grad_qv)
    results += (grad_bias_up, grad_res, grad_gain, grad_shift)
    return tuple(leaf if leaf is grad_bias_up else leaf[None] for leaf in results)


def solution(mesh):
    return jax.shard_map(
        local,
        mesh=mesh,
        in_specs=(
            P(("dp", "pair"), None),
            P(("dp", "pair"), None),
            P(("dp", "pair"), None),
            P(("dp", "pair")),
            P(("dp", "pair"), None),
            P("pipe", "pair", None),
            P("pipe", "pair", None),
            P("pipe", "pair", None),
            P("pipe", "pair", None),
            P("pipe", None, "pair"),
            P("pipe", "pair"),
            P("pipe", None, "pair"),
            P("pipe", None, "pair"),
            P("pipe", None, "pair"),
        ),
        out_specs=(
            P("pipe", ("dp", "pair"), None),
            P("pipe", ("dp", "pair"), None),
            P("pipe", "pair", None),
            P("pipe", "pair", None),
            P("pipe", "pair", None),
            P("pipe", "pair", None),
            P("pipe", None, "pair"),
            P("pipe", "pair"),
            P("pipe", None, "pair"),
            P("pipe", None, "pair"),
            P("pipe", None, "pair"),
        ),
        check_vma=False,
    )
```

```python
import jax
import jax.numpy as jnp
from jax import lax
from jax.experimental import pallas as pl
from jax.experimental.pallas import tpu as pltpu
from jax.sharding import PartitionSpec as P

D = 768
HEADS = 12
HEAD = 64
FF = 3072
TEXT = 176
SLOTS = 64
SEQ = 240
KEYS = 256
MB = 2
LANES = 128
STEP = 256


epsilon = 1e-06
masked_score = -1e30
gelu_one = 0.7978845608028654
gelu_two = 0.044715
low = jnp.bfloat16
wide = jnp.float32
swap = [(0, 1), (1, 0)]
combine_cost = 1 << 35
later_cost = 1 << 35
store_cost = 1 << 29


def passed_along(block, axis, distance):
    devices = range(lax.axis_size(axis))
    route = [(i - distance, i) for i in devices if i - distance in devices]
    return lax.ppermute(block, axis, route)


def after(value, earlier):
    return value if earlier is None else lax.optimization_barrier((value, earlier))[0]


def dot(left, right):
    return lax.dot_general(left, right, (((1,), (0,)), ((), ())), preferred_element_type=wide)


def dot_rows(left, right):
    return lax.dot_general(left, right, (((1,), (1,)), ((), ())), preferred_element_type=wide)


def dot_columns(left, right):
    return lax.dot_general(left, right, (((0,), (0,)), ((), ())), preferred_element_type=wide)


def column_sum(values):
    return jnp.sum(values, axis=0, keepdims=True)


def at_columns(start, size=STEP):
    return slice(start, start + size)


def score_bias(code_ref, document):
    code = code_ref[8 * document : 8 * document + 1, :]
    slot = lax.broadcasted_iota(jnp.int32, (SEQ, KEYS), 0) - TEXT
    keep = (code > -2) & ((slot < 0) | (code == -1) | (code == slot))
    return jnp.where(keep, 0.0, masked_score)


def in_first_head(rows):
    return lax.broadcasted_iota(jnp.int32, (rows, LANES), 1) < HEAD


def head_ones():
    first = lax.broadcasted_iota(jnp.int32, (1, LANES), 1) < HEAD
    first = jnp.where(first, 1.0, 0.0)
    return (first, 1.0 - first)


def of_head(values, row):
    return values * row.astype(values.dtype)


def normalize(values):
    center = values - jnp.mean(values, axis=1, keepdims=True)
    scale = lax.rsqrt(jnp.mean(center * center, axis=1, keepdims=True) + epsilon)
    return (center * scale, scale)


def normalize_back(grad, normal, scale):
    flat = jnp.mean(grad, axis=1, keepdims=True)
    along = jnp.mean(grad * normal, axis=1, keepdims=True)
    return scale * (grad - flat - normal * along)


def rows_of(document, size=SEQ):
    return slice(document * size, document * size + size)


def pack_kernel(count_ref, *refs):
    sources, (packed_ref, code_ref), held, sems = (refs[:7], refs[7:9], refs[9:16], refs[16])
    copies = [
        pltpu.make_async_copy(source, target, sems.at[k])
        for k, (source, target) in enumerate(zip(sources, held))
    ]
    for copy in copies:
        copy.start()
    for copy in copies:
        copy.wait()
    half = D // 2
    for place, ref in enumerate(held[:4]):
        packed_ref[2 * place : 2 * place + 2, :] = ref[...].astype(wide)
    for place in range(FF // D):
        packed_ref[8 + place : 9 + place, :] = held[4][
            0:1, half * place : half * place + half
        ].astype(wide)
    packed_ref[12:16, :] = jnp.zeros((4, half), wide)
    code = jnp.where(held[5][...] == 1, held[6][...], -2)
    slot = lax.broadcasted_iota(jnp.int32, (1, SLOTS), 1)
    for document in range(MB):
        rows = slice(8 * document, 8 * document + 8)
        code_ref[rows, :] = jnp.full((8, KEYS), -2, jnp.int32)
        code_ref[8 * document : 8 * document + 1, 0:TEXT] = code[document : document + 1, :]
        code_ref[8 * document : 8 * document + 1, TEXT:SEQ] = jnp.where(
            slot < count_ref[document], -1, -2
        )


def unpack_kernel(own_ref, other_ref, vec_ref, bu_ref):
    half = D // 2
    me = lax.axis_index("pair")
    for ref, place in ((own_ref, me), (other_ref, 1 - me)):
        vec_ref[:, pl.ds(pl.multiple_of(place * half, LANES), half)] = ref[0:8, :]
        for row in range(FF // D):
            start = place * (FF // 2) + row * half
            bu_ref[0:1, pl.ds(pl.multiple_of(start, LANES), half)] = ref[8 + row : 9 + row, :]


def join_kernel(count, place_of, *refs):
    half, full, sems = (refs[:count], refs[-count - 1 : -1], refs[-1])
    place = place_of(lax.axis_index("pair"))
    copies = []
    for k in range(count):
        rows = half[k].shape[0]
        if rows == full[k].shape[0]:
            target = full[k]
        else:
            target = full[k].at[pl.ds(pl.multiple_of(place * rows, rows), rows)]
        copies.append(pltpu.make_async_copy(half[k], target, sems.at[k]))
    for copy in copies:
        copy.start()
    for copy in copies:
        copy.wait()


def join_both_kernel(own_ref, other_ref, full_ref, sems):
    me = lax.axis_index("pair")
    rows = own_ref.shape[0]
    copies = []
    for part, (source, place) in enumerate(((own_ref, me), (other_ref, 1 - me))):
        target = full_ref.at[pl.ds(pl.multiple_of(place * rows, rows), rows)]
        copies.append(pltpu.make_async_copy(source, target, sems.at[part]))
    for copy in copies:
        copy.start()
    for copy in copies:
        copy.wait()


def attend_kernel(
    document, source_row, source_ref, w_ref, code_ref, vec_ref,
    x_ref, q_ref, k_ref, v_ref, c_ref, l_ref,
):
    rows, keys = (rows_of(document), rows_of(document, KEYS))
    real = slice(document * KEYS, document * KEYS + SEQ)
    rest = slice(document * KEYS + SEQ, document * KEYS + KEYS)
    x = source_ref[source_row : source_row + SEQ, :]
    x_ref[rows, :] = x
    for start in range(0, D, STEP):
        cols = at_columns(start)
        queries = dot(x, w_ref[:, cols]) + vec_ref[0:1, cols]
        q_ref[rows, cols] = (queries * 0.125).astype(low)
        k_ref[real, cols] = dot(x, w_ref[:, at_columns(D + start)]).astype(low)
        values = dot(x, w_ref[:, at_columns(2 * D + start)]) + vec_ref[1:2, cols]
        v_ref[real, cols] = values.astype(low)
    k_ref[rest, :] = jnp.zeros((KEYS - SEQ, D), low)
    v_ref[rest, :] = jnp.zeros((KEYS - SEQ, D), low)
    bias = score_bias(code_ref, document)
    bias = jnp.concatenate([bias, bias], axis=0)
    first = in_first_head(SEQ)
    lane = lax.broadcasted_iota(jnp.int32, (SEQ, LANES), 1) % HEAD
    kept = jnp.zeros((SEQ, LANES), wide)
    ones = jnp.ones((KEYS, LANES), low)
    for start in range(0, D, LANES):
        cols = at_columns(start, LANES)
        q, k, v = (q_ref[rows, cols], k_ref[keys, cols], v_ref[keys, cols])
        queries = jnp.concatenate([of_head(q, row) for row in head_ones()], axis=0)
        scores = dot_rows(queries, k) + bias
        top = jnp.max(scores, axis=1, keepdims=True)
        weight = jnp.exp(scores - top).astype(low)
        both = dot(weight, jnp.concatenate([v, ones], axis=1))
        total = jnp.where(first, both[:SEQ, :LANES], both[SEQ:, :LANES])
        sums = jnp.where(first, both[:SEQ, LANES:], both[SEQ:, LANES:])
        c_ref[rows, cols] = (total / sums).astype(low)
        logs = jnp.where(first, top[:SEQ], top[SEQ:]) + jnp.log(sums)
        kept = jnp.where(lane == start // LANES, logs, kept)
    l_ref[rows, :] = kept


def feed_up_kernel(
    document, x_ref, c_ref, wo_ref, wu_ref, vec_ref, bu_ref,
    h1_ref, n1_ref, f_ref, s_ref, rs_ref, r_ref,
):
    rows = rows_of(document)
    c = c_ref[rows, :]
    for start in range(0, D, STEP):
        cols = at_columns(start)
        r_ref[:, cols] = (
            x_ref[rows, cols].astype(wide) + dot(c, wo_ref[:, cols]) + vec_ref[2:3, cols]
        )
    h1, scale = normalize(r_ref[...])
    h1_ref[rows, :] = h1.astype(low)
    rs_ref[rows, :] = jnp.broadcast_to(scale, (SEQ, LANES))
    n1 = h1 * vec_ref[4:5, :] + vec_ref[6:7, :]
    n1_low = n1.astype(low)
    n1_ref[rows, :] = n1_low
    r_ref[...] = n1 + vec_ref[3:4, :]
    for start in range(0, FF, STEP):
        cols = at_columns(start)
        u = dot(n1_low, wu_ref[:, cols]) + bu_ref[0:1, cols]
        square = u * u
        bend = jnp.tanh(u * (gelu_one + gelu_one * gelu_two * square))
        half = 0.5 + 0.5 * bend
        f_ref[rows, cols] = (u * half).astype(low)
        slope = half + u * (half * (1.0 - bend)) * (gelu_one + 3 * gelu_one * gelu_two * square)
        s_ref[rows, cols] = slope.astype(low)


def feed_down_kernel(
    document, r_ref, f_ref, wd_ref, vec_ref, section_ref, h2_ref, rs_ref, *rest
):
    sum_ref = rest[-1]
    rows = rows_of(document)
    f = f_ref[rows, :]
    for start in range(0, D, STEP):
        cols = at_columns(start)
        sum_ref[:, cols] = r_ref[:, cols] + dot(f, wd_ref[:, cols])
    h2, scale = normalize(sum_ref[...])
    h2_ref[rows, :] = h2.astype(low)
    rs_ref[rows, :] = jnp.broadcast_to(scale, (SEQ, LANES))
    y = (h2 * vec_ref[5:6, :] + vec_ref[7:8, :]).astype(low)
    section_ref[rows, :] = y
    for y_ref in rest[:-1]:
        y_ref[...] = y


def top_back_kernel(
    document, source_row, source_ref, h2_ref, rs_ref, vec_ref, e2_ref, sm_ref, dr2_ref
):
    rows = rows_of(document)
    g = source_ref[source_row : source_row + SEQ, :].astype(wide)
    h2 = h2_ref[rows, :].astype(wide)
    dr2 = normalize_back(g * vec_ref[5:6, :], h2, rs_ref[rows, 0:1])
    e2 = dr2.astype(low)
    dr2_ref[...] = dr2
    e2_ref[rows, :] = e2
    sm_ref[8 * document : 8 * document + 1, :] = column_sum(g * h2)
    sm_ref[8 * document + 1 : 8 * document + 2, :] = column_sum(g)
    sm_ref[8 * document + 2 : 8 * document + 3, :] = column_sum(e2.astype(wide))


def feed_back_kernel(
    document, dr2_ref, e2_ref, s_ref, h1_ref, rs_ref, wd_ref, wu_ref, vec_ref,
    du_ref, e1_ref, sm_ref, smu_ref, dr1_ref,
):
    rows = rows_of(document)
    e2 = e2_ref[rows, :]
    for start in range(0, FF, STEP):
        cols = at_columns(start)
        du = (dot_rows(e2, wd_ref[cols, :]) * s_ref[rows, cols].astype(wide)).astype(low)
        du_ref[rows, cols] = du
        smu_ref[8 * document : 8 * document + 1, cols] = column_sum(du.astype(wide))
    du = du_ref[rows, :]
    for start in range(0, D, STEP):
        cols = at_columns(start)
        dr1_ref[:, cols] = dr2_ref[:, cols] + dot_rows(du, wu_ref[cols, :])
    g = dr1_ref[...]
    h1 = h1_ref[rows, :].astype(wide)
    dr1 = normalize_back(g * vec_ref[4:5, :], h1, rs_ref[rows, 0:1])
    e1 = dr1.astype(low)
    dr1_ref[...] = dr1
    e1_ref[rows, :] = e1
    sm_ref[8 * document : 8 * document + 1, :] = column_sum(g * h1)
    sm_ref[8 * document + 1 : 8 * document + 2, :] = column_sum(g)
    sm_ref[8 * document + 2 : 8 * document + 3, :] = column_sum(e1.astype(wide))


def attend_back_kernel(
    document, first, last, e1_ref, q_ref, k_ref, v_ref, c_ref, l_ref, wo_ref, code_ref, *refs
):
    dc_ref = refs[-1]
    if last == D:
        dr1_ref, wq_ref, dp_ref, sm_ref, ig_ref = refs[:5]
    else:
        dp_ref, sm_ref = refs[:2]
    rows, keys = (rows_of(document), rows_of(document, KEYS))
    e1 = e1_ref[rows, :]
    for start in range(first, last, STEP):
        cols = at_columns(start)
        dc_ref[:, cols] = dot_rows(e1, wo_ref[cols, :]).astype(low)
    bias = score_bias(code_ref, document)
    for start in range(first, last, LANES):
        cols = at_columns(start, LANES)
        q, k, v, dc = (q_ref[rows, cols], k_ref[keys, cols], v_ref[keys, cols], dc_ref[:, cols])
        product = dc.astype(wide) * c_ref[rows, cols].astype(wide)
        dq, dk, dv = (0.0, 0.0, 0.0)
        for head, row in enumerate(head_ones()):
            q_head, k_head, dc_head = (of_head(leaf, row) for leaf in (q, k, dc))
            column = HEAD * head + start // LANES
            logs = l_ref[rows, column : column + 1]
            inner = jnp.sum(of_head(product, row), axis=1, keepdims=True)
            p = jnp.exp(dot_rows(q_head, k) + bias - logs)
            ds = (p * (dot_rows(dc_head, v) - inner)).astype(low)
            dq = dq + dot(ds, k_head)
            both = dot_columns(
                jnp.concatenate([ds, p.astype(low)], axis=1),
                jnp.concatenate([q_head, dc_head], axis=1),
            )
            dk = dk + both[:KEYS, :LANES]
            dv = dv + both[KEYS:, LANES:]
        dq = dq.astype(low) * low(0.125)
        dv = dv[:SEQ].astype(low)
        dp_ref[rows, cols] = dq
        dp_ref[rows, at_columns(D + start, LANES)] = dk[:SEQ].astype(low)
        dp_ref[rows, at_columns(2 * D + start, LANES)] = dv
        sm_ref[8 * document : 8 * document + 1, cols] = column_sum(dq.astype(wide))
        sm_ref[8 * document + 1 : 8 * document + 2, cols] = column_sum(dv.astype(wide))
    if last < D:
        return
    dp = dp_ref[rows, :]
    for start in range(0, D, STEP):
        cols = at_columns(start)
        gi = (dr1_ref[:, cols] + dot_rows(dp, wq_ref[cols, :])).astype(low)
        ig_ref[rows, cols] = gi
        for gi_ref in refs[5:-1]:
            gi_ref[:, cols] = gi


def weight_kernel(pairs, rows, added, mine, *refs):
    me = lax.axis_index("pair")
    sums, part = (refs[2 * pairs : -1], refs[-1])
    owner = me if mine else 1 - me
    block = D // 2
    column = 0
    for k in range(pairs):
        left, right = refs[2 * k : 2 * k + 2]
        half = left.shape[1] // 2
        width = right.shape[1]
        for row in range(0, half, block):
            lefts = left[rows, pl.ds(pl.multiple_of(owner * half + row, LANES), block)]
            for start in range(0, width, STEP):
                place = (slice(row, row + block), at_columns(column + start))
                value = dot_columns(lefts, right[rows, at_columns(start)])
                if added:
                    value = value + part[place].astype(wide)
                part[place] = value.astype(low)
        column += width
    if sums:
        small_part(sums, owner, part, column)


def first_weight_kernel(pairs, mine, *refs):
    first = lax.axis_index("pipe") == 0
    pl.when(first)(lambda: weight_kernel(pairs, rows_of(0), False, mine, *refs))
    pl.when(jnp.logical_not(first))(
        lambda: weight_kernel(pairs, slice(0, MB * SEQ), False, mine, *refs)
    )


def small_part(sums, owner, part, column):
    top_ref, feed_ref, attend_ref, up_ref = sums
    order = (
        (attend_ref, 0), (attend_ref, 1), (feed_ref, 2), (top_ref, 2),
        (feed_ref, 0), (top_ref, 0), (feed_ref, 1), (top_ref, 1),
    )
    places = [(ref, row, D // 2) for ref, row in order] + [(up_ref, 0, FF // 2)]
    lines = []
    for ref, row, half in places:
        for start in range(0, half, LANES):
            cols = pl.ds(pl.multiple_of(owner * half + start, LANES), LANES)
            lines.append(ref[row : row + 1, cols] + ref[row + 8 : row + 9, cols])
    lines.append(jnp.zeros((48 - len(lines), LANES), wide))
    tile = at_columns(column, LANES)
    part[0:48, tile] = jnp.concatenate(lines, axis=0).astype(low)
    part[48:, tile] = jnp.zeros((part.shape[0] - 48, LANES), low)


def ring_row(stride, size, step, rows):
    index = lax.rem(ring_at(stride, size) - step + size, size)
    return pl.multiple_of(index * rows, rows)


def combine_kernel(stride, size, step, *refs):
    terms, arrived, out_ref = (refs[:2], refs[2:-1], refs[-1])
    first = ring_row(stride, size, step, out_ref.shape[0])

    def piece(k, carry):
        here = pl.ds(pl.multiple_of(k * 16, 16), 16)
        there = pl.ds(pl.multiple_of(first + k * 16, 16), 16)
        value = terms[0][there, :].astype(wide) + terms[1][there, :].astype(wide)
        for ref in arrived:
            value = value + ref[here, :].astype(wide)
        out_ref[here, :] = value.astype(low)
        return carry

    lax.fori_loop(0, out_ref.shape[0] // 16, piece, 0)


def store_kernel(stride, size, step, cuts, block_ref, *refs):
    count = len(cuts)
    totals, scratch, sems = (refs[:count], refs[count:-1], refs[-1])
    rows = block_ref.shape[0]
    first = ring_row(stride, size, step - 1, rows)

    def piece(k, carry):
        here = pl.ds(pl.multiple_of(k * 16, 16), 16)
        column = 0
        for part, cut in enumerate(cuts):
            scratch[part][here, :] = block_ref[here, column : column + cut].astype(wide)
            column += cut
        return carry

    lax.fori_loop(0, rows // 16, piece, 0)
    copies = [
        pltpu.make_async_copy(scratch[k], totals[k].at[pl.ds(first, rows)], sems.at[k])
        for k in range(count)
    ]
    for copy in copies:
        copy.start()
    for copy in copies:
        copy.wait()


def finish_kernel(sum_ref, qv_ref, up_ref, res_ref, gain_ref, shift_ref, held_ref, sem):
    copy = pltpu.make_async_copy(sum_ref.at[pl.ds(0, 48)], held_ref, sem.at[0])
    copy.start()
    copy.wait()
    line = 0
    for ref in (qv_ref, res_ref, gain_ref, shift_ref, up_ref):
        for row in range(ref.shape[0]):
            for start in range(0, ref.shape[1], LANES):
                ref[row : row + 1, at_columns(start, LANES)] = held_ref[line : line + 1, :]
                line += 1


def near(shape, dtype):
    return pltpu.VMEM(shape, dtype)


def far(shape, dtype):
    return pltpu.HBM(shape, dtype)


def run(
    kernel, name, operands, outputs, scratch=(), flops=0, section=None, keep=None, spaces=None
):
    keep = [] if keep is None else list(keep)
    count = len(operands)
    spaces = [pltpu.VMEM] * count if spaces is None else list(spaces)
    placed = [getattr(leaf, "memory_space", pltpu.VMEM) for leaf in outputs]
    spaces += placed[: len(keep)]
    operands = [
        leaf
        if space in (None, pltpu.SMEM)
        else pltpu.with_memory_space_constraint(leaf, space)
        for leaf, space in zip(list(operands) + keep, spaces)
    ]

    def body(*refs):
        used = refs[:count] + refs[count + len(keep) :]
        if section is None:
            kernel(*used)
        else:
            pl.when(lax.axis_index("pipe") == section)(lambda: kernel(*used))

    return pl.pallas_call(
        body,
        out_shape=tuple(outputs),
        in_specs=[pl.BlockSpec(memory_space=space or pltpu.VMEM) for space in spaces],
        out_specs=tuple(pl.BlockSpec(memory_space=space) for space in placed),
        scratch_shapes=list(scratch),
        input_output_aliases={count + k: k for k in range(len(keep))},
        name=name,
        cost_estimate=pl.CostEstimate(flops=flops, bytes_accessed=0, transcendentals=0),
        compiler_params=pltpu.CompilerParams(vmem_limit_bytes=4 << 20),
    )(*operands)


def join_halves(name, halves, place_of, space, keep=None, whole=()):
    outputs = [near((2 * leaf.shape[0], leaf.shape[1]), leaf.dtype) for leaf in halves]
    outputs += [near(leaf.shape, leaf.dtype) for leaf in whole]
    halves = list(halves) + list(whole)
    return run(
        lambda *refs: join_kernel(len(halves), place_of, *refs),
        name,
        halves,
        outputs,
        [pltpu.SemaphoreType.DMA((len(halves),))],
        keep=keep,
        spaces=[space] * len(halves),
    )


def join_both(name, own, other):
    return run(
        join_both_kernel,
        name,
        [own, other],
        [near((2 * own.shape[0], own.shape[1]), own.dtype)],
        [pltpu.SemaphoreType.DMA((2,))],
    )[0]


def attend(section, document, source, source_row, w_qkv, code, vec, keep):
    rows = near((MB * SEQ, D), low)
    keys = near((MB * KEYS, D), low)
    return run(
        lambda *refs: attend_kernel(document, source_row, *refs),
        "attend",
        [source, w_qkv, code, vec],
        [rows, rows, keys, keys, rows, near((MB * SEQ, LANES), wide)],
        flops=2 * SEQ * D * (3 * D + 4 * KEYS),
        section=section,
        keep=keep,
    )


def feed_up(section, document, x, c, w_out, w_up, vec, bu, keep):
    rows = near((MB * SEQ, D), low)
    inner = near((MB * SEQ, FF), low)
    outs = run(
        lambda *refs: feed_up_kernel(document, *refs),
        "feed_up",
        [x, c, w_out, w_up, vec, bu],
        [rows, rows, inner, inner, near((MB * SEQ, LANES), wide)]
        + [near((SEQ, D), wide)],
        flops=2 * SEQ * D * (D + FF),
        section=section,
        keep=keep,
    )
    return (outs[:-1], outs[-1])


def feed_down(section, document, r, f, w_down, vec, keep):
    outs = run(
        lambda *refs: feed_down_kernel(document, *refs),
        "feed_down",
        [r, f, w_down, vec],
        [near((MB * SEQ, D), low), near((MB * SEQ, D), low), near((MB * SEQ, LANES), wide)]
        + [near((SEQ, D), low)] * (1 - section),
        [pltpu.VMEM((SEQ, D), wide)],
        flops=2 * SEQ * D * FF,
        section=section,
        keep=keep,
    )
    return (outs[:3], outs[3:])


def top_back(section, document, source, source_row, h2, rs, vec, keep):
    outs = run(
        lambda *refs: top_back_kernel(document, source_row, *refs),
        "top_back",
        [source, h2, rs, vec],
        [near((MB * SEQ, D), low), near((MB * 8, D), wide), near((SEQ, D), wide)],
        flops=2 * SEQ * D * D,
        section=section,
        keep=keep,
    )
    return (outs[:-1], outs[-1])


def feed_back(section, document, dr2, e2, slope, h1, rs, w_down, w_up, vec, keep):
    outs = run(
        lambda *refs: feed_back_kernel(document, *refs),
        "feed_back",
        [dr2, e2, slope, h1, rs, w_down, w_up, vec],
        [near((MB * SEQ, FF), low), near((MB * SEQ, D), low), near((MB * 8, D), wide)]
        + [near((MB * 8, FF), wide), near((SEQ, D), wide)],
        flops=2 * SEQ * D * 2 * FF,
        section=section,
        keep=keep,
    )
    return (outs[:-1], outs[-1])


def attend_back(section, document, first, last, e1, saved, w_out, code, extra, keep):
    outputs = [near((MB * SEQ, 3 * D), low), near((MB * 8, D), wide)]
    if last == D:
        outputs += [near((MB * SEQ, D), low)] + [near((SEQ, D), low)] * section
    share = 6 * D if last == D else 0
    return run(
        lambda *refs: attend_back_kernel(document, first, last, *refs),
        "attend_back",
        [e1, *saved, w_out, code, *extra],
        outputs,
        [pltpu.VMEM((SEQ, D), low)],
        flops=2 * SEQ * ((last - first) * (D + 10 * KEYS) + share * D),
        section=section,
        keep=keep,
    )


def weight_halves(name, *pairs, sums=None, keep=None):
    half = pairs[0][0].shape[1] // 2
    width = sum(right.shape[1] for left, right in pairs) + (LANES if sums is not None else 0)
    parts = []
    for mine in (False, True):
        if keep is None:
            kernel = lambda *refs: first_weight_kernel(len(pairs), mine, *refs)
        else:
            kernel = lambda *refs: weight_kernel(len(pairs), rows_of(1), True, mine, *refs)
        leaves = [leaf for pair in pairs for leaf in pair] + list(sums or ())
        if mine:
            leaves[0] = after(leaves[0], parts[0])
        parts += run(
            kernel,
            name,
            leaves,
            [near((half, width), low)],
            flops=2 * MB * SEQ * half * width,
            section=None if keep is None else 0,
            keep=None if keep is None else keep[len(parts) : len(parts) + 1],
        )
    return parts


def ring_levels(total):
    sizes = []
    while total > 1:
        size = max([k for k in range(2, 9) if total % k == 0], default=total)
        sizes.append(size)
        total //= size
    return sizes


def ring_place(total, stride, size, device):
    own = device // stride % size
    if total == size and size % 2 == 0:
        return jnp.where(own % 2 == 0, own // 2, size - (own + 1) // 2)
    return own


def ring_at(stride, size):
    at = ring_place(lax.axis_size("dp"), stride, size, lax.axis_index("dp"))
    return jnp.where(lax.axis_index("pair") == 0, at, lax.rem(size - at, size))


def ring_route(total, stride, size):
    order = list(range(size))
    if total == size and size % 2 == 0:
        order = list(range(0, size, 2)) + list(range(size - 1, 0, -2))
    route = []
    for device in range(total):
        own = device // stride % size
        target = order[(order.index(own) + 1) % size]
        target = device + (target - own) * stride
        route.append((device * 2, target * 2))
        route.append((target * 2 + 1, device * 2 + 1))
    return route


def ring_combine(stride, size, step, terms, arrived):
    rows = terms[0].shape[0] // size
    width = terms[0].shape[1]
    if rows % 16 == 0:
        return run(
            lambda *refs: combine_kernel(stride, size, step, *refs),
            "combine",
            list(terms) + arrived,
            [near((rows, width), low)],
            flops=combine_cost if step < 2 else later_cost,
        )[0]
    index = (ring_at(stride, size) - step + size) % size
    value = 0.0
    for leaf in terms:
        piece = lax.dynamic_slice_in_dim(leaf, index * rows, rows, 0)
        value = value + piece.astype(wide)
    for leaf in arrived:
        value = value + leaf.astype(wide)
    return value.astype(low)


def ring_store(stride, size, step, block, cuts, totals, dtype):
    rows = block.shape[0]
    if rows % 16 == 0 and dtype == wide:
        return run(
            lambda *refs: store_kernel(stride, size, step, cuts, *refs),
            "store",
            [block],
            [far((size * rows, cut), wide) for cut in cuts],
            [pltpu.VMEM((rows, cut), wide) for cut in cuts]
            + [pltpu.SemaphoreType.DMA((len(cuts),))],
            flops=store_cost,
            keep=totals,
        )
    if totals is None:
        totals = [jnp.zeros((size * rows, cut), dtype) for cut in cuts]
    index = (ring_at(stride, size) + 1 - step + size) % size
    column = 0
    stored = []
    for leaf, cut in zip(totals, cuts):
        piece = block[:, column : column + cut].astype(dtype)
        stored.append(lax.dynamic_update_slice_in_dim(leaf, piece, index * rows, 0))
        column += cut
    return stored


def ring_steps(terms, widths):
    total = lax.axis_size("dp")
    levels = []
    stride = 1
    for size in ring_levels(total):
        levels.append((stride, size))
        stride *= size
    token = yield None
    terms = [terms[0], after(terms[1], token)]
    running = None
    for stride, size in levels:
        route = ring_route(total, stride, size)
        if running is not None:
            terms = [running, jnp.zeros_like(running)]
        for step in range(size):
            arrived = []
            if step > 0:
                arrived = [after(lax.ppermute(running, ("dp", "pair"), route), token)]
            running = ring_combine(stride, size, step, terms, arrived)
            token = yield running
    for depth, (stride, size) in enumerate(levels[::-1]):
        route = ring_route(total, stride, size)
        last = depth == len(levels) - 1
        dtype, cuts = (wide, widths) if last else (low, [sum(widths)])
        totals = None
        for step in range(size):
            if step > 0:
                running = after(lax.ppermute(running, ("dp", "pair"), route), token)
            totals = ring_store(stride, size, step, running, cuts, totals, dtype)
            if step > 0:
                token = yield tuple(totals)
        running = totals[0]
    return totals


class Steps:
    def __init__(self, steps, left=0):
        self.steps, self.left, self.result = (steps, left, None)
        next(steps)

    def advance(self, token):
        self.left -= 1
        try:
            return self.steps.send(token)
        except StopIteration as done:
            self.result = done.value
            return token


def ring(own, away, widths):
    left = sum(2 * size - 1 for size in ring_levels(lax.axis_size("dp")))
    return Steps(ring_steps([own, from_pair(away)], widths), left)


def finish(sums):
    pairs = jax.ShapeDtypeStruct((2, D // 2), wide)
    outputs = [pairs, jax.ShapeDtypeStruct((1, FF // 2), wide), pairs, pairs, pairs]
    scratch = [pltpu.VMEM((48, LANES), wide), pltpu.SemaphoreType.DMA((1,))]
    return run(finish_kernel, "finish", [sums], outputs, scratch, spaces=[pltpu.HBM])


def export_kernel(*refs):
    count = len(refs) // 2
    copies = [
        pltpu.make_async_copy(refs[k], refs[count + k], refs[-1].at[k]) for k in range(count)
    ]
    for copy in copies:
        copy.start()
    for copy in copies:
        copy.wait()


def export(leaf, earlier):
    return run(
        export_kernel,
        "export",
        [after(leaf, earlier)],
        [far(leaf.shape, leaf.dtype)],
        [pltpu.SemaphoreType.DMA((1,))],
    )[0]


def from_pair(leaf):
    return lax.ppermute(leaf, "pair", swap)


def local(
    inputs,
    cotangent,
    text_mask,
    seg_count,
    align,
    w_qkv,
    w_out,
    w_up,
    w_down,
    bias_qv,
    bias_up,
    bias_res,
    norm_gain,
    norm_shift,
):
    own = [w_qkv[0], w_out[0], w_up[0], w_down[0]]
    other_qkv = from_pair(own[0])
    params = [bias_qv[0], bias_res[0], norm_gain[0], norm_shift[0], bias_up, text_mask, align]
    packed, code = run(
        pack_kernel,
        "pack",
        [seg_count] + params,
        [near((16, D // 2), wide), near((MB * 8, KEYS), jnp.int32)],
        [pltpu.VMEM(leaf.shape, leaf.dtype) for leaf in params]
        + [pltpu.SemaphoreType.DMA((len(params),))],
        spaces=[pltpu.SMEM] + [pltpu.HBM] * len(params),
    )
    packed_other = from_pair(packed)
    mine = lambda me: me
    others = lambda me: 1 - me
    other_out = from_pair(own[1])
    held = [after(own[0], packed), own[1]]
    joined = join_halves("join_own", held, mine, pltpu.HBM, whole=(inputs,))
    inputs = joined[2]
    vec, bu = run(
        unpack_kernel,
        "unpack",
        [packed, after(packed_other, joined[0])],
        [near((8, D), wide), near((8, FF), wide)],
    )
    other_qkv, other_out, vec = lax.optimization_barrier((other_qkv, other_out, vec))
    other_up = from_pair(after(own[2], other_qkv))
    wq, wo = join_halves("join_qkv", [other_qkv, other_out], others, pltpu.VMEM, joined[:2])

    attended, raised, lowered = (None, None, None)
    topped, fed_back, attended_back = (None, None, None)
    onward, backward = ([None] * MB, [None] * MB)
    for section, document in ((0, 0), (0, 1), (1, 0), (1, 1)):
        source, row = (inputs, document * SEQ) if section == 0 else (onward[document], 0)
        if attended_back is not None:
            source = after(source, attended_back[0])
        attended = attend(section, document, source, row, wq, code, vec, attended)
        x, q, k, v, c, logs = attended
        if raised is None:
            other_up = after(other_up, x)
            other_down = from_pair(after(own[3], other_up))
            wu = join_both("join_up", own[2], other_up)
        raised, r = feed_up(section, document, x, c, wo, wu, vec, bu, raised)
        h1, n1, f, slope, rs1 = raised
        if lowered is None:
            wd = join_both("join_down", own[3], after(other_down, r))
        lowered, y = feed_down(section, document, r, f, wd, vec, lowered)
        section_out, h2, rs2 = lowered
        if section == 0:
            onward[document] = passed_along(y[0], "pipe", 1)
            continue
        topped, dr2 = top_back(section, document, cotangent, document * SEQ, h2, rs2, vec, topped)
        fed_back, dr1 = feed_back(
            section, document, dr2, topped[0], slope, h1, rs1, wd, wu, vec, fed_back
        )
        attended_back = attend_back(
            section, document, 0, D, fed_back[1], (q, k, v, c, logs), wo, code, (dr1, wq),
            attended_back,
        )
        backward[document] = passed_along(attended_back[3], "pipe", -1)
        attended_back = attended_back[:3]
    saved = (q, k, v, c, logs)

    source = after(backward[0], attended_back[0])
    topped, dr2 = top_back(0, 0, source, 0, h2, rs2, vec, topped)
    fed_back, dr1 = feed_back(0, 0, dr2, topped[0], slope, h1, rs1, wd, wu, vec, fed_back)
    attended_back = attend_back(
        0, 0, 0, D, fed_back[1], saved, wo, code, (dr1, wq), attended_back
    )
    share_down = weight_halves("weight_down", (f, topped[0]))
    share_up = weight_halves("weight_up", (n1, fed_back[0]))
    empty = (topped[1], fed_back[2], attended_back[1], fed_back[3])
    share_rest = weight_halves("weight_rest", (x, attended_back[0]), (c, fed_back[1]), sums=empty)

    section_out = export(section_out, share_rest[1])
    source = after(backward[1], (share_down[1], share_up[1], share_rest[1], section_out))
    topped, dr2 = top_back(0, 1, source, 0, h2, rs2, vec, topped)
    away, own = weight_halves("weight_down", (f, topped[0]), keep=share_down)
    dr2 = after(dr2, away)
    ring_down = ring(own, away, [D])
    fed_back, dr1 = feed_back(0, 1, dr2, topped[0], slope, h1, rs1, wd, wu, vec, fed_back)
    e2, small_top = topped
    du, e1, small_feed, small_up = fed_back
    token = ring_down.advance(du)
    away, own = weight_halves("weight_up", (n1, after(du, token)), keep=share_up)
    ring_up = ring(own, away, [FF])
    dp, small_attend, input_grad = attend_back(
        0, 1, 0, D, after(e1, away), saved, wo, code, (dr1, wq), attended_back
    )
    token = ring_down.advance(dp)
    token = ring_up.advance(token)
    dp = after(dp, token)
    sums = [small_top, small_feed, small_attend, small_up]
    away, own = weight_halves("weight_rest", (x, dp), (c, e1), sums=sums, keep=share_rest)
    ring_rest = ring(own, away, [3 * D, D, LANES])
    token = away

    rings = [ring_down, ring_up, ring_rest]
    token = ring_down.advance(token)
    token = ring_up.advance(token)
    turn = 0
    while any(each.left > 0 for each in rings):
        extra = [ring_rest] if turn < 2 else []
        for each in [ring_rest, ring_down] + extra + [ring_up]:
            if each.left > 0:
                token = each.advance(token)
        turn += 1
        if turn == 2:
            input_grad = token = export(input_grad, token)
    for each in rings:
        while each.result is None:
            token = each.advance(token)
    (grad_down,), (grad_up,), (grad_qkv, grad_out, sums) = (each.result for each in rings)
    grad_qv, grad_bias_up, grad_res, grad_gain, grad_shift = finish(sums)
    results = (section_out, input_grad, grad_qkv, grad_out, grad_up, grad_down, grad_qv)
    results += (grad_bias_up, grad_res, grad_gain, grad_shift)
    return tuple(leaf if leaf is grad_bias_up else leaf[None] for leaf in results)


def solution(mesh):
    return jax.shard_map(
        local,
        mesh=mesh,
        in_specs=(
            P(("dp", "pair"), None),
            P(("dp", "pair"), None),
            P(("dp", "pair"), None),
            P(("dp", "pair")),
            P(("dp", "pair"), None),
            P("pipe", "pair", None),
            P("pipe", "pair", None),
            P("pipe", "pair", None),
            P("pipe", "pair", None),
            P("pipe", None, "pair"),
            P("pipe", "pair"),
            P("pipe", None, "pair"),
            P("pipe", None, "pair"),
            P("pipe", None, "pair"),
        ),
        out_specs=(
            P("pipe", ("dp", "pair"), None),
            P("pipe", ("dp", "pair"), None),
            P("pipe", "pair", None),
            P("pipe", "pair", None),
            P("pipe", "pair", None),
            P("pipe", "pair", None),
            P("pipe", None, "pair"),
            P("pipe", "pair"),
            P("pipe", None, "pair"),
            P("pipe", None, "pair"),
            P("pipe", None, "pair"),
        ),
        check_vma=False,
    )
```

```python
import jax
import jax.numpy as jnp
from jax import lax
from jax.experimental import pallas as pl
from jax.experimental.pallas import tpu as pltpu
from jax.sharding import PartitionSpec as P

D = 768
HEADS = 12
HEAD = 64
FF = 3072
TEXT = 176
SLOTS = 64
SEQ = 240
KEYS = 256
MB = 2
LANES = 128
STEP = 256


epsilon = 1e-06
masked_score = -1e30
gelu_one = 0.7978845608028654
gelu_two = 0.044715
low = jnp.bfloat16
wide = jnp.float32
swap = [(0, 1), (1, 0)]
combine_cost = 1 << 35
later_cost = 1 << 35
store_cost = 1 << 29


def passed_along(block, axis, distance):
    devices = range(lax.axis_size(axis))
    route = [(i - distance, i) for i in devices if i - distance in devices]
    return lax.ppermute(block, axis, route)


def after(value, earlier):
    return value if earlier is None else lax.optimization_barrier((value, earlier))[0]


def dot(left, right):
    return lax.dot_general(left, right, (((1,), (0,)), ((), ())), preferred_element_type=wide)


def dot_rows(left, right):
    return lax.dot_general(left, right, (((1,), (1,)), ((), ())), preferred_element_type=wide)


def dot_columns(left, right):
    return lax.dot_general(left, right, (((0,), (0,)), ((), ())), preferred_element_type=wide)


def column_sum(values):
    return jnp.sum(values, axis=0, keepdims=True)


def at_columns(start, size=STEP):
    return slice(start, start + size)


def score_bias(code_ref, document):
    code = code_ref[8 * document : 8 * document + 1, :]
    slot = lax.broadcasted_iota(jnp.int32, (SEQ, KEYS), 0) - TEXT
    keep = (code > -2) & ((slot < 0) | (code == -1) | (code == slot))
    return jnp.where(keep, 0.0, masked_score)


def in_first_head(rows):
    return lax.broadcasted_iota(jnp.int32, (rows, LANES), 1) < HEAD


def head_ones():
    first = lax.broadcasted_iota(jnp.int32, (1, LANES), 1) < HEAD
    first = jnp.where(first, 1.0, 0.0)
    return (first, 1.0 - first)


def of_head(values, row):
    return values * row.astype(values.dtype)


def normalize(values):
    center = values - jnp.mean(values, axis=1, keepdims=True)
    scale = lax.rsqrt(jnp.mean(center * center, axis=1, keepdims=True) + epsilon)
    return (center * scale, scale)


def normalize_back(grad, normal, scale):
    flat = jnp.mean(grad, axis=1, keepdims=True)
    along = jnp.mean(grad * normal, axis=1, keepdims=True)
    return scale * (grad - flat - normal * along)


def rows_of(document, size=SEQ):
    return slice(document * size, document * size + size)


def pack_kernel(*refs):
    sources, (packed_ref, code_ref), held, sems = (refs[:8], refs[8:10], refs[10:18], refs[18])
    copies = [
        pltpu.make_async_copy(source, target, sems.at[k])
        for k, (source, target) in enumerate(zip(sources, held))
    ]
    for copy in copies:
        copy.start()
    for copy in copies:
        copy.wait()
    half = D // 2
    for place, ref in enumerate(held[:4]):
        packed_ref[2 * place : 2 * place + 2, :] = ref[...].astype(wide)
    for place in range(FF // D):
        packed_ref[8 + place : 9 + place, :] = held[4][
            0:1, half * place : half * place + half
        ].astype(wide)
    packed_ref[12:16, :] = jnp.zeros((4, half), wide)
    code = jnp.where(held[5][...] == 1, held[6][...], -2)
    slot = lax.broadcasted_iota(jnp.int32, (1, SLOTS), 1)
    for document in range(MB):
        rows = slice(8 * document, 8 * document + 8)
        code_ref[rows, :] = jnp.full((8, KEYS), -2, jnp.int32)
        code_ref[8 * document : 8 * document + 1, 0:TEXT] = code[document : document + 1, :]
        code_ref[8 * document : 8 * document + 1, TEXT:SEQ] = jnp.where(
            slot < held[7][document], -1, -2
        )


def unpack_kernel(own_ref, other_ref, vec_ref, bu_ref):
    half = D // 2
    me = lax.axis_index("pair")
    for ref, place in ((own_ref, me), (other_ref, 1 - me)):
        vec_ref[:, pl.ds(pl.multiple_of(place * half, LANES), half)] = ref[0:8, :]
        for row in range(FF // D):
            start = place * (FF // 2) + row * half
            bu_ref[0:1, pl.ds(pl.multiple_of(start, LANES), half)] = ref[8 + row : 9 + row, :]


def join_kernel(count, place_of, *refs):
    half, full, sems = (refs[:count], refs[-count - 1 : -1], refs[-1])
    place = place_of(lax.axis_index("pair"))
    copies = []
    for k in range(count):
        rows = half[k].shape[0]
        if rows == full[k].shape[0]:
            target = full[k]
        else:
            target = full[k].at[pl.ds(pl.multiple_of(place * rows, rows), rows)]
        copies.append(pltpu.make_async_copy(half[k], target, sems.at[k]))
    for copy in copies:
        copy.start()
    for copy in copies:
        copy.wait()


def join_both_kernel(own_ref, other_ref, full_ref, sems):
    me = lax.axis_index("pair")
    rows = own_ref.shape[0]
    copies = []
    for part, (source, place) in enumerate(((own_ref, me), (other_ref, 1 - me))):
        target = full_ref.at[pl.ds(pl.multiple_of(place * rows, rows), rows)]
        copies.append(pltpu.make_async_copy(source, target, sems.at[part]))
    for copy in copies:
        copy.start()
    for copy in copies:
        copy.wait()


def attend_kernel(
    document, source_row, source_ref, w_ref, code_ref, vec_ref,
    x_ref, q_ref, k_ref, v_ref, c_ref, l_ref,
):
    rows, keys = (rows_of(document), rows_of(document, KEYS))
    real = slice(document * KEYS, document * KEYS + SEQ)
    rest = slice(document * KEYS + SEQ, document * KEYS + KEYS)
    x = source_ref[source_row : source_row + SEQ, :]
    x_ref[rows, :] = x
    for start in range(0, D, STEP):
        cols = at_columns(start)
        queries = dot(x, w_ref[:, cols]) + vec_ref[0:1, cols]
        q_ref[rows, cols] = (queries * 0.125).astype(low)
        k_ref[real, cols] = dot(x, w_ref[:, at_columns(D + start)]).astype(low)
        values = dot(x, w_ref[:, at_columns(2 * D + start)]) + vec_ref[1:2, cols]
        v_ref[real, cols] = values.astype(low)
    k_ref[rest, :] = jnp.zeros((KEYS - SEQ, D), low)
    v_ref[rest, :] = jnp.zeros((KEYS - SEQ, D), low)
    bias = score_bias(code_ref, document)
    bias = jnp.concatenate([bias, bias], axis=0)
    first = in_first_head(SEQ)
    lane = lax.broadcasted_iota(jnp.int32, (SEQ, LANES), 1) % HEAD
    kept = jnp.zeros((SEQ, LANES), wide)
    ones = jnp.ones((KEYS, LANES), low)
    for start in range(0, D, LANES):
        cols = at_columns(start, LANES)
        q, k, v = (q_ref[rows, cols], k_ref[keys, cols], v_ref[keys, cols])
        queries = jnp.concatenate([of_head(q, row) for row in head_ones()], axis=0)
        scores = dot_rows(queries, k) + bias
        top = jnp.max(scores, axis=1, keepdims=True)
        weight = jnp.exp(scores - top).astype(low)
        both = dot(weight, jnp.concatenate([v, ones], axis=1))
        total = jnp.where(first, both[:SEQ, :LANES], both[SEQ:, :LANES])
        sums = jnp.where(first, both[:SEQ, LANES:], both[SEQ:, LANES:])
        c_ref[rows, cols] = (total / sums).astype(low)
        logs = jnp.where(first, top[:SEQ], top[SEQ:]) + jnp.log(sums)
        kept = jnp.where(lane == start // LANES, logs, kept)
    l_ref[rows, :] = kept


def feed_up_kernel(
    document, x_ref, c_ref, wo_ref, wu_ref, vec_ref, bu_ref,
    h1_ref, n1_ref, f_ref, s_ref, rs_ref, r_ref,
):
    rows = rows_of(document)
    c = c_ref[rows, :]
    for start in range(0, D, STEP):
        cols = at_columns(start)
        r_ref[:, cols] = (
            x_ref[rows, cols].astype(wide) + dot(c, wo_ref[:, cols]) + vec_ref[2:3, cols]
        )
    h1, scale = normalize(r_ref[...])
    h1_ref[rows, :] = h1.astype(low)
    rs_ref[rows, :] = jnp.broadcast_to(scale, (SEQ, LANES))
    n1 = h1 * vec_ref[4:5, :] + vec_ref[6:7, :]
    n1_low = n1.astype(low)
    n1_ref[rows, :] = n1_low
    r_ref[...] = n1 + vec_ref[3:4, :]
    for start in range(0, FF, STEP):
        cols = at_columns(start)
        u = dot(n1_low, wu_ref[:, cols]) + bu_ref[0:1, cols]
        square = u * u
        bend = jnp.tanh(u * (gelu_one + gelu_one * gelu_two * square))
        half = 0.5 + 0.5 * bend
        active = u * half
        f_ref[rows, cols] = active.astype(low)
        along = 2 * gelu_one + 6 * gelu_one * gelu_two * square
        s_ref[rows, cols] = (half + active * (1.0 - half) * along).astype(low)


def feed_down_kernel(
    document, r_ref, f_ref, wd_ref, vec_ref, section_ref, h2_ref, rs_ref, *rest
):
    sum_ref = rest[-1]
    rows = rows_of(document)
    f = f_ref[rows, :]
    for start in range(0, D, STEP):
        cols = at_columns(start)
        sum_ref[:, cols] = r_ref[:, cols] + dot(f, wd_ref[:, cols])
    h2, scale = normalize(sum_ref[...])
    h2_ref[rows, :] = h2.astype(low)
    rs_ref[rows, :] = jnp.broadcast_to(scale, (SEQ, LANES))
    y = (h2 * vec_ref[5:6, :] + vec_ref[7:8, :]).astype(low)
    section_ref[rows, :] = y
    for y_ref in rest[:-1]:
        y_ref[...] = y


def top_back_kernel(
    document, source_row, source_ref, h2_ref, rs_ref, vec_ref, e2_ref, sm_ref, dr2_ref
):
    rows = rows_of(document)
    g = source_ref[source_row : source_row + SEQ, :].astype(wide)
    h2 = h2_ref[rows, :].astype(wide)
    dr2 = normalize_back(g * vec_ref[5:6, :], h2, rs_ref[rows, 0:1])
    e2 = dr2.astype(low)
    dr2_ref[...] = dr2
    e2_ref[rows, :] = e2
    sm_ref[8 * document : 8 * document + 1, :] = column_sum(g * h2)
    sm_ref[8 * document + 1 : 8 * document + 2, :] = column_sum(g)
    sm_ref[8 * document + 2 : 8 * document + 3, :] = column_sum(e2.astype(wide))


def feed_back_kernel(
    document, dr2_ref, e2_ref, s_ref, h1_ref, rs_ref, wd_ref, wu_ref, vec_ref,
    du_ref, e1_ref, sm_ref, smu_ref, dr1_ref,
):
    rows = rows_of(document)
    e2 = e2_ref[rows, :]
    for start in range(0, FF, STEP):
        cols = at_columns(start)
        du = (dot_rows(e2, wd_ref[cols, :]) * s_ref[rows, cols].astype(wide)).astype(low)
        du_ref[rows, cols] = du
        smu_ref[8 * document : 8 * document + 1, cols] = column_sum(du.astype(wide))
    du = du_ref[rows, :]
    for start in range(0, D, STEP):
        cols = at_columns(start)
        dr1_ref[:, cols] = dr2_ref[:, cols] + dot_rows(du, wu_ref[cols, :])
    g = dr1_ref[...]
    h1 = h1_ref[rows, :].astype(wide)
    dr1 = normalize_back(g * vec_ref[4:5, :], h1, rs_ref[rows, 0:1])
    e1 = dr1.astype(low)
    dr1_ref[...] = dr1
    e1_ref[rows, :] = e1
    sm_ref[8 * document : 8 * document + 1, :] = column_sum(g * h1)
    sm_ref[8 * document + 1 : 8 * document + 2, :] = column_sum(g)
    sm_ref[8 * document + 2 : 8 * document + 3, :] = column_sum(e1.astype(wide))


def attend_back_kernel(
    document, first, last, e1_ref, q_ref, k_ref, v_ref, c_ref, l_ref, wo_ref, code_ref, *refs
):
    dc_ref = refs[-1]
    if last == D:
        dr1_ref, wq_ref, dp_ref, sm_ref, ig_ref = refs[:5]
    else:
        dp_ref, sm_ref = refs[:2]
    rows, keys = (rows_of(document), rows_of(document, KEYS))
    e1 = e1_ref[rows, :]
    for start in range(first, last, STEP):
        cols = at_columns(start)
        dc_ref[:, cols] = dot_rows(e1, wo_ref[cols, :]).astype(low)
    bias = score_bias(code_ref, document)
    for start in range(first, last, LANES):
        cols = at_columns(start, LANES)
        q, k, v, dc = (q_ref[rows, cols], k_ref[keys, cols], v_ref[keys, cols], dc_ref[:, cols])
        product = dc.astype(wide) * c_ref[rows, cols].astype(wide)
        dq, dk, dv = (0.0, 0.0, 0.0)
        for head, row in enumerate(head_ones()):
            q_head, k_head, dc_head = (of_head(leaf, row) for leaf in (q, k, dc))
            column = HEAD * head + start // LANES
            logs = l_ref[rows, column : column + 1]
            inner = jnp.sum(of_head(product, row), axis=1, keepdims=True)
            p = jnp.exp(dot_rows(q_head, k) + bias - logs)
            ds = (p * (dot_rows(dc_head, v) - inner)).astype(low)
            dq = dq + dot(ds, k_head)
            both = dot_columns(
                jnp.concatenate([ds, p.astype(low)], axis=1),
                jnp.concatenate([q_head, dc_head], axis=1),
            )
            dk = dk + both[:KEYS, :LANES]
            dv = dv + both[KEYS:, LANES:]
        dq = dq.astype(low) * low(0.125)
        dv = dv[:SEQ].astype(low)
        dp_ref[rows, cols] = dq
        dp_ref[rows, at_columns(D + start, LANES)] = dk[:SEQ].astype(low)
        dp_ref[rows, at_columns(2 * D + start, LANES)] = dv
        sm_ref[8 * document : 8 * document + 1, cols] = column_sum(dq.astype(wide))
        sm_ref[8 * document + 1 : 8 * document + 2, cols] = column_sum(dv.astype(wide))
    if last < D:
        return
    dp = dp_ref[rows, :]
    for start in range(0, D, STEP):
        cols = at_columns(start)
        gi = (dr1_ref[:, cols] + dot_rows(dp, wq_ref[cols, :])).astype(low)
        ig_ref[rows, cols] = gi
        for gi_ref in refs[5:-1]:
            gi_ref[:, cols] = gi


def weight_kernel(pairs, rows, added, mine, *refs):
    me = lax.axis_index("pair")
    sums, part = (refs[2 * pairs : -1], refs[-1])
    owner = me if mine else 1 - me
    block = D // 2
    column = 0
    for k in range(pairs):
        left, right = refs[2 * k : 2 * k + 2]
        half = left.shape[1] // 2
        width = right.shape[1]
        for row in range(0, half, block):
            lefts = left[rows, pl.ds(pl.multiple_of(owner * half + row, LANES), block)]
            for start in range(0, width, STEP):
                place = (slice(row, row + block), at_columns(column + start))
                value = dot_columns(lefts, right[rows, at_columns(start)])
                if added:
                    value = value + part[place].astype(wide)
                part[place] = value.astype(low)
        column += width
    if sums:
        small_part(sums, owner, part, column)


def first_weight_kernel(pairs, mine, *refs):
    first = lax.axis_index("pipe") == 0
    pl.when(first)(lambda: weight_kernel(pairs, rows_of(0), False, mine, *refs))
    pl.when(jnp.logical_not(first))(
        lambda: weight_kernel(pairs, slice(0, MB * SEQ), False, mine, *refs)
    )


def small_part(sums, owner, part, column):
    top_ref, feed_ref, attend_ref, up_ref = sums
    order = (
        (attend_ref, 0), (attend_ref, 1), (feed_ref, 2), (top_ref, 2),
        (feed_ref, 0), (top_ref, 0), (feed_ref, 1), (top_ref, 1),
    )
    places = [(ref, row, D // 2) for ref, row in order] + [(up_ref, 0, FF // 2)]
    lines = []
    for ref, row, half in places:
        for start in range(0, half, LANES):
            cols = pl.ds(pl.multiple_of(owner * half + start, LANES), LANES)
            lines.append(ref[row : row + 1, cols] + ref[row + 8 : row + 9, cols])
    lines.append(jnp.zeros((48 - len(lines), LANES), wide))
    tile = at_columns(column, LANES)
    part[0:48, tile] = jnp.concatenate(lines, axis=0).astype(low)
    part[48:, tile] = jnp.zeros((part.shape[0] - 48, LANES), low)


def ring_row(stride, size, step, rows):
    index = lax.rem(ring_at(stride, size) - step + size, size)
    return pl.multiple_of(index * rows, rows)


def combine_kernel(stride, size, step, *refs):
    terms, arrived, out_ref = (refs[:2], refs[2:-1], refs[-1])
    first = ring_row(stride, size, step, out_ref.shape[0])

    def piece(k, carry):
        here = pl.ds(pl.multiple_of(k * 16, 16), 16)
        there = pl.ds(pl.multiple_of(first + k * 16, 16), 16)
        value = terms[0][there, :].astype(wide) + terms[1][there, :].astype(wide)
        for ref in arrived:
            value = value + ref[here, :].astype(wide)
        out_ref[here, :] = value.astype(low)
        return carry

    lax.fori_loop(0, out_ref.shape[0] // 16, piece, 0)


def store_kernel(stride, size, step, cuts, block_ref, *refs):
    count = len(cuts)
    totals, scratch, sems = (refs[:count], refs[count:-1], refs[-1])
    rows = block_ref.shape[0]
    first = ring_row(stride, size, step - 1, rows)

    def piece(k, carry):
        here = pl.ds(pl.multiple_of(k * 16, 16), 16)
        column = 0
        for part, cut in enumerate(cuts):
            scratch[part][here, :] = block_ref[here, column : column + cut].astype(wide)
            column += cut
        return carry

    lax.fori_loop(0, rows // 16, piece, 0)
    copies = [
        pltpu.make_async_copy(scratch[k], totals[k].at[pl.ds(first, rows)], sems.at[k])
        for k in range(count)
    ]
    for copy in copies:
        copy.start()
    for copy in copies:
        copy.wait()


def finish_kernel(sum_ref, qv_ref, up_ref, res_ref, gain_ref, shift_ref, held_ref, sem):
    copy = pltpu.make_async_copy(sum_ref.at[pl.ds(0, 48)], held_ref, sem.at[0])
    copy.start()
    copy.wait()
    line = 0
    for ref in (qv_ref, res_ref, gain_ref, shift_ref, up_ref):
        for row in range(ref.shape[0]):
            for start in range(0, ref.shape[1], LANES):
                ref[row : row + 1, at_columns(start, LANES)] = held_ref[line : line + 1, :]
                line += 1


def near(shape, dtype):
    return pltpu.VMEM(shape, dtype)


def far(shape, dtype):
    return pltpu.HBM(shape, dtype)


def run(
    kernel, name, operands, outputs, scratch=(), flops=0, section=None, keep=None, spaces=None
):
    keep = [] if keep is None else list(keep)
    count = len(operands)
    spaces = [pltpu.VMEM] * count if spaces is None else list(spaces)
    placed = [getattr(leaf, "memory_space", pltpu.VMEM) for leaf in outputs]
    spaces += placed[: len(keep)]
    operands = [
        leaf
        if space in (None, pltpu.SMEM)
        else pltpu.with_memory_space_constraint(leaf, space)
        for leaf, space in zip(list(operands) + keep, spaces)
    ]

    def body(*refs):
        used = refs[:count] + refs[count + len(keep) :]
        if section is None:
            kernel(*used)
        else:
            pl.when(lax.axis_index("pipe") == section)(lambda: kernel(*used))

    return pl.pallas_call(
        body,
        out_shape=tuple(outputs),
        in_specs=[pl.BlockSpec(memory_space=space or pltpu.VMEM) for space in spaces],
        out_specs=tuple(pl.BlockSpec(memory_space=space) for space in placed),
        scratch_shapes=list(scratch),
        input_output_aliases={count + k: k for k in range(len(keep))},
        name=name,
        cost_estimate=pl.CostEstimate(flops=flops, bytes_accessed=0, transcendentals=0),
        compiler_params=pltpu.CompilerParams(vmem_limit_bytes=(6 if name.startswith("weight") else 4) << 20),
    )(*operands)


def join_halves(name, halves, place_of, space, keep=None, whole=()):
    outputs = [near((2 * leaf.shape[0], leaf.shape[1]), leaf.dtype) for leaf in halves]
    outputs += [near(leaf.shape, leaf.dtype) for leaf in whole]
    halves = list(halves) + list(whole)
    return run(
        lambda *refs: join_kernel(len(halves), place_of, *refs),
        name,
        halves,
        outputs,
        [pltpu.SemaphoreType.DMA((len(halves),))],
        keep=keep,
        spaces=[space] * len(halves),
    )


def join_both(name, own, other):
    return run(
        join_both_kernel,
        name,
        [own, other],
        [near((2 * own.shape[0], own.shape[1]), own.dtype)],
        [pltpu.SemaphoreType.DMA((2,))],
    )[0]


def attend(section, document, source, source_row, w_qkv, code, vec, keep):
    rows = near((MB * SEQ, D), low)
    keys = near((MB * KEYS, D), low)
    return run(
        lambda *refs: attend_kernel(document, source_row, *refs),
        "attend",
        [source, w_qkv, code, vec],
        [rows, rows, keys, keys, rows, near((MB * SEQ, LANES), wide)],
        flops=2 * SEQ * D * (3 * D + 4 * KEYS),
        section=section,
        keep=keep,
    )


def feed_up(section, document, x, c, w_out, w_up, vec, bu, keep):
    rows = near((MB * SEQ, D), low)
    inner = near((MB * SEQ, FF), low)
    outs = run(
        lambda *refs: feed_up_kernel(document, *refs),
        "feed_up",
        [x, c, w_out, w_up, vec, bu],
        [rows, rows, inner, inner, near((MB * SEQ, LANES), wide)]
        + [near((SEQ, D), wide)],
        flops=2 * SEQ * D * (D + FF),
        section=section,
        keep=keep,
    )
    return (outs[:-1], outs[-1])


def feed_down(section, document, r, f, w_down, vec, keep):
    outs = run(
        lambda *refs: feed_down_kernel(document, *refs),
        "feed_down",
        [r, f, w_down, vec],
        [near((MB * SEQ, D), low), near((MB * SEQ, D), low), near((MB * SEQ, LANES), wide)]
        + [near((SEQ, D), low)] * (1 - section),
        [pltpu.VMEM((SEQ, D), wide)],
        flops=2 * SEQ * D * FF,
        section=section,
        keep=keep,
    )
    return (outs[:3], outs[3:])


def top_back(section, document, source, source_row, h2, rs, vec, keep):
    outs = run(
        lambda *refs: top_back_kernel(document, source_row, *refs),
        "top_back",
        [source, h2, rs, vec],
        [near((MB * SEQ, D), low), near((MB * 8, D), wide), near((SEQ, D), wide)],
        flops=2 * SEQ * D * D,
        section=section,
        keep=keep,
    )
    return (outs[:-1], outs[-1])


def feed_back(section, document, dr2, e2, slope, h1, rs, w_down, w_up, vec, keep):
    outs = run(
        lambda *refs: feed_back_kernel(document, *refs),
        "feed_back",
        [dr2, e2, slope, h1, rs, w_down, w_up, vec],
        [near((MB * SEQ, FF), low), near((MB * SEQ, D), low), near((MB * 8, D), wide)]
        + [near((MB * 8, FF), wide), near((SEQ, D), wide)],
        flops=2 * SEQ * D * 2 * FF,
        section=section,
        keep=keep,
    )
    return (outs[:-1], outs[-1])


def attend_back(section, document, first, last, e1, saved, w_out, code, extra, keep):
    outputs = [near((MB * SEQ, 3 * D), low), near((MB * 8, D), wide)]
    if last == D:
        outputs += [near((MB * SEQ, D), low)] + [near((SEQ, D), low)] * section
    share = 6 * D if last == D else 0
    return run(
        lambda *refs: attend_back_kernel(document, first, last, *refs),
        "attend_back",
        [e1, *saved, w_out, code, *extra],
        outputs,
        [pltpu.VMEM((SEQ, D), low)],
        flops=2 * SEQ * ((last - first) * (D + 10 * KEYS) + share * D),
        section=section,
        keep=keep,
    )


def weight_halves(name, *pairs, sums=None, keep=None):
    half = pairs[0][0].shape[1] // 2
    width = sum(right.shape[1] for left, right in pairs) + (LANES if sums is not None else 0)
    parts = []
    for mine in (False, True):
        if keep is None:
            kernel = lambda *refs: first_weight_kernel(len(pairs), mine, *refs)
        else:
            kernel = lambda *refs: weight_kernel(len(pairs), rows_of(1), True, mine, *refs)
        leaves = [leaf for pair in pairs for leaf in pair] + list(sums or ())
        if mine:
            leaves[0] = after(leaves[0], parts[0])
        parts += run(
            kernel,
            name,
            leaves,
            [near((half, width), low)],
            flops=2 * MB * SEQ * half * width,
            section=None if keep is None else 0,
            keep=None if keep is None else keep[len(parts) : len(parts) + 1],
        )
    return parts


def ring_levels(total):
    sizes = []
    while total > 1:
        size = max([k for k in range(2, 9) if total % k == 0], default=total)
        sizes.append(size)
        total //= size
    return sizes


def ring_place(total, stride, size, device):
    own = device // stride % size
    if total == size and size % 2 == 0:
        return jnp.where(own % 2 == 0, own // 2, size - (own + 1) // 2)
    return own


def ring_at(stride, size):
    at = ring_place(lax.axis_size("dp"), stride, size, lax.axis_index("dp"))
    return jnp.where(lax.axis_index("pair") == 0, at, lax.rem(size - at, size))


def ring_route(total, stride, size):
    order = list(range(size))
    if total == size and size % 2 == 0:
        order = list(range(0, size, 2)) + list(range(size - 1, 0, -2))
    route = []
    for device in range(total):
        own = device // stride % size
        target = order[(order.index(own) + 1) % size]
        target = device + (target - own) * stride
        route.append((device * 2, target * 2))
        route.append((target * 2 + 1, device * 2 + 1))
    return route


def ring_combine(stride, size, step, terms, arrived):
    rows = terms[0].shape[0] // size
    width = terms[0].shape[1]
    if rows % 16 == 0:
        return run(
            lambda *refs: combine_kernel(stride, size, step, *refs),
            "combine",
            list(terms) + arrived,
            [near((rows, width), low)],
            flops=combine_cost if step < 2 else later_cost,
        )[0]
    index = (ring_at(stride, size) - step + size) % size
    value = 0.0
    for leaf in terms:
        piece = lax.dynamic_slice_in_dim(leaf, index * rows, rows, 0)
        value = value + piece.astype(wide)
    for leaf in arrived:
        value = value + leaf.astype(wide)
    return value.astype(low)


def ring_store(stride, size, step, block, cuts, totals, dtype):
    rows = block.shape[0]
    if rows % 16 == 0 and dtype == wide:
        return run(
            lambda *refs: store_kernel(stride, size, step, cuts, *refs),
            "store",
            [block],
            [far((size * rows, cut), wide) for cut in cuts],
            [pltpu.VMEM((rows, cut), wide) for cut in cuts]
            + [pltpu.SemaphoreType.DMA((len(cuts),))],
            flops=store_cost,
            keep=totals,
        )
    if totals is None:
        totals = [jnp.zeros((size * rows, cut), dtype) for cut in cuts]
    index = (ring_at(stride, size) + 1 - step + size) % size
    column = 0
    stored = []
    for leaf, cut in zip(totals, cuts):
        piece = block[:, column : column + cut].astype(dtype)
        stored.append(lax.dynamic_update_slice_in_dim(leaf, piece, index * rows, 0))
        column += cut
    return stored


def ring_steps(terms, widths):
    total = lax.axis_size("dp")
    levels = []
    stride = 1
    for size in ring_levels(total):
        levels.append((stride, size))
        stride *= size
    token = yield None
    terms = [terms[0], after(terms[1], token)]
    running = None
    for stride, size in levels:
        route = ring_route(total, stride, size)
        if running is not None:
            terms = [running, jnp.zeros_like(running)]
        for step in range(size):
            arrived = []
            if step > 0:
                arrived = [after(lax.ppermute(running, ("dp", "pair"), route), token)]
            running = ring_combine(stride, size, step, terms, arrived)
            token = yield running
    for depth, (stride, size) in enumerate(levels[::-1]):
        route = ring_route(total, stride, size)
        last = depth == len(levels) - 1
        dtype, cuts = (wide, widths) if last else (low, [sum(widths)])
        totals = None
        for step in range(size):
            if step > 0:
                running = after(lax.ppermute(running, ("dp", "pair"), route), token)
            totals = ring_store(stride, size, step, running, cuts, totals, dtype)
            if step > 0:
                token = yield tuple(totals)
        running = totals[0]
    return totals


class Steps:
    def __init__(self, steps, left=0):
        self.steps, self.left, self.result = (steps, left, None)
        next(steps)

    def advance(self, token):
        self.left -= 1
        try:
            return self.steps.send(token)
        except StopIteration as done:
            self.result = done.value
            return token


def ring(own, away, widths):
    left = sum(2 * size - 1 for size in ring_levels(lax.axis_size("dp")))
    return Steps(ring_steps([own, from_pair(away)], widths), left)


def finish(sums):
    pairs = jax.ShapeDtypeStruct((2, D // 2), wide)
    outputs = [pairs, jax.ShapeDtypeStruct((1, FF // 2), wide), pairs, pairs, pairs]
    scratch = [pltpu.VMEM((48, LANES), wide), pltpu.SemaphoreType.DMA((1,))]
    return run(finish_kernel, "finish", [sums], outputs, scratch, spaces=[pltpu.HBM])


def export_kernel(*refs):
    count = len(refs) // 2
    copies = [
        pltpu.make_async_copy(refs[k], refs[count + k], refs[-1].at[k]) for k in range(count)
    ]
    for copy in copies:
        copy.start()
    for copy in copies:
        copy.wait()


def export(leaf, earlier):
    return run(
        export_kernel,
        "export",
        [after(leaf, earlier)],
        [far(leaf.shape, leaf.dtype)],
        [pltpu.SemaphoreType.DMA((1,))],
    )[0]


def from_pair(leaf):
    return lax.ppermute(leaf, "pair", swap)


def local(
    inputs,
    cotangent,
    text_mask,
    seg_count,
    align,
    w_qkv,
    w_out,
    w_up,
    w_down,
    bias_qv,
    bias_up,
    bias_res,
    norm_gain,
    norm_shift,
):
    own = [w_qkv[0], w_out[0], w_up[0], w_down[0]]
    other_qkv = from_pair(own[0])
    params = [bias_qv[0], bias_res[0], norm_gain[0], norm_shift[0], bias_up, text_mask, align]
    params += [seg_count]
    packed, code = run(
        pack_kernel,
        "pack",
        params,
        [near((16, D // 2), wide), near((MB * 8, KEYS), jnp.int32)],
        [pltpu.VMEM(leaf.shape, leaf.dtype) for leaf in params[:-1]]
        + [pltpu.SMEM(seg_count.shape, seg_count.dtype)]
        + [pltpu.SemaphoreType.DMA((len(params),))],
        spaces=[pltpu.HBM] * len(params),
    )
    packed_other = from_pair(packed)
    mine = lambda me: me
    others = lambda me: 1 - me
    other_out = from_pair(own[1])
    held = [after(own[0], packed), own[1]]
    joined = join_halves("join_own", held, mine, pltpu.HBM, whole=(inputs,))
    inputs = joined[2]
    vec, bu = run(
        unpack_kernel,
        "unpack",
        [packed, after(packed_other, joined[0])],
        [near((8, D), wide), near((8, FF), wide)],
    )
    other_qkv, other_out, vec = lax.optimization_barrier((other_qkv, other_out, vec))
    other_up = from_pair(after(own[2], other_qkv))
    wq, wo = join_halves("join_qkv", [other_qkv, other_out], others, pltpu.VMEM, joined[:2])

    attended, raised, lowered = (None, None, None)
    topped, fed_back, attended_back = (None, None, None)
    onward, backward = ([None] * MB, [None] * MB)
    for section, document in ((0, 0), (0, 1), (1, 0), (1, 1)):
        source, row = (inputs, document * SEQ) if section == 0 else (onward[document], 0)
        if attended_back is not None:
            source = after(source, attended_back[0])
        attended = attend(section, document, source, row, wq, code, vec, attended)
        x, q, k, v, c, logs = attended
        if raised is None:
            other_up = after(other_up, x)
            other_down = from_pair(after(own[3], other_up))
            wu = join_both("join_up", own[2], other_up)
        raised, r = feed_up(section, document, x, c, wo, wu, vec, bu, raised)
        h1, n1, f, slope, rs1 = raised
        if lowered is None:
            wd = join_both("join_down", own[3], after(other_down, r))
        lowered, y = feed_down(section, document, r, f, wd, vec, lowered)
        section_out, h2, rs2 = lowered
        if section == 0:
            onward[document] = passed_along(y[0], "pipe", 1)
            continue
        topped, dr2 = top_back(section, document, cotangent, document * SEQ, h2, rs2, vec, topped)
        fed_back, dr1 = feed_back(
            section, document, dr2, topped[0], slope, h1, rs1, wd, wu, vec, fed_back
        )
        attended_back = attend_back(
            section, document, 0, D, fed_back[1], (q, k, v, c, logs), wo, code, (dr1, wq),
            attended_back,
        )
        backward[document] = passed_along(attended_back[3], "pipe", -1)
        attended_back = attended_back[:3]
    saved = (q, k, v, c, logs)

    source = after(backward[0], attended_back[0])
    topped, dr2 = top_back(0, 0, source, 0, h2, rs2, vec, topped)
    fed_back, dr1 = feed_back(0, 0, dr2, topped[0], slope, h1, rs1, wd, wu, vec, fed_back)
    attended_back = attend_back(
        0, 0, 0, D, fed_back[1], saved, wo, code, (dr1, wq), attended_back
    )
    share_down = weight_halves("weight_down", (f, topped[0]))
    share_up = weight_halves("weight_up", (n1, fed_back[0]))
    empty = (topped[1], fed_back[2], attended_back[1], fed_back[3])
    share_rest = weight_halves("weight_rest", (x, attended_back[0]), (c, fed_back[1]), sums=empty)

    section_out = export(section_out, share_rest[1])
    source = after(backward[1], (share_down[1], share_up[1], share_rest[1], section_out))
    topped, dr2 = top_back(0, 1, source, 0, h2, rs2, vec, topped)
    away, own = weight_halves("weight_down", (f, topped[0]), keep=share_down)
    dr2 = after(dr2, away)
    ring_down = ring(own, away, [D])
    fed_back, dr1 = feed_back(0, 1, dr2, topped[0], slope, h1, rs1, wd, wu, vec, fed_back)
    e2, small_top = topped
    du, e1, small_feed, small_up = fed_back
    token = ring_down.advance(du)
    away, own = weight_halves("weight_up", (n1, after(du, token)), keep=share_up)
    ring_up = ring(own, away, [FF])
    dp, small_attend, input_grad = attend_back(
        0, 1, 0, D, after(e1, away), saved, wo, code, (dr1, wq), attended_back
    )
    token = ring_down.advance(dp)
    token = ring_up.advance(token)
    dp = after(dp, token)
    sums = [small_top, small_feed, small_attend, small_up]
    away, own = weight_halves("weight_rest", (x, dp), (c, e1), sums=sums, keep=share_rest)
    ring_rest = ring(own, away, [3 * D, D, LANES])
    token = away

    rings = [ring_down, ring_up, ring_rest]
    token = ring_down.advance(token)
    token = ring_up.advance(token)
    turn = 0
    while any(each.left > 0 for each in rings):
        extra = [ring_rest] if turn < 2 else []
        for each in [ring_rest, ring_up] + extra + [ring_down]:
            if each.left > 0:
                token = each.advance(token)
        turn += 1
        if turn == 2:
            input_grad = token = export(input_grad, token)
    for each in rings:
        while each.result is None:
            token = each.advance(token)
    (grad_down,), (grad_up,), (grad_qkv, grad_out, sums) = (each.result for each in rings)
    grad_qv, grad_bias_up, grad_res, grad_gain, grad_shift = finish(sums)
    results = (section_out, input_grad, grad_qkv, grad_out, grad_up, grad_down, grad_qv)
    results += (grad_bias_up, grad_res, grad_gain, grad_shift)
    return tuple(leaf if leaf is grad_bias_up else leaf[None] for leaf in results)


def solution(mesh):
    return jax.shard_map(
        local,
        mesh=mesh,
        in_specs=(
            P(("dp", "pair"), None),
            P(("dp", "pair"), None),
            P(("dp", "pair"), None),
            P(("dp", "pair")),
            P(("dp", "pair"), None),
            P("pipe", "pair", None),
            P("pipe", "pair", None),
            P("pipe", "pair", None),
            P("pipe", "pair", None),
            P("pipe", None, "pair"),
            P("pipe", "pair"),
            P("pipe", None, "pair"),
            P("pipe", None, "pair"),
            P("pipe", None, "pair"),
        ),
        out_specs=(
            P("pipe", ("dp", "pair"), None),
            P("pipe", ("dp", "pair"), None),
            P("pipe", "pair", None),
            P("pipe", "pair", None),
            P("pipe", "pair", None),
            P("pipe", "pair", None),
            P("pipe", None, "pair"),
            P("pipe", "pair"),
            P("pipe", None, "pair"),
            P("pipe", None, "pair"),
            P("pipe", None, "pair"),
        ),
        check_vma=False,
    )
```
